256 devices in a mesh: cluster: 8 (over y, core), sub: 32 (over z, x).
Axes of the slice: x: 4, y: 4, z: 8, core: 2. Of those that a mesh axis runs over, the one named last changes fastest.
Arguments:
- dual_ops: float32 [8, 32, 1536, 1536], P('cluster', 'sub')
- rhs: float32 [8, 32, 1536, 128], P('cluster', 'sub'), may hold values from -6 to 6
- corner_basis: float32 [8, 32, 24, 1536], P('cluster', 'sub'), may hold values from -0.15625 to 0.15625
- scaling: float32 [8, 32, 1536], P('cluster', 'sub'), may hold values from 0.5 to 1.5
- cluster_corner_inverse: float32 [8, 384, 384], P('cluster'), may hold values from -0.3125 to 0.3125
- coarse_map: float32 [8, 48, 384], P('cluster'), may hold values from -0.3125 to 0.3125
- global_inv: float32 [48, 48], replicated, may hold values from -0.875 to 0.875
- row_index: int32 [8, 32, 4, 384], P('cluster', 'sub'), may hold values from 0 to 1535, as said below
- pair_counts: int32 [8, 32, 4], P('cluster', 'sub'), may hold values from 0 to 384, as said below
- corner_map: int32 [8, 32, 24], P('cluster', 'sub'), may hold values from 0 to 383
Outputs:
- multipliers: float32 [8, 32, 1536, 128], P('cluster', 'sub')
- residual: float32 [8, 32, 1536, 128], P('cluster', 'sub')
The draws below stay inside these ranges and needn't reach their ends.
Inputs may be any that keep to these rules, and one draw needn't show every extreme that they name: `row_index`: the 384 entries of one subdomain's four directions together hold every row 0 to 1535 once. pair_counts of a direction equals the neighbour's count of the direction pointing back; it is 0 toward a missing neighbour.
All inputs are finite; a program needn't handle non-finite values.
Results may differ from the reference program's by a relative error of at most 0.00027.
Values sent between devices are 32-bit elements; how exact they have to be, the bound alone decides.
No kernel may reach another device: no remote copies, remote signals or barrier semaphores. Data moves between devices by JAX's collectives and lax.ppermute only.
A program may use at most 64 MiB of HBM per device.

```python
import math
import jax
import jax.numpy as jnp
from jax import lax

IFACE = 1536
SLOT = 384
LOADS = 128
CDOF = 24
CCL = 384
GDOF = 48
ITERS = 3
CLUSTERS = 8
SUBS = 32


def draw_dual_ops(key, part):
    key = jax.random.fold_in(key, 11)
    shape = (CLUSTERS, SUBS, IFACE, IFACE)
    base = jax.random.normal(key, shape, jnp.float32)
    base = base * (0.6 / math.sqrt(IFACE))
    sym = (base + jnp.swapaxes(base, 2, 3)) * 0.70710678
    diag = jax.random.uniform(jax.random.fold_in(key, 1), (CLUSTERS, SUBS, IFACE), jnp.float32, 2.5, 4.0)
    return sym + diag[..., None] * jnp.eye(IFACE, dtype=jnp.float32)


def draw_row_index(key, part):
    key = jax.random.fold_in(key, 37)
    keys = jax.random.split(key, CLUSTERS * SUBS)
    perms = jax.vmap(lambda single: jax.random.permutation(single, IFACE))(keys)
    return perms.reshape(CLUSTERS, SUBS, 4, SLOT).astype(jnp.int32)


def draw_pair_counts(key, part):
    key = jax.random.fold_in(key, 23)
    lower = SLOT // 4
    sub_edges = jax.random.randint(key, (CLUSTERS, SUBS - 1), lower, SLOT + 1, jnp.int32).at[0, 0].set(SLOT)
    clus_edges = jax.random.randint(jax.random.fold_in(key, 1), (CLUSTERS - 1, SUBS), lower, SLOT + 1, jnp.int32).at[0, 0].set(SLOT)
    zero_column = jnp.zeros((CLUSTERS, 1), jnp.int32)
    zero_row = jnp.zeros((1, SUBS), jnp.int32)
    minus_sub = jnp.concatenate([zero_column, sub_edges], axis=1)
    plus_sub = jnp.concatenate([sub_edges, zero_column], axis=1)
    minus_clus = jnp.concatenate([zero_row, clus_edges], axis=0)
    plus_clus = jnp.concatenate([clus_edges, zero_row], axis=0)
    return jnp.stack([minus_sub, plus_sub, minus_clus, plus_clus], axis=2)


def set_ends(result, key, smallest, top_value):
    longest = result.shape.index(max(result.shape))
    spots = []
    for shift in (0, 1):
        where = [jax.random.randint(jax.random.fold_in(key, axis), (), 0, length) for axis, length in enumerate(result.shape)]
        where[longest] = (where[longest] + shift) % result.shape[longest]
        spots.append(tuple(where))
    return result.at[spots[0]].set(smallest).at[spots[1]].set(top_value)


def steps_of(stream_key, extent, cuts, smallest, top_value):
    level = 1.0
    for axis_at, shards_of in cuts:
        draws = jax.random.uniform(jax.random.fold_in(jax.random.fold_in(stream_key, 6), axis_at), (shards_of,), jnp.float32, smallest / len(cuts), top_value / len(cuts))
        level = level * jnp.repeat(jnp.exp(draws), extent[axis_at] // shards_of).reshape((-1,) + (1,) * (len(extent) - 1 - axis_at))
    return level


def noise(rng, dims, scale, most, cuts=(), kind=jnp.bfloat16):
    gain = steps_of(rng, dims, cuts, -0.22, 0.18) if cuts else 1.0
    result = jax.random.normal(rng, dims, jnp.float32) * scale * gain
    return jnp.minimum(jnp.maximum(result, -most), most).astype(kind)


def setup_inputs(seed: int = 0) -> dict:
    seeds = jax.random.split(jax.random.key(seed), 11)
    return {
        "dual_ops": draw_dual_ops(jax.random.fold_in(seeds[10], 71), 0),
        "rhs": noise(seeds[1], (CLUSTERS, SUBS, IFACE, LOADS), 1.0, 6.0, ((0, 8), (1, 32)), jnp.float32),
        "corner_basis": noise(seeds[2], (CLUSTERS, SUBS, CDOF, IFACE), IFACE ** -0.5, 0.15625, ((0, 8), (1, 32)), jnp.float32),
        "scaling": jnp.clip(0.5 + 1.0 * jax.random.uniform(seeds[3], (CLUSTERS, SUBS, IFACE), jnp.float32) ** steps_of(seeds[3], (CLUSTERS, SUBS, IFACE), ((0, 8), (1, 32)), -0.2, 0.2), 0.5, 1.5),
        "cluster_corner_inverse": noise(seeds[4], (CLUSTERS, CCL, CCL), CCL ** -0.5, 0.3125, ((0, 8),), jnp.float32),
        "coarse_map": noise(seeds[5], (CLUSTERS, GDOF, CCL), CCL ** -0.5, 0.3125, ((0, 8),), jnp.float32),
        "global_inv": noise(seeds[6], (GDOF, GDOF), GDOF ** -0.5, 0.875, (), jnp.float32),
        "row_index": draw_row_index(jax.random.fold_in(seeds[10], 71), 0),
        "pair_counts": draw_pair_counts(jax.random.fold_in(seeds[10], 71), 0),
        "corner_map": set_ends(jax.random.randint(seeds[9], (CLUSTERS, SUBS, CDOF), 0, CCL), jax.random.fold_in(seeds[9], 1), 0, CCL - 1).astype(jnp.int32),
    }


HIGHEST_ACCURACY = lax.Precision.HIGHEST


def slot_masks(row_index, pair_counts):
    live_slot = (jnp.arange(SLOT, dtype=jnp.int32)[None, None, None, :] < pair_counts[..., None]).astype(jnp.float32)
    flat_ids = row_index.reshape(CLUSTERS, SUBS, 4 * SLOT)

    def spread(ids, vals):
        return jnp.zeros((IFACE,), jnp.float32).at[ids].add(vals)

    live_rows = jax.vmap(jax.vmap(spread))(flat_ids, live_slot.reshape(CLUSTERS, SUBS, 4 * SLOT))
    return live_slot, live_rows


def jump(vector, row_index, live_slot, live_rows):
    flat_ids = row_index.reshape(CLUSTERS, SUBS, 4 * SLOT)
    slot_vals = jnp.take_along_axis(vector, flat_ids[..., None], axis=2)
    slot_vals = slot_vals.reshape(CLUSTERS, SUBS, 4, SLOT, LOADS) * live_slot[..., None]
    zero_column = jnp.zeros((CLUSTERS, 1, SLOT, LOADS), jnp.float32)
    zero_row = jnp.zeros((1, SUBS, SLOT, LOADS), jnp.float32)
    from_left = jnp.concatenate([zero_column, slot_vals[:, :-1, 1]], axis=1)
    from_right = jnp.concatenate([slot_vals[:, 1:, 0], zero_column], axis=1)
    from_below = jnp.concatenate([zero_row, slot_vals[:-1, :, 3]], axis=0)
    from_above = jnp.concatenate([slot_vals[1:, :, 2], zero_row], axis=0)
    received = jnp.stack([from_left, from_right, from_below, from_above], axis=2) * live_slot[..., None]

    def spread(ids, vals):
        return jnp.zeros((IFACE, LOADS), jnp.float32).at[ids].add(vals)

    returned = jax.vmap(jax.vmap(spread))(flat_ids, received.reshape(CLUSTERS, SUBS, 4 * SLOT, LOADS))
    return live_rows[..., None] * (vector - returned)


def apply_ops(dual_ops, vector):
    def one_cluster(pair):
        return jnp.einsum("sij,sjr->sir", pair[0], pair[1], precision=HIGHEST_ACCURACY)

    return lax.map(one_cluster, (dual_ops, vector))


def precondition(vector, corner_basis, scaling, cluster_corner_inverse, coarse_map, global_inv, onehot, row_index, live_slot, live_rows):
    local = jnp.einsum("csxi,csir->csxr", corner_basis, vector, precision=HIGHEST_ACCURACY)
    corner_residual = jnp.einsum("csxk,csxr->ckr", onehot, local, precision=HIGHEST_ACCURACY)
    halfway_solution = jnp.einsum("nim,nmd->nid", cluster_corner_inverse, corner_residual, precision=HIGHEST_ACCURACY)
    coarse_solution = jnp.einsum("nvs,nvi->nsi", cluster_corner_inverse, halfway_solution, precision=HIGHEST_ACCURACY)
    global_res = jnp.einsum("cgk,ckr->gr", coarse_map, corner_residual, precision=HIGHEST_ACCURACY)
    global_half = jnp.dot(global_inv, global_res, precision=HIGHEST_ACCURACY, preferred_element_type=jnp.float32)
    global_x = jnp.dot(global_inv.T, global_half, precision=HIGHEST_ACCURACY, preferred_element_type=jnp.float32)
    cluster_vec = coarse_solution + jnp.einsum("cgk,gr->ckr", coarse_map, global_x, precision=HIGHEST_ACCURACY)
    corner_vals = jnp.einsum("csxk,ckr->csxr", onehot, cluster_vec, precision=HIGHEST_ACCURACY)
    scaled = scaling[..., None] * vector + jnp.einsum("csxi,csxr->csir", corner_basis, corner_vals, precision=HIGHEST_ACCURACY)
    return jump(scaled, row_index, live_slot, live_rows)


def reference(dual_ops, rhs, corner_basis, scaling, cluster_corner_inverse, coarse_map, global_inv, row_index, pair_counts, corner_map):
    live_slot, live_rows = slot_masks(row_index, pair_counts)
    onehot = (corner_map[..., None] == jnp.arange(CCL, dtype=jnp.int32)).astype(jnp.float32)

    def prec(vector):
        return precondition(vector, corner_basis, scaling, cluster_corner_inverse, coarse_map, global_inv, onehot, row_index, live_slot, live_rows)

    multipliers = jnp.zeros((CLUSTERS, SUBS, IFACE, LOADS), jnp.float32)
    residual = jump(rhs, row_index, live_slot, live_rows)
    precond = prec(residual)
    search = precond
    rz_now = jnp.sum(residual * precond, axis=(0, 1, 2))
    for step in range(ITERS):
        image = jump(apply_ops(dual_ops, search), row_index, live_slot, live_rows)
        alpha = rz_now / jnp.sum(search * image, axis=(0, 1, 2))
        multipliers = multipliers + alpha * search
        residual = residual - alpha * image
        precond = prec(residual)
        rz_next = jnp.sum(residual * precond, axis=(0, 1, 2))
        search = precond + (rz_next / rz_now) * search
        rz_now = rz_next
    return multipliers, residual
```

```python
import jax
import jax.numpy as jnp
from jax import lax
from jax.experimental import pallas as pl
from jax.experimental.pallas import tpu as pltpu
from jax.sharding import PartitionSpec as P

F32 = jnp.float32
BF16 = jnp.bfloat16
VMEM_LIMIT = 40 * 1024 * 1024
CID_LANE = 25
SCALE_LANE = 24
MAP_LANE = 32
ROWS_AT_ONCE = 8


def dot(left, right, contract=((1,), (0,))):
    return lax.dot_general(
        left, right, (contract, ((), ())), precision=lax.Precision.HIGHEST, preferred_element_type=F32
    )


def call(kernel, outs, vmem, smem=(), scratch=(), name=None, flops=0):
    specs = [pl.BlockSpec(memory_space=pltpu.SMEM)] * len(smem)
    specs += [pl.BlockSpec(memory_space=pltpu.VMEM)] * len(vmem)
    moved = sum(a.size * a.dtype.itemsize for a in vmem) + sum(4 * o.size for o in outs)
    return pl.pallas_call(
        kernel,
        out_shape=outs,
        in_specs=specs,
        out_specs=[pl.BlockSpec(memory_space=pltpu.VMEM)] * len(outs),
        scratch_shapes=list(scratch),
        compiler_params=pltpu.CompilerParams(vmem_limit_bytes=VMEM_LIMIT),
        cost_estimate=pl.CostEstimate(flops=flops, bytes_accessed=moved, transcendentals=0),
        name=name,
    )(*smem, *vmem)


def out(*shape):
    return jax.ShapeDtypeStruct(shape, F32)


def live_block(count, slot, lanes):
    return lax.broadcasted_iota(jnp.int32, (slot, lanes), 0) < count


def pack_kernel(idx, rhs, basis, scaling, cid, cmap, pa, pb, pc, pd, wide, static, cpad):
    cdof = basis.shape[0]
    slot = pa.shape[0] // 2
    wide[...] = jnp.zeros_like(wide)
    wide[0:cdof, :] = basis[...]
    wide[SCALE_LANE : SCALE_LANE + 1, :] = scaling[...]
    static[...] = wide[...].T
    cpad[...] = jnp.zeros_like(cpad)
    cpad[MAP_LANE : MAP_LANE + cmap.shape[0], :] = cmap[...]
    ids = cid[...]
    onehot = jnp.where(
        ids == lax.broadcasted_iota(jnp.int32, (cdof, cpad.shape[1]), 1), 1.0, 0.0
    ).astype(F32)
    extra = dot(onehot, cpad[...], ((1,), (1,)))
    lane = lax.broadcasted_iota(jnp.int32, extra.shape, 1)
    extra = jnp.where(lane == CID_LANE, ids.astype(F32), extra)
    for block, ref in enumerate((pa, pb, pc, pd)):

        def move(step, carry, block=block, ref=ref):
            base = step * ROWS_AT_ONCE
            for r in range(ROWS_AT_ONCE):
                row = idx[block * slot + base + r]
                ref[pl.ds(base + r, 1), :] = rhs[pl.ds(row, 1), :]
                ref[pl.ds(slot + base + r, 1), :] = static[pl.ds(row, 1), :]
            return carry

        lax.fori_loop(0, slot // ROWS_AT_ONCE, move, 0)
        ref[slot : slot + cdof, :] = ref[slot : slot + cdof, :] + extra


def first_kernel(
    cnt, crow, pa, pb, pc, pd, qa, qb, qc, qd, r0, ft, ct, dsum, x0, nq, pay
):
    slot = pa.shape[0] // 2
    cdof = SCALE_LANE
    lanes = pa.shape[1]
    lane = lax.broadcasted_iota(jnp.int32, (slot, lanes), 1)
    own = lane < cdof
    nq[...] = jnp.zeros_like(nq)
    nq[0:cdof, :] = pa[slot : slot + cdof, :]
    for block, (mine, theirs) in enumerate(((pa, qa), (pb, qb), (pc, qc), (pd, qd))):
        rows = slice(block * slot, (block + 1) * slot)
        live = live_block(cnt[block], slot, lanes)
        res = jnp.where(live, mine[0:slot, :] - theirs[0:slot, :], 0.0)
        r0[rows, :] = res
        stat = mine[slot : 2 * slot, :]
        other = theirs[slot : 2 * slot, :]
        basis_mine = jnp.where(own & live, stat, 0.0)
        basis_other = jnp.where(own & live, other, 0.0)
        full = basis_mine - pltpu.roll(basis_other, cdof * (block + 1), 1)
        ft[rows, :] = full
        x0[rows, lanes : 2 * lanes] = full
        weight = jnp.sum(jnp.where((lane == SCALE_LANE) & live, stat + other, 0.0), axis=1, keepdims=True)
        weight = jnp.broadcast_to(weight, (slot, lanes))
        dsum[rows, :] = weight
        x0[rows, 0:lanes] = weight * res
        start = cdof * (block + 1)
        nq[start : start + cdof, :] = other[0:cdof, :]
        ct[:, rows] = basis_mine.T[0 : ct.shape[0], :]
    pay[...] = jnp.zeros_like(pay)
    pay[0:32, :] = dot(ct[...], r0[...])
    pay[cdof : cdof + 1, :] = crow[...]


def operator_kernel(idx, x, b, o, natural, split, result):
    step = pl.program_id(0)
    rows, n = x.shape
    tile = b.shape[0]

    @pl.when(step == 0)
    def _():
        def move(at, carry):
            base = at * ROWS_AT_ONCE
            for r in range(ROWS_AT_ONCE):
                natural[pl.ds(idx[base + r], 1), :] = x[pl.ds(base + r, 1), :]
            return carry

        lax.fori_loop(0, rows // ROWS_AT_ONCE, move, 0)
        value = natural[...]
        high = value.astype(BF16)
        split[:, 0:n] = high
        split[:, n : 2 * n] = (value - high.astype(F32)).astype(BF16)

    part = b[...]
    high = part.astype(BF16)
    low = (part - high.astype(F32)).astype(BF16)
    first = jnp.dot(high, split[...], preferred_element_type=F32)
    second = jnp.dot(low, split[:, 0:n], preferred_element_type=F32)
    result[pl.ds(step * tile, tile), :] = first[:, 0:n] + (first[:, n : 2 * n] + second)

    @pl.when(step == pl.num_programs(0) - 1)
    def _():
        def move(at, carry):
            base = at * ROWS_AT_ONCE
            for r in range(ROWS_AT_ONCE):
                o[pl.ds(base + r, 1), :] = result[pl.ds(idx[base + r], 1), :]
            return carry

        lax.fori_loop(0, rows // ROWS_AT_ONCE, move, 0)


def apply_operator(idx, x, operator):
    rows, n = x.shape
    tile = 256
    return pl.pallas_call(
        operator_kernel,
        out_shape=out(rows, n),
        grid_spec=pltpu.PrefetchScalarGridSpec(
            num_scalar_prefetch=1,
            grid=(rows // tile,),
            in_specs=[
                pl.BlockSpec((rows, n), lambda i, idx: (0, 0)),
                pl.BlockSpec((tile, rows), lambda i, idx: (i, 0)),
            ],
            out_specs=pl.BlockSpec((rows, n), lambda i, idx: (0, 0)),
            scratch_shapes=[
                pltpu.VMEM((rows, n), F32),
                pltpu.VMEM((rows, 2 * n), BF16),
                pltpu.VMEM((rows, n), F32),
            ],
        ),
        compiler_params=pltpu.CompilerParams(vmem_limit_bytes=VMEM_LIMIT),
        cost_estimate=pl.CostEstimate(
            flops=6 * rows * rows * n, bytes_accessed=4 * rows * rows, transcendentals=0
        ),
        name="operator",
    )(idx, x, operator)


def corner_kernel(y, nq, coarse, cmap, p1, cvab):
    subs, rows, lanes = y.shape
    ccl = coarse.shape[0]
    cdof = SCALE_LANE
    gdof = cmap.shape[0]
    per = lanes // rows
    pieces = []
    which = lax.broadcasted_iota(jnp.int32, (ccl, lanes), 0).astype(F32)
    for group in range(subs // per):
        ids = y[group * per, cdof : cdof + 1, :]
        for r in range(1, per):
            ids = ids + y[group * per + r, cdof : cdof + 1, :]
        pieces.append(jnp.where(which == ids, 1.0, 0.0).astype(F32))
    onehot = jnp.concatenate(pieces, axis=1)
    sums = dot(onehot, y[...].reshape(subs * rows, lanes))
    solved = dot(coarse[...], sums)
    chosen = jnp.where(
        nq[0 : 3 * cdof, CID_LANE : CID_LANE + 1]
        == lax.broadcasted_iota(jnp.int32, (3 * cdof, ccl), 1).astype(F32),
        1.0,
        0.0,
    ).astype(F32)
    values = dot(chosen, solved)
    p1[0:gdof, :] = dot(cmap[...], sums)
    p1[gdof : gdof + 8, :] = jnp.sum(y[:, cdof : cdof + 8, :], axis=0)
    p1[gdof + 8 : gdof + 8 + cdof, :] = values[0:cdof, :]
    cvab[...] = values[cdof : 3 * cdof, :]


def pair_kernel(place, own, other, p2):
    cdof = SCALE_LANE
    top = own.shape[0] - cdof
    odd = place[0] == 1
    p2[0:top, :] = own[0:top, :] + other[0:top, :]
    mine = own[top : top + cdof, :]
    theirs = other[top : top + cdof, :]
    p2[top : top + cdof, :] = jnp.where(odd, theirs, mine)
    p2[top + cdof : top + 2 * cdof, :] = jnp.where(odd, mine, theirs)


def corner_values(place, p2, c2, c4, c6, cvab, nq, ggpad, cv):
    cdof = SCALE_LANE
    top = p2.shape[0] - 2 * cdof
    gdof = top - 8
    even = slice(top, top + cdof)
    odd = slice(top + cdof, top + 2 * cdof)
    is_odd = place[0] == 1
    total = (p2[0:top, :] + c2[0:top, :]) + (c4[0:top, :] + c6[0:top, :])
    lift = dot(ggpad[...], total[0:gdof, :])
    cv[0:cdof, :] = jnp.where(is_odd, p2[odd, :], p2[even, :])
    cv[cdof : 3 * cdof, :] = cvab[...]
    cv[3 * cdof : 4 * cdof, :] = jnp.where(is_odd, p2[even, :], p2[odd, :])
    far = place[1] == 1
    cv[4 * cdof : 5 * cdof, :] = jnp.where(
        is_odd,
        jnp.where(far, c6[even, :], c2[even, :]),
        jnp.where(far, c6[odd, :], c2[odd, :]),
    )
    cv[5 * cdof : 128, :] = jnp.zeros((128 - 5 * cdof, cv.shape[1]), F32)
    cv[...] = cv[...] + dot(nq[...], lift)
    return total[gdof : gdof + 8, :]


def stage0_kernel(
    place, p2, c2, c4, c6, cvab, nq, ggpad, tb, x0, ft, v0, ua, ub, uc, ud, cv
):
    corner_values(place, p2, c2, c4, c6, cvab, nq, ggpad, cv)
    lanes = ft.shape[1]
    slot = ua.shape[0]
    value = cv[...]
    v0[...] = x0[:, 0:lanes] + dot(ft[...], value)
    for block, ref in enumerate((ua, ub, uc, ud)):
        rows = slice(block * slot, (block + 1) * slot)
        ref[...] = tb[rows, 0:lanes] + dot(tb[rows, lanes : 2 * lanes], value)


def stage1_kernel(
    place, p2, c2, c4, c6, cvab, nq, ggpad, tb, ft, t, dsw, v0, r0, w0,
    u0a, u0b, u0c, u0d, v1, bv1, z1, r1, scal, ua, ub, uc, ud, cv,
):
    dots = corner_values(place, p2, c2, c4, c6, cvab, nq, ggpad, cv)
    lanes = ft.shape[1]
    slot = ua.shape[0]
    value = cv[...]
    alpha = dots[1:2, :] / dots[2:3, :]
    scal[...] = dots
    scal[0:1, :] = alpha
    new = dsw[...] + dot(ft[...], value)
    v1[...] = new
    z1[...] = v0[...] - alpha * new
    r1[...] = r0[...] - alpha * w0[...]
    for block, (ref, old) in enumerate(((ua, u0a), (ub, u0b), (uc, u0c), (ud, u0d))):
        rows = slice(block * slot, (block + 1) * slot)
        image = t[rows, :] + dot(tb[rows, lanes : 2 * lanes], value)
        bv1[rows, :] = image
        ref[...] = old[...] - alpha * image


def column_sum(value):
    return jnp.sum(value, axis=0, keepdims=True)


def stage2_kernel(
    place, p2, c2, c4, c6, cvab, nq, ggpad, tb, ft, t, dsw, v0, w0, v1, bv1, z1, r1, s1, scal,
    u1a, u1b, u1c, u1d, z2, p1, xs, r2, q1, scal2, dots2, ua, ub, uc, ud, cv,
):
    dots = corner_values(place, p2, c2, c4, c6, cvab, nq, ggpad, cv)
    lanes = ft.shape[1]
    slot = ua.shape[0]
    value = cv[...]
    alpha0 = scal[0:1, :]
    rz0 = scal[1:2, :]
    pq0 = scal[2:3, :]
    rz1 = dots[1:2, :]
    beta = rz1 / rz0
    pq1 = dots[2:3, :] + beta * (dots[3:4, :] + dots[4:5, :]) + beta * beta * pq0
    alpha = rz1 / pq1
    scal2[...] = jnp.zeros_like(scal2)
    scal2[1:2, :] = rz1
    scal2[2:3, :] = pq1
    search = z1[...] + beta * v0[...]
    p1[...] = search
    xs[...] = alpha0 * v0[...] + alpha * search
    image_q = s1[...] + beta * w0[...]
    q1[...] = image_q
    res = r1[...] - alpha * image_q
    r2[...] = res
    new = z1[...] - alpha * (dsw[...] + dot(ft[...], value) + beta * v1[...])
    z2[...] = new
    zs = jnp.zeros((1, lanes), F32)
    ps = jnp.zeros((1, lanes), F32)
    for block, (ref, old) in enumerate(((ua, u1a), (ub, u1b), (uc, u1c), (ud, u1d))):
        rows = slice(block * slot, (block + 1) * slot)
        image = t[rows, :] + dot(tb[rows, lanes : 2 * lanes], value) + beta * bv1[rows, :]
        fresh = old[...] - alpha * image
        ref[...] = fresh
        zs = zs + column_sum(fresh * z2[rows, :])
        ps = ps + column_sum(fresh * p1[rows, :])
    dots2[...] = jnp.zeros_like(dots2)
    dots2[1:2, :] = column_sum(res * new)
    dots2[2:3, :] = 2.0 * zs
    dots2[3:4, :] = column_sum(image_q * new)
    dots2[4:5, :] = 2.0 * ps


def jump_rows(cnt, mine, theirs, w):
    slot = mine[0].shape[0]
    for block in range(4):
        live = live_block(cnt[block], slot, w.shape[1])
        w[block * slot : (block + 1) * slot, :] = jnp.where(
            live, mine[block][...] - theirs[block][...], 0.0
        )


def jump1_kernel(
    cnt, ua, ub, uc, ud, qa, qb, qc, qd, dsum, ct, crow, r0, v0, w, dsw, pay
):
    jump_rows(cnt, (ua, ub, uc, ud), (qa, qb, qc, qd), w)
    value = w[...]
    dsw[...] = dsum[...] * value
    pay[...] = dot(ct[...], value)
    pay[SCALE_LANE : SCALE_LANE + 1, :] = crow[...]
    pay[SCALE_LANE + 1 : SCALE_LANE + 2, :] = column_sum(r0[...] * v0[...])
    pay[SCALE_LANE + 2 : SCALE_LANE + 3, :] = column_sum(value * v0[...])


def jump2_kernel(
    cnt, ua, ub, uc, ud, qa, qb, qc, qd, dsum, ct, crow, r1, z1, w0, v0, w, dsw, pay
):
    jump_rows(cnt, (ua, ub, uc, ud), (qa, qb, qc, qd), w)
    value = w[...]
    dsw[...] = dsum[...] * value
    pay[...] = dot(ct[...], value)
    at = SCALE_LANE
    pay[at : at + 1, :] = crow[...]
    pay[at + 1 : at + 2, :] = column_sum(r1[...] * z1[...])
    pay[at + 2 : at + 3, :] = column_sum(value * z1[...])
    pay[at + 3 : at + 4, :] = column_sum(w0[...] * z1[...])
    pay[at + 4 : at + 5, :] = column_sum(value * v0[...])


def last_kernel(
    idx, cnt, ua, ub, uc, ud, qa, qb, qc, qd, z2, p1, xs, r2, q1, scal2, d0, d2, d4, d6,
    mult, resid, first, second,
):
    dots = (d0[...] + d2[...]) + (d4[...] + d6[...])
    beta = dots[1:2, :] / scal2[1:2, :]
    pq = dots[2:3, :] + beta * (dots[3:4, :] + dots[4:5, :]) + beta * beta * scal2[2:3, :]
    alpha = dots[1:2, :] / pq
    jump_rows(cnt, (ua, ub, uc, ud), (qa, qb, qc, qd), second)
    first[...] = xs[...] + alpha * (z2[...] + beta * p1[...])
    second[...] = r2[...] - alpha * (second[...] + beta * q1[...])

    def move(at, carry):
        base = at * ROWS_AT_ONCE
        for r in range(ROWS_AT_ONCE):
            row = idx[base + r]
            mult[pl.ds(row, 1), :] = first[pl.ds(base + r, 1), :]
            resid[pl.ds(row, 1), :] = second[pl.ds(base + r, 1), :]
        return carry

    lax.fori_loop(0, first.shape[0] // ROWS_AT_ONCE, move, 0)


def body(
    dual_ops,
    rhs,
    corner_basis,
    scaling,
    cluster_corner_inverse,
    coarse_map,
    global_inv,
    row_index,
    pair_counts,
    corner_map,
):
    operator = dual_ops[0, 0]
    loads = rhs[0, 0]
    basis = corner_basis[0, 0]
    weights = scaling[0]
    factor = cluster_corner_inverse[0]
    lift_map = coarse_map[0]
    row_ids = row_index[0, 0]
    counts = pair_counts[0, 0]
    corners = corner_map[0, 0]
    slot = row_ids.shape[1]
    order, lanes = loads.shape
    cdof = basis.shape[0]
    subs = lax.axis_size("sub")
    clusters = lax.axis_size("cluster")
    gdof = lift_map.shape[0]

    s = lax.axis_index("sub")
    c = lax.axis_index("cluster")
    s_odd = s % 2
    c_odd = c % 2
    pairs_a = [(i, i ^ 1) for i in range(subs)]
    pairs_b = [(i, i + 1) for i in range(1, subs - 1, 2)]
    pairs_b += [(j, i) for i, j in pairs_b]
    pairs_c = [(i, i ^ 1) for i in range(clusters)]
    pairs_d = [(i, i + 1) for i in range(1, clusters - 1, 2)]
    pairs_d += [(j, i) for i, j in pairs_d]
    across = [[(i, i ^ k) for i in range(clusters)] for k in (2, 4, 6)]

    def chosen(array):
        return jnp.stack(
            [
                jnp.where(s_odd == 0, array[1], array[0]),
                jnp.where(s_odd == 0, array[0], array[1]),
                jnp.where(c_odd == 0, array[3], array[2]),
                jnp.where(c_odd == 0, array[2], array[3]),
            ],
            0,
        )

    idx = chosen(row_ids).reshape(-1)
    cnt = chosen(counts)
    chip = c // 2
    next_chip = jnp.where(c_odd == 1, chip + 1, chip - 1)
    far = ((chip ^ next_chip) == 3).astype(jnp.int32)
    place = jnp.stack([c_odd, far]).astype(jnp.int32)

    group_rows = 32
    ids = jnp.concatenate(
        [corners.astype(F32), jnp.full((group_rows - cdof,), -1.0, F32)]
    )
    per = lanes // group_rows
    crow = jnp.where(
        jnp.arange(per, dtype=jnp.int32)[:, None] == s % per, ids[None, :], 0.0
    ).reshape(1, lanes)

    def exchange(blocks):
        return [
            lax.ppermute(blocks[0], "sub", pairs_a),
            lax.ppermute(blocks[1], "sub", pairs_b),
            lax.ppermute(blocks[2], "cluster", pairs_c),
            lax.ppermute(blocks[3], "cluster", pairs_d),
        ]

    def spread(rows):
        return lax.all_to_all(
            jnp.broadcast_to(rows[None], (subs,) + rows.shape), "sub", 0, 0, tiled=True
        )

    coarse = dot(factor, factor, ((0,), (0,)))
    gg = dot(global_inv, global_inv, ((0,), (0,)))
    ggpad = jnp.zeros((128, gdof), F32).at[MAP_LANE : MAP_LANE + gdof].set(gg)

    def clusterwise(pay):
        gathered = spread(pay)
        p1, cvab = call(
            corner_kernel,
            [out(gdof + 8 + cdof, lanes), out(2 * cdof, lanes)],
            [gathered, nq, coarse, lift_map],
            name="corner",
        )
        other = lax.ppermute(p1, "cluster", pairs_c)
        (p2,) = call(
            pair_kernel,
            [out(gdof + 8 + 2 * cdof, lanes)],
            [p1, other],
            smem=[place],
            name="pair",
        )
        moved = [lax.ppermute(p2, "cluster", k) for k in across]
        return [p2, *moved, cvab, nq, ggpad]

    block_out = [out(slot, lanes)] * 4
    full = out(order, lanes)
    cv_scratch = [pltpu.VMEM((128, lanes), F32)]

    packs = call(
        pack_kernel,
        [out(2 * slot, lanes)] * 4,
        [loads, basis, weights, corners[:, None], lift_map],
        smem=[idx],
        scratch=[
            pltpu.VMEM((128, order), F32),
            pltpu.VMEM((order, 128), F32),
            pltpu.VMEM((128, factor.shape[0]), F32),
        ],
        name="pack",
    )
    r0, ft, ct, dsum, x0, nq, pay = call(
        first_kernel,
        [
            full,
            full,
            out(group_rows, order),
            full,
            out(order, 2 * lanes),
            out(128, lanes),
            out(group_rows, lanes),
        ],
        [crow, *packs, *exchange(packs)],
        smem=[cnt],
        name="first",
    )

    coarse_part = clusterwise(pay)
    tb = apply_operator(idx, x0, operator)
    v0, *u0 = call(
        stage0_kernel,
        [full] + block_out,
        [*coarse_part, tb, x0, ft],
        smem=[place],
        scratch=cv_scratch,
        name="stage0",
    )
    w0, dsw, pay = call(
        jump1_kernel,
        [full, full, out(group_rows, lanes)],
        [*u0, *exchange(u0), dsum, ct, crow, r0, v0],
        smem=[cnt],
        name="jump1",
    )

    coarse_part = clusterwise(pay)
    t = apply_operator(idx, dsw, operator)
    v1, bv1, z1, r1, scal, *u1 = call(
        stage1_kernel,
        [full] * 4 + [out(8, lanes)] + block_out,
        [*coarse_part, tb, ft, t, dsw, v0, r0, w0, *u0],
        smem=[place],
        scratch=cv_scratch,
        name="stage1",
    )
    s1, dsw, pay = call(
        jump2_kernel,
        [full, full, out(group_rows, lanes)],
        [*u1, *exchange(u1), dsum, ct, crow, r1, z1, w0, v0],
        smem=[cnt],
        name="jump2",
    )

    coarse_part = clusterwise(pay)
    t = apply_operator(idx, dsw, operator)
    z2, p1, xs, r2, q1, scal2, dots2, *u2 = call(
        stage2_kernel,
        [full] * 5 + [out(8, lanes)] * 2 + block_out,
        [*coarse_part, tb, ft, t, dsw, v0, w0, v1, bv1, z1, r1, s1, scal, *u1],
        smem=[place],
        scratch=cv_scratch,
        name="stage2",
    )
    received = exchange(u2)
    dots = jnp.sum(spread(dots2), axis=0)
    dots = dots + lax.ppermute(dots, "cluster", pairs_c)
    moved = [lax.ppermute(dots, "cluster", k) for k in across]
    multipliers, residual = call(
        last_kernel,
        [full, full],
        [*u2, *received, z2, p1, xs, r2, q1, scal2, dots, *moved],
        smem=[idx, cnt],
        scratch=[pltpu.VMEM((order, lanes), F32)] * 2,
        name="last",
    )
    return (multipliers[None, None], residual[None, None])


def solution(mesh):
    in_specs = (
        P("cluster", "sub", None, None),
        P("cluster", "sub", None, None),
        P("cluster", "sub", None, None),
        P("cluster", "sub", None),
        P("cluster", None, None),
        P("cluster", None, None),
        P(),
        P("cluster", "sub", None, None),
        P("cluster", "sub", None),
        P("cluster", "sub", None),
    )
    out_specs = (P("cluster", "sub", None, None), P("cluster", "sub", None, None))
    return jax.shard_map(body, mesh=mesh, in_specs=in_specs, out_specs=out_specs, check_vma=False)
```

```python
import functools

import jax
import jax.numpy as jnp
from jax import lax
from jax.experimental import pallas as pl
from jax.experimental.pallas import tpu as pltpu
from jax.sharding import PartitionSpec as P

F32 = jnp.float32
BF16 = jnp.bfloat16
VMEM_LIMIT = 12 * 1024 * 1024
OPERATOR_VMEM = 24 * 1024 * 1024
PACK_VMEM = 60 * 1024 * 1024
CID_LANE = 25
SCALE_LANE = 24
MAP_LANE = 32
ROWS_AT_ONCE = 8
CHUNK = 128
BLOCK_ROWS = 32


def dot(left, right, contract=((1,), (0,))):
    return lax.dot_general(
        left, right, (contract, ((), ())), precision=lax.Precision.HIGHEST, preferred_element_type=F32
    )


def call(kernel, outs, vmem, smem=(), scratch=(), name=None, flops=0):
    specs = [pl.BlockSpec(memory_space=pltpu.SMEM)] * len(smem)
    specs += [pl.BlockSpec(memory_space=pltpu.VMEM)] * len(vmem)
    moved = sum(a.size * a.dtype.itemsize for a in vmem) + sum(o.size * o.dtype.itemsize for o in outs)
    return pl.pallas_call(
        kernel,
        out_shape=outs,
        in_specs=specs,
        out_specs=[pl.BlockSpec(memory_space=pltpu.VMEM)] * len(outs),
        scratch_shapes=list(scratch),
        compiler_params=pltpu.CompilerParams(vmem_limit_bytes=VMEM_LIMIT),
        cost_estimate=pl.CostEstimate(flops=flops, bytes_accessed=moved, transcendentals=0),
        name=name,
    )(*smem, *vmem)


def out(*shape, dtype=F32):
    return jax.ShapeDtypeStruct(shape, dtype)


def halves(value):
    high = value.astype(BF16)
    return high, (value - high.astype(F32)).astype(BF16)


def dot16(left, right):
    return jnp.dot(left, right, preferred_element_type=F32)


def live_block(count, slot, lanes):
    return lax.broadcasted_iota(jnp.int32, (slot, lanes), 0) < count


def block_of(place, block):
    return place[2 + block]


def pack_kernel(
    place, idx, rhs, basis, scaling, corners, cmap, pa, pb, pc, pd, crow, wide, static, cpad
):
    cdof = basis.shape[0]
    slot = pa.shape[0] // 2
    lanes = pa.shape[1]
    wide[...] = jnp.zeros_like(wide)
    wide[0:cdof, :] = basis[...]
    wide[SCALE_LANE : SCALE_LANE + 1, :] = scaling[...]
    static[...] = wide[...].T
    cpad[...] = jnp.zeros_like(cpad)
    cpad[MAP_LANE : MAP_LANE + cmap.shape[0], :] = cmap[...]
    row = corners[...].astype(F32)
    lane = lax.broadcasted_iota(jnp.int32, (cdof, cdof), 1)
    ids = jnp.sum(
        jnp.where(lane == lax.broadcasted_iota(jnp.int32, (cdof, cdof), 0), row, 0.0),
        axis=1,
        keepdims=True,
    )
    onehot = jnp.where(
        ids == lax.broadcasted_iota(jnp.int32, (cdof, cpad.shape[1]), 1).astype(F32), 1.0, 0.0
    ).astype(F32)
    extra = dot(onehot, cpad[...], ((1,), (1,)))
    lane = lax.broadcasted_iota(jnp.int32, extra.shape, 1)
    extra = jnp.where(lane == CID_LANE, ids, extra)
    lane = lax.broadcasted_iota(jnp.int32, (8, lanes), 1)
    crow[...] = jnp.where((lane >= cdof) & (lane < BLOCK_ROWS), -1.0, 0.0)
    crow[0:1, 0:cdof] = row
    crow[...] = pltpu.roll(crow[...], place[6] * BLOCK_ROWS, 1)
    for block, ref in enumerate((pa, pb, pc, pd)):

        def move(step, carry, block=block, ref=ref):
            base = step * ROWS_AT_ONCE
            for r in range(ROWS_AT_ONCE):
                row = idx[block * slot + base + r]
                ref[pl.ds(base + r, 1), :] = rhs[pl.ds(row, 1), :]
                ref[pl.ds(slot + base + r, 1), :] = static[pl.ds(row, 1), :]
            return carry

        lax.fori_loop(0, slot // ROWS_AT_ONCE, move, 0)
        ref[slot : slot + cdof, :] = ref[slot : slot + cdof, :] + extra


def pack_rows(place, idx, rhs, basis, scaling, corners, cmap, slot):
    order, lanes = rhs.shape
    vmem = (rhs, basis, scaling, corners, cmap)
    outs = [out(2 * slot, lanes)] * 4 + [out(8, lanes)]
    whole = lambda array: pl.BlockSpec(array.shape, lambda i: (0, 0))
    return pl.pallas_call(
        pack_kernel,
        out_shape=outs,
        grid=(1,),
        in_specs=[pl.BlockSpec(memory_space=pltpu.SMEM)] * 2 + [whole(a) for a in vmem],
        out_specs=[pl.BlockSpec(memory_space=pltpu.VMEM)] * len(outs),
        scratch_shapes=[
            pltpu.VMEM((128, order), F32),
            pltpu.VMEM((order, 128), F32),
            pltpu.VMEM((128, cmap.shape[1]), F32),
        ],
        compiler_params=pltpu.CompilerParams(vmem_limit_bytes=PACK_VMEM),
        name="pack",
    )(place, idx, *vmem)


def own_kernel(place, cnt, pa, pb, pc, pd, ct2):
    slot = pa.shape[0] // 2
    for block, mine in enumerate((pa, pb, pc, pd)):
        rows = slice(block * slot, (block + 1) * slot)
        stat = mine[slot : 2 * slot, :]
        lane = lax.broadcasted_iota(jnp.int32, stat.shape, 1)
        live = live_block(cnt[block_of(place, block)], slot, stat.shape[1])
        basis = jnp.where((lane < SCALE_LANE) & live, stat, 0.0).T[0:BLOCK_ROWS, :]
        high, low = halves(basis)
        ct2[0:BLOCK_ROWS, rows] = high
        ct2[BLOCK_ROWS : 2 * BLOCK_ROWS, rows] = low


def restricted(ct2, w2):
    lanes = w2.shape[1] // 2
    both = dot16(ct2[...], w2[...])
    return both[0:BLOCK_ROWS, 0:lanes] + (
        both[0:BLOCK_ROWS, lanes : 2 * lanes] + both[BLOCK_ROWS : 2 * BLOCK_ROWS, 0:lanes]
    )


def send(pay, values, crow, sums):
    cdof = SCALE_LANE
    pay[0] = values
    pay[0, cdof : cdof + 1, :] = crow[0:1, :]
    for at, value in enumerate(sums):
        row = cdof + 1 + at
        pay[0, row : row + 1, :] = column_sum(value)
    message = pay[0]
    for other in range(1, pay.shape[0]):
        pay[other] = message


def sweep(slot):
    for block in range(4):
        for start in range(0, slot, CHUNK):
            yield block, slice(start, start + CHUNK), slice(
                block * slot + start, block * slot + start + CHUNK
            )


def live_chunk(place, cnt, block, rows, lanes):
    row = lax.broadcasted_iota(jnp.int32, (CHUNK, lanes), 0) + rows.start
    return row < cnt[block_of(place, block)]


def first_kernel(place, cnt, crow, pa, pb, pc, pd, qa, qb, qc, qd, ct2, r0, pay, w2):
    slot = pa.shape[0] // 2
    lanes = pa.shape[1]
    mine, theirs = (pa, pb, pc, pd), (qa, qb, qc, qd)
    for block, part, rows in sweep(slot):
        live = live_chunk(place, cnt, block, part, lanes)
        value = jnp.where(live, mine[block][part, :] - theirs[block][part, :], 0.0)
        r0[rows, :] = value
        w2[rows, 0:lanes], w2[rows, lanes : 2 * lanes] = halves(value)
    send(pay, restricted(ct2, w2), crow, [])


def static_kernel(place, cnt, pa, pb, pc, pd, qa, qb, qc, qd, r0, gpad, fts, ft, dsum, dsw, ng, nq):
    slot = pa.shape[0] // 2
    cdof = SCALE_LANE
    lanes = pa.shape[1]
    lane = lax.broadcasted_iota(jnp.int32, (CHUNK, lanes), 1)
    own = lane < cdof
    mine, theirs = (pa, pb, pc, pd), (qa, qb, qc, qd)
    nq[...] = jnp.zeros_like(nq)
    nq[0:cdof, :] = pa[slot : slot + cdof, :]
    for block in range(4):
        start = cdof * (block + 1)
        nq[start : start + cdof, :] = theirs[block][slot : slot + cdof, :]
    ng[...] = dot(nq[...], gpad[...])
    for block, part, rows in sweep(slot):
        live = live_chunk(place, cnt, block, part, lanes)
        low_rows = slice(slot + part.start, slot + part.stop)
        stat = mine[block][low_rows, :]
        other = theirs[block][low_rows, :]
        basis_mine = jnp.where(own & live, stat, 0.0)
        basis_other = jnp.where(own & live, other, 0.0)
        full = basis_mine - pltpu.roll(basis_other, cdof * (block + 1), 1)
        fts[rows, 0:lanes], fts[rows, lanes : 2 * lanes] = halves(full)
        ft[rows, :] = full
        weight = jnp.sum(
            jnp.where((lane == cdof) & live, stat + other, 0.0), axis=1, keepdims=True
        )
        weight = jnp.broadcast_to(weight, (CHUNK, lanes))
        dsum[rows, :] = weight
        dsw[rows, :] = weight * r0[rows, :]


def coarse_kernel(factor, ginv, coarse, gpad):
    gdof = ginv.shape[0]
    coarse[...] = dot(factor[...], factor[...], ((0,), (0,)))
    gpad[...] = jnp.zeros_like(gpad)
    gpad[MAP_LANE : MAP_LANE + gdof, :] = dot(ginv[...], ginv[...], ((0,), (0,)))


def split_kernel(x, split):
    lanes = x.shape[1]
    for start in range(0, x.shape[0], CHUNK):
        rows = slice(start, start + CHUNK)
        split[rows, 0:lanes], split[rows, lanes : 2 * lanes] = halves(x[rows, :])


def go_home(idx, pairs):
    def move(at, carry):
        base = at * ROWS_AT_ONCE
        for r in range(ROWS_AT_ONCE):
            row = idx[base + r]
            for source, target in pairs:
                target[pl.ds(row, 1), :] = source[pl.ds(base + r, 1), :]
        return carry

    lax.fori_loop(0, idx.shape[0] // ROWS_AT_ONCE, move, 0)


def halves_kernel(b, b2):
    rows = b.shape[1]
    b2[:, 0:rows], b2[:, rows : 2 * rows] = halves(b[...])


def split_operator(operator):
    rows = operator.shape[0]
    tile = 256
    return pl.pallas_call(
        halves_kernel,
        out_shape=out(rows, 2 * rows, dtype=BF16),
        grid=(rows // tile,),
        in_specs=[pl.BlockSpec((tile, rows), lambda i: (i, 0))],
        out_specs=pl.BlockSpec((tile, 2 * rows), lambda i: (i, 0)),
        compiler_params=pltpu.CompilerParams(vmem_limit_bytes=OPERATOR_VMEM),
        cost_estimate=pl.CostEstimate(
            flops=0, bytes_accessed=8 * rows * rows, transcendentals=0
        ),
        name="halves",
    )(operator)


def operator_kernel(idx, x, b2, o, natural, split):
    rows, n = x.shape
    tile = rows // 2
    go_home(idx, ((x, natural),))
    for start in range(0, rows, CHUNK):
        part = slice(start, start + CHUNK)
        low_part = slice(rows + start, rows + start + CHUNK)
        high, low = halves(natural[part, :])
        split[part, 0:n] = high
        split[part, n : 2 * n] = low
        split[low_part, 0:n] = high
        split[low_part, n : 2 * n] = jnp.zeros((CHUNK, n), BF16)

    def multiply(at, carry):
        part = pl.ds(at * tile, tile)
        both = dot16(b2[part, :], split[...])
        natural[part, :] = both[:, 0:n] + both[:, n : 2 * n]
        return carry

    lax.fori_loop(0, rows // tile, multiply, 0)

    def move(at, carry):
        base = at * ROWS_AT_ONCE
        for r in range(ROWS_AT_ONCE):
            o[pl.ds(base + r, 1), :] = natural[pl.ds(idx[base + r], 1), :]
        return carry

    lax.fori_loop(0, rows // ROWS_AT_ONCE, move, 0)


def apply_operator(idx, x, b2):
    rows, n = x.shape
    (result,) = call(
        operator_kernel,
        [out(rows, n)],
        [x, b2],
        smem=[idx],
        scratch=[pltpu.VMEM((rows, n), F32), pltpu.VMEM((2 * rows, 2 * n), BF16)],
        name="operator",
        flops=6 * rows * rows * n,
    )
    return result


def gathered_product(y, table, p1, cvab):
    subs, rows, lanes = y.shape
    value = y[...].reshape(subs * rows, lanes)
    high, low = halves(value)
    both = dot16(table[...], jnp.concatenate([high, low], axis=1))
    half = both.shape[0] // 2
    total = both[0:half, 0:lanes] + (both[0:half, lanes:] + both[half:, 0:lanes])
    top = p1.shape[0]
    p1[...] = total[0:top, :]
    cvab[...] = total[top:, :]


def table_kernel(y, pa, qa, qb, coarse, cmap, table, p1, cvab, reach2):
    subs, rows, lanes = y.shape
    cdof = SCALE_LANE
    slot = pa.shape[0] // 2
    gdof, ccl = cmap.shape
    number = lax.broadcasted_iota(jnp.int32, (cdof, ccl), 1).astype(F32)
    chosen = [
        jnp.where(ref[slot : slot + cdof, CID_LANE : CID_LANE + 1] == number, 1.0, 0.0)
        for ref in (pa, qa, qb)
    ]
    reach = jnp.concatenate(
        [cmap[...], jnp.zeros((8, ccl), F32), dot(jnp.concatenate(chosen, axis=0), coarse[...])],
        axis=0,
    )
    reach2[0:128, :], reach2[128:256, :] = halves(reach)
    per = lanes // rows
    which = lax.broadcasted_iota(jnp.int32, (ccl, lanes), 0).astype(F32)
    row = lax.broadcasted_iota(jnp.int32, (256, lanes), 0)
    column = lax.broadcasted_iota(jnp.int32, (256, lanes), 1) % rows
    kept = (row - gdof == column - cdof) & (row > gdof) & (row < gdof + 8)
    unit = jnp.where(kept, 1.0, 0.0)
    for group in range(subs // per):
        ids = y[group * per, cdof : cdof + 1, :]
        for r in range(1, per):
            ids = ids + y[group * per + r, cdof : cdof + 1, :]
        onehot = jnp.where(which == ids, 1.0, 0.0).astype(BF16)
        at = slice(group * lanes, (group + 1) * lanes)
        table[:, at] = (dot16(reach2[...], onehot) + unit).astype(BF16)
    gathered_product(y, table, p1, cvab)


def corner_kernel(y, table, p1, cvab):
    gathered_product(y, table, p1, cvab)


def pair_kernel(place, own, other, p2):
    cdof = SCALE_LANE
    top = own.shape[0] - cdof
    odd = place[0] == 1
    p2[0:top, :] = own[0:top, :] + other[0:top, :]
    mine = own[top : top + cdof, :]
    theirs = other[top : top + cdof, :]
    p2[top : top + cdof, :] = jnp.where(odd, theirs, mine)
    p2[top + cdof : top + 2 * cdof, :] = jnp.where(odd, mine, theirs)


def corner_values(place, p2, c2, c4, c6, cvab, ng, cv, cv2):
    cdof = SCALE_LANE
    top = p2.shape[0] - 2 * cdof
    gdof = top - 8
    lanes = cv.shape[1]
    even = slice(top, top + cdof)
    odd = slice(top + cdof, top + 2 * cdof)
    is_odd = place[0] == 1
    total = (p2[0:top, :] + c2[0:top, :]) + (c4[0:top, :] + c6[0:top, :])
    cv[0:cdof, :] = jnp.where(is_odd, p2[odd, :], p2[even, :])
    cv[cdof : 3 * cdof, :] = cvab[...]
    cv[3 * cdof : 4 * cdof, :] = jnp.where(is_odd, p2[even, :], p2[odd, :])
    far = place[1] == 1
    cv[4 * cdof : 5 * cdof, :] = jnp.where(
        is_odd,
        jnp.where(far, c6[even, :], c2[even, :]),
        jnp.where(far, c6[odd, :], c2[odd, :]),
    )
    cv[5 * cdof : 128, :] = jnp.zeros((128 - 5 * cdof, lanes), F32)
    high, low = halves(cv[...] + dot(ng[...], total[0:gdof, :]))
    cv2[0:128, 0:lanes] = high
    cv2[128:256, 0:lanes] = high
    cv2[0:128, lanes : 2 * lanes] = low
    cv2[128:256, lanes : 2 * lanes] = jnp.zeros((128, lanes), BF16)
    return total[gdof : gdof + 8, :]


def times_corner(matrix, rows, cv2):
    both = dot16(matrix[rows, :], cv2[...])
    lanes = both.shape[1] // 2
    return both[:, 0:lanes] + both[:, lanes:]


def column_sum(value):
    return jnp.sum(value, axis=0, keepdims=True)


def stage0_kernel(
    place, p2, c2, c4, c6, cvab, ng, t, dsw, fts, bfs, v0, ua, ub, uc, ud, cv, cv2
):
    corner_values(place, p2, c2, c4, c6, cvab, ng, cv, cv2)
    lanes = cv.shape[1]
    blocks = (ua, ub, uc, ud)
    for block, part, rows in sweep(ua.shape[0]):
        v0[rows, :] = dsw[rows, :] + times_corner(fts, rows, cv2)
        blocks[block][part, :] = t[rows, :] + times_corner(bfs, rows, cv2)


def stage1_kernel(
    place, p2, c2, c4, c6, cvab, ng, fts, bfs, t, dsw, v0, r0, w0,
    u0a, u0b, u0c, u0d, v1, bv1, z1, r1, scal, ua, ub, uc, ud, cv, cv2,
):
    dots = corner_values(place, p2, c2, c4, c6, cvab, ng, cv, cv2)
    alpha = dots[1:2, :] / dots[2:3, :]
    scal[...] = dots
    scal[0:1, :] = alpha
    olds, news = (u0a, u0b, u0c, u0d), (ua, ub, uc, ud)
    for block, part, rows in sweep(ua.shape[0]):
        new = dsw[rows, :] + times_corner(fts, rows, cv2)
        v1[rows, :] = new
        z1[rows, :] = v0[rows, :] - alpha * new
        r1[rows, :] = r0[rows, :] - alpha * w0[rows, :]
        image = t[rows, :] + times_corner(bfs, rows, cv2)
        bv1[rows, :] = image
        news[block][part, :] = olds[block][part, :] - alpha * image


def stage2_kernel(
    place, p2, c2, c4, c6, cvab, ng, fts, bfs, t, dsw, v0, w0, v1, bv1, z1, r1, s1, scal,
    u1a, u1b, u1c, u1d, z2, p1, r2, q1, scal2, dots2, ua, ub, uc, ud, cv, cv2,
):
    dots = corner_values(place, p2, c2, c4, c6, cvab, ng, cv, cv2)
    lanes = cv.shape[1]
    rz0 = scal[1:2, :]
    pq0 = scal[2:3, :]
    rz1 = dots[1:2, :]
    beta = rz1 / rz0
    pq1 = dots[2:3, :] + beta * (dots[3:4, :] + dots[4:5, :]) + beta * beta * pq0
    alpha = rz1 / pq1
    scal2[...] = jnp.zeros_like(scal2)
    scal2[0:1, :] = scal[0:1, :]
    scal2[1:2, :] = rz1
    scal2[2:3, :] = pq1
    scal2[3:4, :] = alpha
    olds, news = (u1a, u1b, u1c, u1d), (ua, ub, uc, ud)
    sums = [jnp.zeros((8, lanes), F32) for _ in range(4)]

    def folded(value):
        return jnp.sum(value.reshape(CHUNK // 8, 8, lanes), axis=0)

    for block, part, rows in sweep(ua.shape[0]):
        search = z1[rows, :] + beta * v0[rows, :]
        p1[rows, :] = search
        image_q = s1[rows, :] + beta * w0[rows, :]
        q1[rows, :] = image_q
        res = r1[rows, :] - alpha * image_q
        r2[rows, :] = res
        new = z1[rows, :] - alpha * (
            dsw[rows, :] + times_corner(fts, rows, cv2) + beta * v1[rows, :]
        )
        z2[rows, :] = new
        image = t[rows, :] + times_corner(bfs, rows, cv2) + beta * bv1[rows, :]
        fresh = olds[block][part, :] - alpha * image
        news[block][part, :] = fresh
        sums[0] = sums[0] + folded(res * new)
        sums[1] = sums[1] + folded(fresh * new)
        sums[2] = sums[2] + folded(image_q * new)
        sums[3] = sums[3] + folded(fresh * search)
    dots2[0] = jnp.zeros((8, lanes), F32)
    dots2[0, 1:2, :] = column_sum(sums[0])
    dots2[0, 2:3, :] = 2.0 * column_sum(sums[1])
    dots2[0, 3:4, :] = column_sum(sums[2])
    dots2[0, 4:5, :] = 2.0 * column_sum(sums[3])
    message = dots2[0]
    for other in range(1, dots2.shape[0]):
        dots2[other] = message


def jump_kernel(pairs, place, cnt, ua, ub, uc, ud, qa, qb, qc, qd, dsum, ct2, crow, *rest):
    fields, (w, dsw, pay, w2) = rest[:-4], rest[-4:]
    lanes = w.shape[1]
    mine, theirs = (ua, ub, uc, ud), (qa, qb, qc, qd)
    sums = [jnp.zeros((8, lanes), F32) for _ in pairs]
    for block, part, rows in sweep(ua.shape[0]):
        live = live_chunk(place, cnt, block, part, lanes)
        value = jnp.where(live, mine[block][part, :] - theirs[block][part, :], 0.0)
        w[rows, :] = value
        dsw[rows, :] = dsum[rows, :] * value
        w2[rows, 0:lanes], w2[rows, lanes : 2 * lanes] = halves(value)
        for at, (left, right) in enumerate(pairs):
            first = value if left < 0 else fields[left][rows, :]
            product = first * fields[right][rows, :]
            sums[at] = sums[at] + jnp.sum(product.reshape(CHUNK // 8, 8, lanes), axis=0)
    send(pay, restricted(ct2, w2), crow, sums)


def sum_kernel(x, o):
    o[...] = jnp.sum(x[...], axis=0)


def add_kernel(x, y, o):
    o[...] = x[...] + y[...]


def home_kernel(idx, scal2, z2, p1, r2, q1, v0, z2n, p1n, r2n, q1n, xsn, xs):
    xs[...] = scal2[0:1, :] * v0[...] + scal2[3:4, :] * p1[...]

    go_home(idx, ((z2, z2n), (p1, p1n), (r2, r2n), (q1, q1n), (xs, xsn)))


def home_jump_kernel(place, cnt, idx, ua, ub, uc, ud, qa, qb, qc, qd, s2n, s2):
    lanes = s2.shape[1]
    mine, theirs = (ua, ub, uc, ud), (qa, qb, qc, qd)
    for block, part, rows in sweep(ua.shape[0]):
        live = live_chunk(place, cnt, block, part, lanes)
        s2[rows, :] = jnp.where(live, mine[block][part, :] - theirs[block][part, :], 0.0)

    go_home(idx, ((s2, s2n),))


def last_kernel(z2, p1, r2, q1, xs, s2, scal2, d0, d2, d4, d6, mult, resid):
    dots = (d0[...] + d2[...]) + (d4[...] + d6[...])
    beta = dots[1:2, :] / scal2[1:2, :]
    pq = dots[2:3, :] + beta * (dots[3:4, :] + dots[4:5, :]) + beta * beta * scal2[2:3, :]
    alpha = dots[1:2, :] / pq
    for start in range(0, z2.shape[0], CHUNK):
        rows = slice(start, start + CHUNK)
        mult[rows, :] = xs[rows, :] + alpha * (z2[rows, :] + beta * p1[rows, :])
        resid[rows, :] = r2[rows, :] - alpha * (s2[rows, :] + beta * q1[rows, :])


def body(
    dual_ops,
    rhs,
    corner_basis,
    scaling,
    cluster_corner_inverse,
    coarse_map,
    global_inv,
    row_index,
    pair_counts,
    corner_map,
):
    operator = dual_ops[0, 0]
    loads = rhs[0, 0]
    basis = corner_basis[0, 0]
    weights = scaling[0]
    factor = cluster_corner_inverse[0]
    lift_map = coarse_map[0]
    row_ids = row_index[0, 0]
    cnt = pair_counts[0, 0]
    corners = corner_map[0]
    slot = row_ids.shape[1]
    order, lanes = loads.shape
    cdof = basis.shape[0]
    subs = lax.axis_size("sub")
    clusters = lax.axis_size("cluster")
    gdof = lift_map.shape[0]

    s = lax.axis_index("sub")
    c = lax.axis_index("cluster")
    s_odd = s % 2
    c_odd = c % 2
    pairs_a = [(i, i ^ 1) for i in range(subs)]
    pairs_b = [(i, i + 1) for i in range(1, subs - 1, 2)]
    pairs_b += [(j, i) for i, j in pairs_b]
    pairs_c = [(i, i ^ 1) for i in range(clusters)]
    pairs_d = [(i, i + 1) for i in range(1, clusters - 1, 2)]
    pairs_d += [(j, i) for i, j in pairs_d]
    across = [[(i, i ^ k) for i in range(clusters)] for k in (2, 4, 6)]

    chip = c // 2
    next_chip = jnp.where(c_odd == 1, chip + 1, chip - 1)
    far = ((chip ^ next_chip) == 3).astype(jnp.int32)
    sides = [1 - s_odd, s_odd, 3 - c_odd, 2 + c_odd]
    place = jnp.stack(
        [v.astype(jnp.int32) for v in (c_odd, far, *sides, s % (lanes // BLOCK_ROWS), far)]
    )

    idx = jnp.concatenate(
        [
            jnp.where(s_odd == 0, row_ids[1], row_ids[0]),
            jnp.where(s_odd == 0, row_ids[0], row_ids[1]),
            jnp.where(c_odd == 0, row_ids[3], row_ids[2]),
            jnp.where(c_odd == 0, row_ids[2], row_ids[3]),
        ]
    )

    def exchange(blocks):
        return [
            lax.ppermute(blocks[0], "sub", pairs_a),
            lax.ppermute(blocks[1], "sub", pairs_b),
            lax.ppermute(blocks[2], "cluster", pairs_c),
            lax.ppermute(blocks[3], "cluster", pairs_d),
        ]

    def spread(messages):
        return lax.all_to_all(messages, "sub", 0, 0, tiled=True)

    def together(*values):
        return lax.optimization_barrier(values)

    def clusterwise(p1, cvab):
        other = lax.ppermute(p1, "cluster", pairs_c)
        (p2,) = call(
            pair_kernel,
            [out(gdof + 8 + 2 * cdof, lanes)],
            [p1, other],
            smem=[place],
            name="pair",
        )
        moved = [lax.ppermute(p2, "cluster", k) for k in across]
        return [p2, *moved, cvab]

    block_out = [out(slot, lanes)] * 4
    full = out(order, lanes)
    small = [out(gdof + 8 + cdof, lanes), out(2 * cdof, lanes)]
    cv_scratch = [pltpu.VMEM((128, lanes), F32), pltpu.VMEM((256, 2 * lanes), BF16)]
    w2_scratch = [pltpu.VMEM((order, 2 * lanes), BF16)]

    *packs, crow = pack_rows(place, idx, loads, basis, weights, corners, lift_map, slot)
    packs_in = exchange(packs)
    (ct2,) = call(
        own_kernel, [out(2 * BLOCK_ROWS, order, dtype=BF16)], [*packs], smem=[place, cnt], name="own"
    )
    coarse, gpad = call(
        coarse_kernel,
        [out(*factor.shape), out(128, gdof)],
        [factor, global_inv],
        name="coarse",
    )
    b2 = split_operator(operator)
    b2, ct2, coarse, gpad, *packs_in = together(b2, ct2, coarse, gpad, *packs_in)
    r0, pay = call(
        first_kernel,
        [full, out(subs, BLOCK_ROWS, lanes)],
        [crow, *packs, *packs_in, ct2],
        smem=[place, cnt],
        scratch=w2_scratch,
        name="first",
    )

    y = spread(pay)
    y, r0 = together(y, r0)
    table, p1, cvab = call(
        table_kernel,
        [out(256, subs * BLOCK_ROWS, dtype=BF16)] + small,
        [y, packs[0], *packs_in[:2], coarse, lift_map],
        scratch=[pltpu.VMEM((256, factor.shape[0]), BF16)],
        name="table",
    )
    cluster_part = clusterwise(p1, cvab)
    fts, ft, dsum, dsw, ng = call(
        static_kernel,
        [
            out(order, 2 * lanes, dtype=BF16),
            full,
            full,
            full,
            out(128, gdof),
        ],
        [*packs, *packs_in, r0, gpad],
        smem=[place, cnt],
        scratch=[pltpu.VMEM((128, lanes), F32)],
        name="static",
    )
    t = apply_operator(idx, dsw, b2)
    bf = apply_operator(idx, ft, b2)
    (bfs,) = call(split_kernel, [out(order, 2 * lanes, dtype=BF16)], [bf], name="split")
    v0, *u0 = call(
        stage0_kernel,
        [full] + block_out,
        [*cluster_part, ng, t, dsw, fts, bfs],
        smem=[place],
        scratch=cv_scratch,
        name="stage0",
    )
    w0, dsw, pay = call(
        functools.partial(jump_kernel, ((0, 1), (-1, 1))),
        [full, full, out(subs, BLOCK_ROWS, lanes)],
        [*u0, *exchange(u0), dsum, ct2, crow, r0, v0],
        smem=[place, cnt],
        scratch=w2_scratch,
        name="jump1",
    )

    y = spread(pay)
    y, dsw = together(y, dsw)
    p1, cvab = call(corner_kernel, small, [y, table], name="corner")
    cluster_part = clusterwise(p1, cvab)
    t = apply_operator(idx, dsw, b2)
    v1, bv1, z1, r1, scal, *u1 = call(
        stage1_kernel,
        [full] * 4 + [out(8, lanes)] + block_out,
        [*cluster_part, ng, fts, bfs, t, dsw, v0, r0, w0, *u0],
        smem=[place],
        scratch=cv_scratch,
        name="stage1",
    )
    s1, dsw, pay = call(
        functools.partial(jump_kernel, ((0, 1), (-1, 1), (2, 1), (-1, 3))),
        [full, full, out(subs, BLOCK_ROWS, lanes)],
        [*u1, *exchange(u1), dsum, ct2, crow, r1, z1, w0, v0],
        smem=[place, cnt],
        scratch=w2_scratch,
        name="jump2",
    )

    y = spread(pay)
    y, dsw = together(y, dsw)
    p1, cvab = call(corner_kernel, small, [y, table], name="corner")
    cluster_part = clusterwise(p1, cvab)
    t = apply_operator(idx, dsw, b2)
    z2, p1, r2, q1, scal2, dots2, *u2 = call(
        stage2_kernel,
        [full] * 4 + [out(8, lanes), out(subs, 8, lanes)] + block_out,
        [*cluster_part, ng, fts, bfs, t, dsw, v0, w0, v1, bv1, z1, r1, s1, scal, *u1],
        smem=[place],
        scratch=cv_scratch,
        name="stage2",
    )

    dots = spread(dots2)
    dots, z2, scal2, *u2 = together(dots, z2, scal2, *u2)
    u2_in = exchange(u2)
    (dots,) = call(sum_kernel, [out(8, lanes)], [dots], name="sum")
    other = lax.ppermute(dots, "cluster", pairs_c)
    (dots,) = call(add_kernel, [out(8, lanes)], [dots, other], name="add")
    moved = [lax.ppermute(dots, "cluster", k) for k in across]
    home = call(
        home_kernel,
        [full] * 5,
        [scal2, z2, p1, r2, q1, v0],
        smem=[idx],
        scratch=[pltpu.VMEM((order, lanes), F32)],
        name="home",
    )
    (s2,) = call(
        home_jump_kernel,
        [full],
        [*u2, *u2_in],
        smem=[place, cnt, idx],
        scratch=[pltpu.VMEM((order, lanes), F32)],
        name="home_jump",
    )
    multipliers, residual = call(
        last_kernel,
        [full, full],
        [*home, s2, scal2, dots, *moved],
        name="last",
    )
    return (multipliers[None, None], residual[None, None])


def solution(mesh):
    in_specs = (
        P("cluster", "sub", None, None),
        P("cluster", "sub", None, None),
        P("cluster", "sub", None, None),
        P("cluster", "sub", None),
        P("cluster", None, None),
        P("cluster", None, None),
        P(),
        P("cluster", "sub", None, None),
        P("cluster", "sub", None),
        P("cluster", "sub", None),
    )
    out_specs = (P("cluster", "sub", None, None), P("cluster", "sub", None, None))
    return jax.shard_map(body, mesh=mesh, in_specs=in_specs, out_specs=out_specs, check_vma=False)
```

```python
import functools

import jax
import jax.numpy as jnp
from jax import lax
from jax.experimental import pallas as pl
from jax.experimental.pallas import tpu as pltpu
from jax.sharding import PartitionSpec as P

F32 = jnp.float32
BF16 = jnp.bfloat16
VMEM_LIMIT = 12 * 1024 * 1024
PACK_VMEM = 61_816_832
CID_LANE = 25
SCALE_LANE = 24
MAP_LANE = 32
ROWS_AT_ONCE = 32
X_GROUP = 4
SUB_AT = 2
SIDE_AT = 3
COUNT_AT = 7
CHUNK = 128
BLOCK_ROWS = 32


def dot(left, right, contract=((1,), (0,))):
    return lax.dot_general(
        left, right, (contract, ((), ())), precision=lax.Precision.HIGHEST, preferred_element_type=F32
    )


def call(kernel, outs, vmem, smem=(), scratch=(), name=None, flops=0):
    specs = [pl.BlockSpec(memory_space=pltpu.SMEM)] * len(smem)
    specs += [pl.BlockSpec(memory_space=pltpu.VMEM)] * len(vmem)
    moved = sum(a.size * a.dtype.itemsize for a in vmem) + sum(o.size * o.dtype.itemsize for o in outs)
    return pl.pallas_call(
        kernel,
        out_shape=outs,
        in_specs=specs,
        out_specs=[pl.BlockSpec(memory_space=pltpu.VMEM)] * len(outs),
        scratch_shapes=list(scratch),
        compiler_params=pltpu.CompilerParams(vmem_limit_bytes=VMEM_LIMIT),
        cost_estimate=pl.CostEstimate(flops=flops, bytes_accessed=moved, transcendentals=0),
        name=name,
    )(*smem, *vmem)


def out(*shape, dtype=F32):
    return jax.ShapeDtypeStruct(shape, dtype)


def halves(value):
    high = value.astype(BF16)
    return high, (value - high.astype(F32)).astype(BF16)


def dot16(left, right):
    return jnp.dot(left, right, preferred_element_type=F32)


def live_block(count, slot, lanes):
    return lax.broadcasted_iota(jnp.int32, (slot, lanes), 0) < count


def pack_kernel(
    idx, rhs_in, basis_in, scaling_in, corners_in, cmap_in, ginv_in, pa, pb, pc, pd, crow, gpad,
    rhs, scaling, corners, ginv, wide, static, cpad, sems,
):
    cdof = basis_in.shape[0]
    slot = pa.shape[0] // 2
    lanes = pa.shape[1]
    wide[...] = jnp.zeros_like(wide)
    cpad[...] = jnp.zeros_like(cpad)
    moves = (
        (basis_in, wide.at[pl.ds(0, cdof)]),
        (scaling_in, scaling),
        (corners_in, corners),
        (cmap_in, cpad.at[pl.ds(MAP_LANE, cmap_in.shape[0])]),
        (ginv_in, ginv),
        (rhs_in, rhs),
    )
    copies = [
        pltpu.make_async_copy(source, target, sems.at[at])
        for at, (source, target) in enumerate(moves)
    ]
    for copy in copies:
        copy.start()
    for copy in copies[:-1]:
        copy.wait()
    gdof = ginv.shape[0]
    gpad[...] = jnp.zeros_like(gpad)
    gpad[MAP_LANE : MAP_LANE + gdof, :] = dot(ginv[...], ginv[...], ((0,), (0,)))
    wide[SCALE_LANE : SCALE_LANE + 1, :] = scaling[...]
    static[...] = wide[...].T
    row = corners[...].astype(F32)
    lane = lax.broadcasted_iota(jnp.int32, (cdof, cdof), 1)
    ids = jnp.sum(
        jnp.where(lane == lax.broadcasted_iota(jnp.int32, (cdof, cdof), 0), row, 0.0),
        axis=1,
        keepdims=True,
    )
    onehot = jnp.where(
        ids == lax.broadcasted_iota(jnp.int32, (cdof, cpad.shape[1]), 1).astype(F32), 1.0, 0.0
    ).astype(F32)
    extra = dot(onehot, cpad[...], ((1,), (1,)))
    lane = lax.broadcasted_iota(jnp.int32, extra.shape, 1)
    extra = jnp.where(lane == CID_LANE, ids, extra)
    lane = lax.broadcasted_iota(jnp.int32, (8, lanes), 1)
    crow[...] = jnp.where((lane >= cdof) & (lane < BLOCK_ROWS), -1.0, 0.0)
    crow[0:1, 0:cdof] = row
    copies[-1].wait()
    for block, ref in enumerate((pa, pb, pc, pd)):

        def move(step, carry, block=block, ref=ref):
            base = step * ROWS_AT_ONCE
            for r in range(ROWS_AT_ONCE):
                row = idx[block * slot + base + r]
                ref[pl.ds(base + r, 1), :] = rhs[pl.ds(row, 1), :]
                ref[pl.ds(slot + base + r, 1), :] = static[pl.ds(row, 1), :]
            return carry

        lax.fori_loop(0, slot // ROWS_AT_ONCE, move, 0)
        ref[slot : slot + cdof, :] = ref[slot : slot + cdof, :] + extra


def pack_rows(idx, rhs, basis, scaling, corners, cmap, ginv, slot):
    order, lanes = rhs.shape
    arrays = (rhs, basis, scaling, corners, cmap, ginv)
    outs = [out(2 * slot, lanes)] * 4 + [out(8, lanes), out(128, ginv.shape[0])]
    return pl.pallas_call(
        pack_kernel,
        out_shape=outs,
        in_specs=[pl.BlockSpec(memory_space=pltpu.SMEM)]
        + [pl.BlockSpec(memory_space=pltpu.HBM)] * len(arrays),
        out_specs=[pl.BlockSpec(memory_space=pltpu.VMEM)] * len(outs),
        scratch_shapes=[
            pltpu.VMEM((order, lanes), F32),
            pltpu.VMEM(scaling.shape, F32),
            pltpu.VMEM(corners.shape, jnp.int32),
            pltpu.VMEM(ginv.shape, F32),
            pltpu.VMEM((128, order), F32),
            pltpu.VMEM((order, 128), F32),
            pltpu.VMEM((128, cmap.shape[1]), F32),
            pltpu.SemaphoreType.DMA((len(arrays),)),
        ],
        compiler_params=pltpu.CompilerParams(vmem_limit_bytes=PACK_VMEM),
        name="pack",
    )(idx, *arrays)


def own_kernel(place, pa, pb, pc, pd, ct2):
    slot = pa.shape[0] // 2
    for block, mine in enumerate((pa, pb, pc, pd)):
        rows = slice(block * slot, (block + 1) * slot)
        stat = mine[slot : 2 * slot, :]
        lane = lax.broadcasted_iota(jnp.int32, stat.shape, 1)
        live = live_block(place[COUNT_AT + place[SIDE_AT + block]], slot, stat.shape[1])
        basis = jnp.where((lane < SCALE_LANE) & live, stat, 0.0).T[0:BLOCK_ROWS, :]
        high, low = halves(basis)
        ct2[0:BLOCK_ROWS, rows] = high
        ct2[BLOCK_ROWS : 2 * BLOCK_ROWS, rows] = low


def restricted(ct2, w2):
    lanes = w2.shape[1] // 2
    both = dot16(ct2[...], w2[...])
    return both[0:BLOCK_ROWS, 0:lanes] + (
        both[0:BLOCK_ROWS, lanes : 2 * lanes] + both[BLOCK_ROWS : 2 * BLOCK_ROWS, 0:lanes]
    )


def send(pay, values, sums):
    cdof = SCALE_LANE
    pay[0] = values
    for at, value in enumerate(sums):
        row = cdof + 1 + at
        pay[0, row : row + 1, :] = column_sum(value)
    message = pay[0]
    for other in range(1, pay.shape[0]):
        pay[other] = message


def sweep(slot):
    for block in range(4):
        for start in range(0, slot, CHUNK):
            yield block, slice(start, start + CHUNK), slice(
                block * slot + start, block * slot + start + CHUNK
            )


def live_chunk(place, block, rows, lanes):
    row = lax.broadcasted_iota(jnp.int32, (CHUNK, lanes), 0) + rows.start
    return row < place[COUNT_AT + place[SIDE_AT + block]]


def first_kernel(place, crow, pa, pb, pc, pd, qa, qb, qc, qd, ct2, r0, pay, w2):
    slot = pa.shape[0] // 2
    lanes = pa.shape[1]
    mine, theirs = (pa, pb, pc, pd), (qa, qb, qc, qd)
    for block, part, rows in sweep(slot):
        live = live_chunk(place, block, part, lanes)
        value = jnp.where(live, mine[block][part, :] - theirs[block][part, :], 0.0)
        r0[rows, :] = value
        w2[rows, 0:lanes], w2[rows, lanes : 2 * lanes] = halves(value)
    pay[...] = restricted(ct2, w2)
    pay[SCALE_LANE : SCALE_LANE + 1, :] = crow[0:1, :]


def join_kernel(*refs):
    *parts, whole = refs
    rows = parts[0].shape[0]
    for at, part in enumerate(parts):
        whole[at * rows : (at + 1) * rows, :] = part[...]


def static_kernel(place, pa, pb, pc, pd, qa, qb, qc, qd, r0, gpad, fts, ft, dsum, dsw, ng, nq):
    slot = pa.shape[0] // 2
    cdof = SCALE_LANE
    lanes = pa.shape[1]
    lane = lax.broadcasted_iota(jnp.int32, (CHUNK, lanes), 1)
    own = lane < cdof
    mine, theirs = (pa, pb, pc, pd), (qa, qb, qc, qd)
    nq[...] = jnp.zeros_like(nq)
    nq[0:cdof, :] = pa[slot : slot + cdof, :]
    for block in range(4):
        start = cdof * (block + 1)
        nq[start : start + cdof, :] = theirs[block][slot : slot + cdof, :]
    ng[...] = dot(nq[...], gpad[...])
    for block, part, rows in sweep(slot):
        live = live_chunk(place, block, part, lanes)
        low_rows = slice(slot + part.start, slot + part.stop)
        stat = mine[block][low_rows, :]
        other = theirs[block][low_rows, :]
        basis_mine = jnp.where(own & live, stat, 0.0)
        basis_other = jnp.where(own & live, other, 0.0)
        full = basis_mine - pltpu.roll(basis_other, cdof * (block + 1), 1)
        fts[rows, 0:lanes], fts[rows, lanes : 2 * lanes] = halves(full)
        ft[rows, :] = full
        weight = jnp.sum(
            jnp.where((lane == cdof) & live, stat + other, 0.0), axis=1, keepdims=True
        )
        weight = jnp.broadcast_to(weight, (CHUNK, lanes))
        dsum[rows, :] = weight
        dsw[rows, :] = weight * r0[rows, :]


def coarse_kernel(factor, coarse):
    coarse[...] = dot(factor[...], factor[...], ((0,), (0,)))


def split_kernel(x, split):
    lanes = x.shape[1]
    for start in range(0, x.shape[0], CHUNK):
        rows = slice(start, start + CHUNK)
        split[rows, 0:lanes], split[rows, lanes : 2 * lanes] = halves(x[rows, :])


def go_home(idx, pairs):
    def move(at, carry):
        base = at * ROWS_AT_ONCE
        for r in range(ROWS_AT_ONCE):
            row = idx[base + r]
            for source, target in pairs:
                target[pl.ds(row, 1), :] = source[pl.ds(base + r, 1), :]
        return carry

    lax.fori_loop(0, idx.shape[0] // ROWS_AT_ONCE, move, 0)


def halves_kernel(b, b2):
    rows = b.shape[1]
    b2[:, 0:rows], b2[:, rows : 2 * rows] = halves(b[...])


def split_operator(operator):
    rows = operator.shape[0]
    tile = 256
    return pl.pallas_call(
        halves_kernel,
        out_shape=out(rows, 2 * rows, dtype=BF16),
        grid=(rows // tile,),
        in_specs=[pl.BlockSpec((tile, rows), lambda i: (i, 0))],
        out_specs=pl.BlockSpec((tile, 2 * rows), lambda i: (i, 0)),
        compiler_params=pltpu.CompilerParams(vmem_limit_bytes=VMEM_LIMIT),
        cost_estimate=pl.CostEstimate(
            flops=0, bytes_accessed=8 * rows * rows, transcendentals=0
        ),
        name="halves",
    )(operator)


def operator_kernel(idx, x, b2, o, natural, split):
    rows, n = x.shape
    tile = rows // 2
    go_home(idx, ((x, natural),))
    for start in range(0, rows, CHUNK):
        part = slice(start, start + CHUNK)
        low_part = slice(rows + start, rows + start + CHUNK)
        high, low = halves(natural[part, :])
        split[part, 0:n] = high
        split[part, n : 2 * n] = low
        split[low_part, 0:n] = high
        split[low_part, n : 2 * n] = jnp.zeros((CHUNK, n), BF16)

    def multiply(at, carry):
        part = pl.ds(at * tile, tile)
        both = dot16(b2[part, :], split[...])
        natural[part, :] = both[:, 0:n] + both[:, n : 2 * n]
        return carry

    lax.fori_loop(0, rows // tile, multiply, 0)

    def move(at, carry):
        base = at * ROWS_AT_ONCE
        for r in range(ROWS_AT_ONCE):
            o[pl.ds(base + r, 1), :] = natural[pl.ds(idx[base + r], 1), :]
        return carry

    lax.fori_loop(0, rows // ROWS_AT_ONCE, move, 0)


def apply_operator(idx, x, b2):
    rows, n = x.shape
    (result,) = call(
        operator_kernel,
        [out(rows, n)],
        [x, b2],
        smem=[idx],
        scratch=[pltpu.VMEM((rows, n), F32), pltpu.VMEM((2 * rows, 2 * n), BF16)],
        name="operator",
        flops=6 * rows * rows * n,
    )
    return result


def gathered_product(y2, table, p1, cvab):
    lanes = p1.shape[1]
    both = dot16(table[...], y2[...])
    half = both.shape[0] // 2
    total = both[0:half, 0:lanes] + (both[0:half, lanes:] + both[half:, 0:lanes])
    top = p1.shape[0]
    p1[...] = total[0:top, :]
    cvab[...] = total[top:, :]


def table_kernel(ya, yb, yc, yd, pa, qa, qb, coarse, cmap, table, p1, cvab, reach2, y2):
    rows, lanes = BLOCK_ROWS, ya.shape[1]
    cdof = SCALE_LANE
    slot = pa.shape[0] // 2
    gdof, ccl = cmap.shape
    number = lax.broadcasted_iota(jnp.int32, (cdof, ccl), 1).astype(F32)
    chosen = [
        jnp.where(ref[slot : slot + cdof, CID_LANE : CID_LANE + 1] == number, 1.0, 0.0)
        for ref in (pa, qa, qb)
    ]
    reach = jnp.concatenate(
        [cmap[...], jnp.zeros((8, ccl), F32), dot(jnp.concatenate(chosen, axis=0), coarse[...])],
        axis=0,
    )
    reach2[0:128, :], reach2[128:256, :] = halves(reach)
    per = lanes // rows
    which = lax.broadcasted_iota(jnp.int32, (ccl, lanes), 0).astype(F32)
    row = lax.broadcasted_iota(jnp.int32, (256, lanes), 0)
    column = lax.broadcasted_iota(jnp.int32, (256, lanes), 1) % rows
    kept = (row - gdof == column - cdof) & (row > gdof) & (row < gdof + 8)
    unit = jnp.where(kept, 1.0, 0.0)
    for part, y in enumerate((ya, yb, yc, yd)):
        first = part * y.shape[0]
        y2[first : first + y.shape[0], 0:lanes], y2[first : first + y.shape[0], lanes:] = halves(
            y[...]
        )
        for group in range(0, y.shape[0], per * rows):
            ids = y[group + cdof : group + cdof + 8, :]
            for r in range(1, per):
                start = group + r * rows + cdof
                ids = ids + pltpu.roll(y[start : start + 8, :], r * rows, 1)
            onehot = jnp.where(which == ids[0:1, :], 1.0, 0.0).astype(BF16)
            at = slice(first + group, first + group + lanes)
            table[:, at] = (dot16(reach2[...], onehot) + unit).astype(BF16)
    gathered_product(y2, table, p1, cvab)


def corner_kernel(offsets, place, ya, yb, yc, yd, table, p1, cvab, y2):
    rows, lanes = BLOCK_ROWS, ya.shape[1]
    for part, y in enumerate((ya, yb, yc, yd)):
        for at, offset in enumerate(offsets):
            source = (place[SUB_AT] // X_GROUP) ^ offset
            value = y[pl.ds(pl.multiple_of(source * rows, rows), rows), :]
            to = part * y.shape[0] + at * rows
            y2[to : to + rows, 0:lanes], y2[to : to + rows, lanes:] = halves(value)
    gathered_product(y2, table, p1, cvab)


def pair_kernel(place, own, other, p2):
    cdof = SCALE_LANE
    top = own.shape[0] - cdof
    odd = place[0] == 1
    p2[0:top, :] = own[0:top, :] + other[0:top, :]
    mine = own[top : top + cdof, :]
    theirs = other[top : top + cdof, :]
    p2[top : top + cdof, :] = jnp.where(odd, theirs, mine)
    p2[top + cdof : top + 2 * cdof, :] = jnp.where(odd, mine, theirs)


def corner_values(place, p2, c2, c4, c6, cvab, ng, cv, cv2):
    cdof = SCALE_LANE
    top = p2.shape[0] - 2 * cdof
    gdof = top - 8
    lanes = cv.shape[1]
    even = slice(top, top + cdof)
    odd = slice(top + cdof, top + 2 * cdof)
    is_odd = place[0] == 1
    total = (p2[0:top, :] + c2[0:top, :]) + (c4[0:top, :] + c6[0:top, :])
    cv[0:cdof, :] = jnp.where(is_odd, p2[odd, :], p2[even, :])
    cv[cdof : 3 * cdof, :] = cvab[...]
    cv[3 * cdof : 4 * cdof, :] = jnp.where(is_odd, p2[even, :], p2[odd, :])
    far = place[1] == 1
    cv[4 * cdof : 5 * cdof, :] = jnp.where(
        is_odd,
        jnp.where(far, c6[even, :], c2[even, :]),
        jnp.where(far, c6[odd, :], c2[odd, :]),
    )
    cv[5 * cdof : 128, :] = jnp.zeros((128 - 5 * cdof, lanes), F32)
    high, low = halves(cv[...] + dot(ng[...], total[0:gdof, :]))
    cv2[0:128, 0:lanes] = high
    cv2[128:256, 0:lanes] = high
    cv2[0:128, lanes : 2 * lanes] = low
    cv2[128:256, lanes : 2 * lanes] = jnp.zeros((128, lanes), BF16)
    return total[gdof : gdof + 8, :]


def times_corner(matrix, rows, cv2):
    both = dot16(matrix[rows, :], cv2[...])
    lanes = both.shape[1] // 2
    return both[:, 0:lanes] + both[:, lanes:]


def column_sum(value):
    return jnp.sum(value, axis=0, keepdims=True)


def stage0_kernel(
    place, p2, c2, c4, c6, cvab, ng, t, bfs, cv2, ua, ub, uc, ud, cv
):
    corner_values(place, p2, c2, c4, c6, cvab, ng, cv, cv2)
    blocks = (ua, ub, uc, ud)
    for block, part, rows in sweep(ua.shape[0]):
        blocks[block][part, :] = t[rows, :] + times_corner(bfs, rows, cv2)


def shadow0_kernel(cv2, fts, dsw, v0):
    for start in range(0, v0.shape[0], CHUNK):
        rows = slice(start, start + CHUNK)
        v0[rows, :] = dsw[rows, :] + times_corner(fts, rows, cv2)


def shadow1_kernel(scal, cv2, fts, dsw, v0, r0, w0, v1, z1, r1):
    alpha = scal[0:1, :]
    for start in range(0, v0.shape[0], CHUNK):
        rows = slice(start, start + CHUNK)
        new = dsw[rows, :] + times_corner(fts, rows, cv2)
        v1[rows, :] = new
        z1[rows, :] = v0[rows, :] - alpha * new
        r1[rows, :] = r0[rows, :] - alpha * w0[rows, :]


def stage1_kernel(
    place, p2, c2, c4, c6, cvab, ng, bfs, t,
    u0a, u0b, u0c, u0d, cv2, bv1, scal, ua, ub, uc, ud, cv,
):
    dots = corner_values(place, p2, c2, c4, c6, cvab, ng, cv, cv2)
    alpha = dots[1:2, :] / dots[2:3, :]
    scal[...] = dots
    scal[0:1, :] = alpha
    olds, news = (u0a, u0b, u0c, u0d), (ua, ub, uc, ud)
    for block, part, rows in sweep(ua.shape[0]):
        image = t[rows, :] + times_corner(bfs, rows, cv2)
        bv1[rows, :] = image
        news[block][part, :] = olds[block][part, :] - alpha * image


def stage2_kernel(
    place, p2, c2, c4, c6, cvab, ng, fts, bfs, t, dsw, v0, w0, v1, bv1, z1, r1, s1, scal,
    u1a, u1b, u1c, u1d, z2, p1, r2, q1, scal2, dots2, ua, ub, uc, ud, cv, cv2,
):
    dots = corner_values(place, p2, c2, c4, c6, cvab, ng, cv, cv2)
    lanes = cv.shape[1]
    rz0 = scal[1:2, :]
    pq0 = scal[2:3, :]
    rz1 = dots[1:2, :]
    beta = rz1 / rz0
    pq1 = dots[2:3, :] + beta * (dots[3:4, :] + dots[4:5, :]) + beta * beta * pq0
    alpha = rz1 / pq1
    scal2[...] = jnp.zeros_like(scal2)
    scal2[0:1, :] = scal[0:1, :]
    scal2[1:2, :] = rz1
    scal2[2:3, :] = pq1
    scal2[3:4, :] = alpha
    olds, news = (u1a, u1b, u1c, u1d), (ua, ub, uc, ud)
    sums = [jnp.zeros((8, lanes), F32) for _ in range(4)]

    def folded(value):
        return jnp.sum(value.reshape(CHUNK // 8, 8, lanes), axis=0)

    for block, part, rows in sweep(ua.shape[0]):
        search = z1[rows, :] + beta * v0[rows, :]
        p1[rows, :] = search
        image_q = s1[rows, :] + beta * w0[rows, :]
        q1[rows, :] = image_q
        res = r1[rows, :] - alpha * image_q
        r2[rows, :] = res
        new = z1[rows, :] - alpha * (
            dsw[rows, :] + times_corner(fts, rows, cv2) + beta * v1[rows, :]
        )
        z2[rows, :] = new
        image = t[rows, :] + times_corner(bfs, rows, cv2) + beta * bv1[rows, :]
        fresh = olds[block][part, :] - alpha * image
        news[block][part, :] = fresh
        sums[0] = sums[0] + folded(res * new)
        sums[1] = sums[1] + folded(fresh * new)
        sums[2] = sums[2] + folded(image_q * new)
        sums[3] = sums[3] + folded(fresh * search)
    dots2[0] = jnp.zeros((8, lanes), F32)
    dots2[0, 1:2, :] = column_sum(sums[0])
    dots2[0, 2:3, :] = 2.0 * column_sum(sums[1])
    dots2[0, 3:4, :] = column_sum(sums[2])
    dots2[0, 4:5, :] = 2.0 * column_sum(sums[3])
    message = dots2[0]
    for other in range(1, dots2.shape[0]):
        dots2[other] = message


def jump_kernel(pairs, place, ua, ub, uc, ud, qa, qb, qc, qd, dsum, ct2, *rest):
    fields, (w, dsw, pay, w2) = rest[:-4], rest[-4:]
    lanes = w.shape[1]
    mine, theirs = (ua, ub, uc, ud), (qa, qb, qc, qd)
    sums = [jnp.zeros((8, lanes), F32) for _ in pairs]
    for block, part, rows in sweep(ua.shape[0]):
        live = live_chunk(place, block, part, lanes)
        value = jnp.where(live, mine[block][part, :] - theirs[block][part, :], 0.0)
        w[rows, :] = value
        dsw[rows, :] = dsum[rows, :] * value
        w2[rows, 0:lanes], w2[rows, lanes : 2 * lanes] = halves(value)
        for at, (left, right) in enumerate(pairs):
            first = value if left < 0 else fields[left][rows, :]
            product = first * fields[right][rows, :]
            sums[at] = sums[at] + jnp.sum(product.reshape(CHUNK // 8, 8, lanes), axis=0)
    send(pay, restricted(ct2, w2), sums)


def sum_kernel(x, o):
    o[...] = jnp.sum(x[...], axis=0)


def add_kernel(x, y, o):
    o[...] = x[...] + y[...]


def home_kernel(idx, scal2, z2, p1, v0, z2n, p1n, xsn, xs):
    xs[...] = scal2[0:1, :] * v0[...] + scal2[3:4, :] * p1[...]
    go_home(idx, ((z2, z2n), (p1, p1n), (xs, xsn)))


def last_kernel(
    place, idx, z2, p1, xs, r2, q1, ua, ub, uc, ud, qa, qb, qc, qd, scal2, d0, d2, d4, d6,
    mult, resid, work,
):
    dots = (d0[...] + d2[...]) + (d4[...] + d6[...])
    lanes = work.shape[1]
    beta = dots[1:2, :] / scal2[1:2, :]
    pq = dots[2:3, :] + beta * (dots[3:4, :] + dots[4:5, :]) + beta * beta * scal2[2:3, :]
    alpha = dots[1:2, :] / pq
    mine, theirs = (ua, ub, uc, ud), (qa, qb, qc, qd)
    for block, part, rows in sweep(ua.shape[0]):
        live = live_chunk(place, block, part, lanes)
        image = jnp.where(live, mine[block][part, :] - theirs[block][part, :], 0.0)
        work[rows, :] = r2[rows, :] - alpha * (image + beta * q1[rows, :])
        mult[rows, :] = xs[rows, :] + alpha * (z2[rows, :] + beta * p1[rows, :])
    go_home(idx, ((work, resid),))


def body(
    dual_ops,
    rhs,
    corner_basis,
    scaling,
    cluster_corner_inverse,
    coarse_map,
    global_inv,
    row_index,
    pair_counts,
    corner_map,
):
    operator = dual_ops[0, 0]
    loads = rhs[0, 0]
    basis = corner_basis[0, 0]
    weights = scaling[0]
    factor = cluster_corner_inverse[0]
    lift_map = coarse_map[0]
    row_ids = row_index[0, 0]
    corners = corner_map[0]
    slot = row_ids.shape[1]
    order, lanes = loads.shape
    cdof = basis.shape[0]
    subs = lax.axis_size("sub")
    clusters = lax.axis_size("cluster")
    gdof = lift_map.shape[0]

    s = lax.axis_index("sub")
    c = lax.axis_index("cluster")
    s_odd = s % 2
    c_odd = c % 2
    pairs_a = [(i, i ^ 1) for i in range(subs)]
    pairs_b = [(i, (i + 1) % subs) for i in range(1, subs, 2)]
    pairs_b += [(j, i) for i, j in pairs_b]
    pairs_c = [(i, i ^ 1) for i in range(clusters)]
    pairs_d = [(i, (i + 1) % clusters) for i in range(1, clusters, 2)]
    pairs_d += [(j, i) for i, j in pairs_d]
    across = [[(i, i ^ k) for i in range(clusters)] for k in (2, 4, 6)]

    chip = c // 2
    next_chip = jnp.where(c_odd == 1, chip + 1, chip - 1)
    far = ((chip ^ next_chip) == 3).astype(jnp.int32)
    def chosen(array):
        return [
            jnp.where(s_odd == 0, array[1], array[0]),
            jnp.where(s_odd == 0, array[0], array[1]),
            jnp.where(c_odd == 0, array[3], array[2]),
            jnp.where(c_odd == 0, array[2], array[3]),
        ]

    sides = (1 - s_odd, s_odd, 3 - c_odd, 2 + c_odd)
    place = jnp.stack([v.astype(jnp.int32) for v in (c_odd, far, s, *sides)])
    place = jnp.concatenate([place, pair_counts[0, 0]])
    idx = jnp.concatenate(chosen(row_ids))

    def exchange(blocks):
        return [
            lax.ppermute(blocks[0], "sub", pairs_a),
            lax.ppermute(blocks[1], "sub", pairs_b),
            lax.ppermute(blocks[2], "cluster", pairs_c),
            lax.ppermute(blocks[3], "cluster", pairs_d),
        ]

    def spread(messages, groups=None):
        return lax.all_to_all(messages, "sub", 0, 0, tiled=True, axis_index_groups=groups)

    z_count = subs // X_GROUP
    z_groups = [[X_GROUP * z + x for z in range(z_count)] for x in range(X_GROUP)]

    def together(*values):
        return lax.optimization_barrier(values)

    def clusterwise(p1, cvab):
        other = lax.ppermute(p1, "cluster", pairs_c)
        (p2,) = call(
            pair_kernel,
            [out(gdof + 8 + 2 * cdof, lanes)],
            [p1, other],
            smem=[place],
            name="pair",
        )
        moved = [lax.ppermute(p2, "cluster", k) for k in across]
        return [p2, *moved, cvab]

    block_out = [out(slot, lanes)] * 4
    full = out(order, lanes)
    small = [out(gdof + 8 + cdof, lanes), out(2 * cdof, lanes)]
    cv_scratch = [pltpu.VMEM((128, lanes), F32), pltpu.VMEM((256, 2 * lanes), BF16)]
    y2_scratch = [pltpu.VMEM((subs * BLOCK_ROWS, 2 * lanes), BF16)]
    cv2_out = out(256, 2 * lanes, dtype=BF16)
    w2_scratch = [pltpu.VMEM((order, 2 * lanes), BF16)]

    *packs, crow, gpad = pack_rows(
        idx, loads, basis, weights, corners, lift_map, global_inv, slot
    )
    packs_in = exchange(packs)
    (ct2,) = call(
        own_kernel, [out(2 * BLOCK_ROWS, order, dtype=BF16)], [*packs], smem=[place], name="own"
    )
    b2 = split_operator(operator)
    b2, ct2, *packs_in = together(b2, ct2, *packs_in)
    r0, pay = call(
        first_kernel,
        [full, out(BLOCK_ROWS, lanes)],
        [crow, *packs, *packs_in, ct2],
        smem=[place],
        scratch=w2_scratch,
        name="first",
    )

    def round_of(mine, steps):
        return [mine] + [
            lax.ppermute(mine, "sub", [(i, i ^ k) for i in range(subs)]) for k in steps
        ]

    def join(parts):
        rows = len(parts) * parts[0].shape[0]
        return call(join_kernel, [out(rows, lanes)], parts, name="join")[0]

    rounds = ((16,), (4, 8, 12), (1, 2, 3))
    offsets = (0,)
    for steps in rounds[:2]:
        offsets = tuple((k // X_GROUP) ^ o for k in (0, *steps) for o in offsets)
    y = round_of(pay, rounds[0])
    fts, ft, dsum, dsw, ng = call(
        static_kernel,
        [
            out(order, 2 * lanes, dtype=BF16),
            full,
            full,
            full,
            out(128, gdof),
        ],
        [*packs, *packs_in, r0, gpad],
        smem=[place],
        scratch=[pltpu.VMEM((128, lanes), F32)],
        name="static",
    )
    dsw, *y = together(dsw, *y)
    y = round_of(join(y), rounds[1])
    t = apply_operator(idx, dsw, b2)
    t, ft, *y = together(t, ft, *y)
    y = round_of(join(y), rounds[2])
    bf = apply_operator(idx, ft, b2)
    (bfs,) = call(split_kernel, [out(order, 2 * lanes, dtype=BF16)], [bf], name="split")
    (coarse,) = call(coarse_kernel, [out(*factor.shape)], [factor], name="coarse")
    bfs, coarse, *y = together(bfs, coarse, *y)
    table, p1, cvab = call(
        table_kernel,
        [out(256, subs * BLOCK_ROWS, dtype=BF16)] + small,
        [*y, packs[0], *packs_in[:2], coarse, lift_map],
        scratch=[pltpu.VMEM((256, factor.shape[0]), BF16), *y2_scratch],
        name="table",
    )
    cluster_part = clusterwise(p1, cvab)
    cv2, *u0 = call(
        stage0_kernel,
        [cv2_out] + block_out,
        [*cluster_part, ng, t, bfs],
        smem=[place],
        scratch=cv_scratch[:1],
        name="stage0",
    )
    u0_in = exchange(u0)
    (v0,) = call(shadow0_kernel, [full], [cv2, fts, dsw], name="shadow0")
    v0, *u0_in = together(v0, *u0_in)
    w0, dsw, pay = call(
        functools.partial(jump_kernel, ((0, 1), (-1, 1))),
        [full, full, out(z_count, BLOCK_ROWS, lanes)],
        [*u0, *u0_in, dsum, ct2, r0, v0],
        smem=[place],
        scratch=w2_scratch,
        name="jump1",
    )

    y = spread(pay, z_groups)
    y, dsw = together(y, dsw)
    y = round_of(y.reshape(z_count * BLOCK_ROWS, lanes), rounds[2])
    t = apply_operator(idx, dsw, b2)
    t, *y = together(t, *y)
    p1, cvab = call(
        functools.partial(corner_kernel, offsets),
        small,
        [*y, table],
        smem=[place],
        scratch=y2_scratch,
        name="corner",
    )
    cluster_part = clusterwise(p1, cvab)
    cv2, bv1, scal, *u1 = call(
        stage1_kernel,
        [cv2_out, full, out(8, lanes)] + block_out,
        [*cluster_part, ng, bfs, t, *u0],
        smem=[place],
        scratch=cv_scratch[:1],
        name="stage1",
    )
    u1_in = exchange(u1)
    v1, z1, r1 = call(
        shadow1_kernel, [full] * 3, [scal, cv2, fts, dsw, v0, r0, w0], name="shadow1"
    )
    v1, z1, r1, *u1_in = together(v1, z1, r1, *u1_in)
    s1, dsw, pay = call(
        functools.partial(jump_kernel, ((0, 1), (-1, 1), (2, 1), (-1, 3))),
        [full, full, out(z_count, BLOCK_ROWS, lanes)],
        [*u1, *u1_in, dsum, ct2, r1, z1, w0, v0],
        smem=[place],
        scratch=w2_scratch,
        name="jump2",
    )

    y = spread(pay, z_groups)
    y, dsw = together(y, dsw)
    y = round_of(y.reshape(z_count * BLOCK_ROWS, lanes), rounds[2])
    t = apply_operator(idx, dsw, b2)
    t, *y = together(t, *y)
    p1, cvab = call(
        functools.partial(corner_kernel, offsets),
        small,
        [*y, table],
        smem=[place],
        scratch=y2_scratch,
        name="corner",
    )
    cluster_part = clusterwise(p1, cvab)
    z2, p1, r2, q1, scal2, dots2, *u2 = call(
        stage2_kernel,
        [full] * 4 + [out(8, lanes), out(subs, 8, lanes)] + block_out,
        [*cluster_part, ng, fts, bfs, t, dsw, v0, w0, v1, bv1, z1, r1, s1, scal, *u1],
        smem=[place],
        scratch=cv_scratch,
        name="stage2",
    )

    dots = spread(dots2)
    dots, z2, scal2, *u2 = together(dots, z2, scal2, *u2)
    u2_in = exchange(u2)
    (dots,) = call(sum_kernel, [out(8, lanes)], [dots], name="sum")
    other = lax.ppermute(dots, "cluster", pairs_c)
    (dots,) = call(add_kernel, [out(8, lanes)], [dots, other], name="add")
    moved = [lax.ppermute(dots, "cluster", k) for k in across]
    home = call(
        home_kernel,
        [full] * 3,
        [scal2, z2, p1, v0],
        smem=[idx],
        scratch=[pltpu.VMEM((order, lanes), F32)],
        name="home",
        flops=4_000_000_000,
    )
    multipliers, residual = call(
        last_kernel,
        [full, full],
        [*home, r2, q1, *u2, *u2_in, scal2, dots, *moved],
        smem=[place, idx],
        scratch=[pltpu.VMEM((order, lanes), F32)],
        name="last",
    )
    return (multipliers[None, None], residual[None, None])


def solution(mesh):
    in_specs = (
        P("cluster", "sub", None, None),
        P("cluster", "sub", None, None),
        P("cluster", "sub", None, None),
        P("cluster", "sub", None),
        P("cluster", None, None),
        P("cluster", None, None),
        P(),
        P("cluster", "sub", None, None),
        P("cluster", "sub", None),
        P("cluster", "sub", None),
    )
    out_specs = (P("cluster", "sub", None, None), P("cluster", "sub", None, None))
    return jax.shard_map(body, mesh=mesh, in_specs=in_specs, out_specs=out_specs, check_vma=False)
```

```python
import functools

import jax
import jax.numpy as jnp
from jax import lax
from jax.experimental import pallas as pl
from jax.experimental.pallas import tpu as pltpu
from jax.sharding import PartitionSpec as P

F32 = jnp.float32
BF16 = jnp.bfloat16
VMEM_LIMIT = 12 * 1024 * 1024
PACK_VMEM = 61_890_560
HALVES_VMEM = 42_000_384
CID_LANE = 25
SCALE_LANE = 24
MAP_LANE = 32
ROWS_AT_ONCE = 32
X_GROUP = 4
SUB_AT = 2
SIDE_AT = 3
COUNT_AT = 7
CHUNK = 128
BLOCK_ROWS = 32


def dot(left, right, contract=((1,), (0,))):
    return lax.dot_general(
        left, right, (contract, ((), ())), precision=lax.Precision.HIGHEST, preferred_element_type=F32
    )


def call(kernel, outs, vmem, smem=(), scratch=(), name=None, flops=0):
    specs = [pl.BlockSpec(memory_space=pltpu.SMEM)] * len(smem)
    specs += [pl.BlockSpec(memory_space=pltpu.VMEM)] * len(vmem)
    moved = sum(a.size * a.dtype.itemsize for a in vmem) + sum(o.size * o.dtype.itemsize for o in outs)
    return pl.pallas_call(
        kernel,
        out_shape=outs,
        in_specs=specs,
        out_specs=[pl.BlockSpec(memory_space=pltpu.VMEM)] * len(outs),
        scratch_shapes=list(scratch),
        compiler_params=pltpu.CompilerParams(vmem_limit_bytes=VMEM_LIMIT),
        cost_estimate=pl.CostEstimate(flops=flops, bytes_accessed=moved, transcendentals=0),
        name=name,
    )(*smem, *vmem)


def out(*shape, dtype=F32):
    return jax.ShapeDtypeStruct(shape, dtype)


def halves(value):
    high = value.astype(BF16)
    return high, (value - high.astype(F32)).astype(BF16)


def dot16(left, right):
    return jnp.dot(left, right, preferred_element_type=F32)


def live_block(count, slot, lanes):
    return lax.broadcasted_iota(jnp.int32, (slot, lanes), 0) < count


def pack_kernel(
    idx, rhs_in, basis_in, scaling_in, corners_in, cmap_in, pa, pb, pc, pd, crow,
    rhs, scaling, corners, wide, static, cpad, sems,
):
    cdof = basis_in.shape[0]
    slot = pa.shape[0] // 2
    lanes = pa.shape[1]
    wide[...] = jnp.zeros_like(wide)
    cpad[...] = jnp.zeros_like(cpad)
    moves = (
        (basis_in, wide.at[pl.ds(0, cdof)]),
        (scaling_in, scaling),
        (corners_in, corners),
        (cmap_in, cpad.at[pl.ds(MAP_LANE, cmap_in.shape[0])]),
        (rhs_in, rhs),
    )
    copies = [
        pltpu.make_async_copy(source, target, sems.at[at])
        for at, (source, target) in enumerate(moves)
    ]
    for copy in copies:
        copy.start()
    for copy in copies[:-1]:
        copy.wait()
    wide[SCALE_LANE : SCALE_LANE + 1, :] = scaling[...]
    static[...] = wide[...].T
    row = corners[...].astype(F32)
    lane = lax.broadcasted_iota(jnp.int32, (cdof, cdof), 1)
    ids = jnp.sum(
        jnp.where(lane == lax.broadcasted_iota(jnp.int32, (cdof, cdof), 0), row, 0.0),
        axis=1,
        keepdims=True,
    )
    onehot = jnp.where(
        ids == lax.broadcasted_iota(jnp.int32, (cdof, cpad.shape[1]), 1).astype(F32), 1.0, 0.0
    ).astype(F32)
    extra = dot(onehot, cpad[...], ((1,), (1,)))
    lane = lax.broadcasted_iota(jnp.int32, extra.shape, 1)
    extra = jnp.where(lane == CID_LANE, ids, extra)
    lane = lax.broadcasted_iota(jnp.int32, (8, lanes), 1)
    crow[...] = jnp.where((lane >= cdof) & (lane < BLOCK_ROWS), -1.0, 0.0)
    crow[0:1, 0:cdof] = row
    copies[-1].wait()
    for block, ref in enumerate((pa, pb, pc, pd)):

        def move(step, carry, block=block, ref=ref):
            base = step * ROWS_AT_ONCE
            for r in range(ROWS_AT_ONCE):
                row = idx[block * slot + base + r]
                ref[pl.ds(base + r, 1), :] = rhs[pl.ds(row, 1), :]
                ref[pl.ds(slot + base + r, 1), :] = static[pl.ds(row, 1), :]
            return carry

        lax.fori_loop(0, slot // ROWS_AT_ONCE, move, 0)
        ref[slot : slot + cdof, :] = ref[slot : slot + cdof, :] + extra


def pack_rows(idx, rhs, basis, scaling, corners, cmap, slot):
    order, lanes = rhs.shape
    arrays = (rhs, basis, scaling, corners, cmap)
    outs = [out(2 * slot, lanes)] * 4 + [out(8, lanes)]
    return pl.pallas_call(
        pack_kernel,
        out_shape=outs,
        in_specs=[pl.BlockSpec(memory_space=pltpu.SMEM)]
        + [pl.BlockSpec(memory_space=pltpu.HBM)] * len(arrays),
        out_specs=[pl.BlockSpec(memory_space=pltpu.VMEM)] * len(outs),
        scratch_shapes=[
            pltpu.VMEM((order, lanes), F32),
            pltpu.VMEM(scaling.shape, F32),
            pltpu.VMEM(corners.shape, jnp.int32),
            pltpu.VMEM((128, order), F32),
            pltpu.VMEM((order, 128), F32),
            pltpu.VMEM((128, cmap.shape[1]), F32),
            pltpu.SemaphoreType.DMA((len(arrays),)),
        ],
        compiler_params=pltpu.CompilerParams(vmem_limit_bytes=PACK_VMEM),
        name="pack",
    )(idx, *arrays)


def own_kernel(place, pa, pb, pc, pd, ct2):
    slot = pa.shape[0] // 2
    for block, mine in enumerate((pa, pb, pc, pd)):
        rows = slice(block * slot, (block + 1) * slot)
        stat = mine[slot : 2 * slot, :]
        lane = lax.broadcasted_iota(jnp.int32, stat.shape, 1)
        live = live_block(place[COUNT_AT + place[SIDE_AT + block]], slot, stat.shape[1])
        basis = jnp.where((lane < SCALE_LANE) & live, stat, 0.0).T[0:BLOCK_ROWS, :]
        high, low = halves(basis)
        ct2[0:BLOCK_ROWS, rows] = high
        ct2[BLOCK_ROWS : 2 * BLOCK_ROWS, rows] = low


def restricted(ct2, w2):
    lanes = w2.shape[1] // 2
    both = dot16(ct2[...], w2[...])
    return both[0:BLOCK_ROWS, 0:lanes] + (
        both[0:BLOCK_ROWS, lanes : 2 * lanes] + both[BLOCK_ROWS : 2 * BLOCK_ROWS, 0:lanes]
    )


def send(pay, values, extra, start):
    pay[0] = values
    for at, row in enumerate(extra):
        pay[0, start + at : start + at + 1, :] = row
    message = pay[0]
    for other in range(1, pay.shape[0]):
        pay[other] = message


def sweep(slot):
    for block in range(4):
        for start in range(0, slot, CHUNK):
            yield block, slice(start, start + CHUNK), slice(
                block * slot + start, block * slot + start + CHUNK
            )


def live_chunk(place, block, rows, lanes):
    row = lax.broadcasted_iota(jnp.int32, (CHUNK, lanes), 0) + rows.start
    return row < place[COUNT_AT + place[SIDE_AT + block]]


def first_kernel(place, crow, pa, pb, pc, pd, qa, qb, qc, qd, ct2, r0, pay, w2):
    slot = pa.shape[0] // 2
    lanes = pa.shape[1]
    mine, theirs = (pa, pb, pc, pd), (qa, qb, qc, qd)
    for block, part, rows in sweep(slot):
        live = live_chunk(place, block, part, lanes)
        value = jnp.where(live, mine[block][part, :] - theirs[block][part, :], 0.0)
        r0[rows, :] = value
        w2[rows, 0:lanes], w2[rows, lanes : 2 * lanes] = halves(value)
    send(pay, restricted(ct2, w2), [crow[0:1, :]], SCALE_LANE)


def static_kernel(place, pa, pb, pc, pd, qa, qb, qc, qd, r0, gpad, fts, ft, dsum, dsw, ng, nq):
    slot = pa.shape[0] // 2
    cdof = SCALE_LANE
    lanes = pa.shape[1]
    lane = lax.broadcasted_iota(jnp.int32, (CHUNK, lanes), 1)
    own = lane < cdof
    mine, theirs = (pa, pb, pc, pd), (qa, qb, qc, qd)
    nq[...] = jnp.zeros_like(nq)
    nq[0:cdof, :] = pa[slot : slot + cdof, :]
    for block in range(4):
        start = cdof * (block + 1)
        nq[start : start + cdof, :] = theirs[block][slot : slot + cdof, :]
    ng[...] = dot(nq[...], gpad[...])
    for block, part, rows in sweep(slot):
        live = live_chunk(place, block, part, lanes)
        low_rows = slice(slot + part.start, slot + part.stop)
        stat = mine[block][low_rows, :]
        other = theirs[block][low_rows, :]
        basis_mine = jnp.where(own & live, stat, 0.0)
        basis_other = jnp.where(own & live, other, 0.0)
        full = basis_mine - pltpu.roll(basis_other, cdof * (block + 1), 1)
        fts[rows, 0:lanes], fts[rows, lanes : 2 * lanes] = halves(full)
        ft[rows, :] = full
        weight = jnp.sum(
            jnp.where((lane == cdof) & live, stat + other, 0.0), axis=1, keepdims=True
        )
        weight = jnp.broadcast_to(weight, (CHUNK, lanes))
        dsum[rows, :] = weight
        dsw[rows, :] = weight * r0[rows, :]


def coarse_kernel(factor, ginv, coarse, gpad):
    gdof = ginv.shape[0]
    coarse[...] = dot(factor[...], factor[...], ((0,), (0,)))
    gpad[...] = jnp.zeros_like(gpad)
    gpad[MAP_LANE : MAP_LANE + gdof, :] = dot(ginv[...], ginv[...], ((0,), (0,)))


def split_kernel(x, split):
    lanes = x.shape[1]
    for start in range(0, x.shape[0], CHUNK):
        rows = slice(start, start + CHUNK)
        split[rows, 0:lanes], split[rows, lanes : 2 * lanes] = halves(x[rows, :])


def go_home(idx, pairs):
    def move(at, carry):
        base = at * ROWS_AT_ONCE
        for r in range(ROWS_AT_ONCE):
            row = idx[base + r]
            for source, target in pairs:
                target[pl.ds(row, 1), :] = source[pl.ds(base + r, 1), :]
        return carry

    lax.fori_loop(0, idx.shape[0] // ROWS_AT_ONCE, move, 0)


def halves_kernel(b, b2, parts, sems):
    count, tile, rows = parts.shape
    copies = [
        pltpu.make_async_copy(b.at[pl.ds(at * tile, tile)], parts.at[at], sems.at[at])
        for at in range(count)
    ]
    for copy in copies:
        copy.start()
    for at, copy in enumerate(copies):
        copy.wait()
        for start in range(0, tile, 64):
            value = parts[at, start : start + 64, :]
            part = slice(at * tile + start, at * tile + start + 64)
            b2[part, 0:rows], b2[part, rows : 2 * rows] = halves(value)


def split_operator(operator):
    rows = operator.shape[0]
    count = 6
    return pl.pallas_call(
        halves_kernel,
        out_shape=out(rows, 2 * rows, dtype=BF16),
        in_specs=[pl.BlockSpec(memory_space=pltpu.HBM)],
        out_specs=pl.BlockSpec(memory_space=pltpu.VMEM),
        scratch_shapes=[
            pltpu.VMEM((count, rows // count, rows), F32),
            pltpu.SemaphoreType.DMA((count,)),
        ],
        compiler_params=pltpu.CompilerParams(vmem_limit_bytes=HALVES_VMEM),
        cost_estimate=pl.CostEstimate(
            flops=0, bytes_accessed=8 * rows * rows, transcendentals=0
        ),
        name="halves",
    )(operator)


def operator_kernel(idx, x, b2, o, natural, split):
    rows, n = x.shape
    tile = rows // 2
    go_home(idx, ((x, natural),))
    for start in range(0, rows, CHUNK):
        part = slice(start, start + CHUNK)
        low_part = slice(rows + start, rows + start + CHUNK)
        high, low = halves(natural[part, :])
        split[part, 0:n] = high
        split[part, n : 2 * n] = low
        split[low_part, 0:n] = high
        split[low_part, n : 2 * n] = jnp.zeros((CHUNK, n), BF16)

    def multiply(at, carry):
        part = pl.ds(at * tile, tile)
        both = dot16(b2[part, :], split[...])
        natural[part, :] = both[:, 0:n] + both[:, n : 2 * n]
        return carry

    lax.fori_loop(0, rows // tile, multiply, 0)

    def move(at, carry):
        base = at * ROWS_AT_ONCE
        for r in range(ROWS_AT_ONCE):
            o[pl.ds(base + r, 1), :] = natural[pl.ds(idx[base + r], 1), :]
        return carry

    lax.fori_loop(0, rows // ROWS_AT_ONCE, move, 0)


def apply_operator(idx, x, b2):
    rows, n = x.shape
    (result,) = call(
        operator_kernel,
        [out(rows, n)],
        [x, b2],
        smem=[idx],
        scratch=[pltpu.VMEM((rows, n), F32), pltpu.VMEM((2 * rows, 2 * n), BF16)],
        name="operator",
        flops=6 * rows * rows * n,
    )
    return result


def gathered_product(y2, table, p1, cvab):
    lanes = p1.shape[1]
    both = dot16(table[...], y2[...])
    half = both.shape[0] // 2
    total = both[0:half, 0:lanes] + (both[0:half, lanes:] + both[half:, 0:lanes])
    top = p1.shape[0]
    p1[...] = total[0:top, :]
    cvab[...] = total[top:, :]


def table_kernel(ya, yb, yc, yd, pa, qa, qb, coarse, cmap, table, p1, cvab, reach2, y2):
    rows, lanes = BLOCK_ROWS, ya.shape[1]
    cdof = SCALE_LANE
    slot = pa.shape[0] // 2
    gdof, ccl = cmap.shape
    number = lax.broadcasted_iota(jnp.int32, (cdof, ccl), 1).astype(F32)
    chosen = [
        jnp.where(ref[slot : slot + cdof, CID_LANE : CID_LANE + 1] == number, 1.0, 0.0)
        for ref in (pa, qa, qb)
    ]
    reach = jnp.concatenate(
        [cmap[...], jnp.zeros((8, ccl), F32), dot(jnp.concatenate(chosen, axis=0), coarse[...])],
        axis=0,
    )
    reach2[0:128, :], reach2[128:256, :] = halves(reach)
    per = lanes // rows
    which = lax.broadcasted_iota(jnp.int32, (ccl, lanes), 0).astype(F32)
    row = lax.broadcasted_iota(jnp.int32, (256, lanes), 0)
    column = lax.broadcasted_iota(jnp.int32, (256, lanes), 1) % rows
    kept = (row - gdof == column - cdof) & (row > gdof) & (row < gdof + 8)
    unit = jnp.where(kept, 1.0, 0.0)
    for part, y in enumerate((ya, yb, yc, yd)):
        first = part * y.shape[0]
        y2[first : first + y.shape[0], 0:lanes], y2[first : first + y.shape[0], lanes:] = halves(
            y[...]
        )
        for group in range(0, y.shape[0], per * rows):
            ids = y[group + cdof : group + cdof + 8, :]
            for r in range(1, per):
                start = group + r * rows + cdof
                ids = ids + pltpu.roll(y[start : start + 8, :], r * rows, 1)
            onehot = jnp.where(which == ids[0:1, :], 1.0, 0.0).astype(BF16)
            at = slice(first + group, first + group + lanes)
            table[:, at] = (dot16(reach2[...], onehot) + unit).astype(BF16)
    gathered_product(y2, table, p1, cvab)


def corner_kernel(ya, yb, yc, yd, table, p1, cvab, y2):
    lanes = ya.shape[1]
    for part, y in enumerate((ya, yb, yc, yd)):
        rows = slice(part * y.shape[0], (part + 1) * y.shape[0])
        y2[rows, 0:lanes], y2[rows, lanes:] = halves(y[...])
    gathered_product(y2, table, p1, cvab)


def pair_kernel(place, own, other, p2):
    cdof = SCALE_LANE
    top = own.shape[0] - cdof
    odd = place[0] == 1
    p2[0:top, :] = own[0:top, :] + other[0:top, :]
    mine = own[top : top + cdof, :]
    theirs = other[top : top + cdof, :]
    p2[top : top + cdof, :] = jnp.where(odd, theirs, mine)
    p2[top + cdof : top + 2 * cdof, :] = jnp.where(odd, mine, theirs)


def corner_values(place, p2, c2, c4, c6, cvab, ng, cv, cv2):
    cdof = SCALE_LANE
    top = p2.shape[0] - 2 * cdof
    gdof = top - 8
    lanes = cv.shape[1]
    even = slice(top, top + cdof)
    odd = slice(top + cdof, top + 2 * cdof)
    is_odd = place[0] == 1
    total = (p2[0:top, :] + c2[0:top, :]) + (c4[0:top, :] + c6[0:top, :])
    cv[0:cdof, :] = jnp.where(is_odd, p2[odd, :], p2[even, :])
    cv[cdof : 3 * cdof, :] = cvab[...]
    cv[3 * cdof : 4 * cdof, :] = jnp.where(is_odd, p2[even, :], p2[odd, :])
    far = place[1] == 1
    cv[4 * cdof : 5 * cdof, :] = jnp.where(
        is_odd,
        jnp.where(far, c6[even, :], c2[even, :]),
        jnp.where(far, c6[odd, :], c2[odd, :]),
    )
    cv[5 * cdof : 128, :] = jnp.zeros((128 - 5 * cdof, lanes), F32)
    high, low = halves(cv[...] + dot(ng[...], total[0:gdof, :]))
    cv2[0:128, 0:lanes] = high
    cv2[128:256, 0:lanes] = high
    cv2[0:128, lanes : 2 * lanes] = low
    cv2[128:256, lanes : 2 * lanes] = jnp.zeros((128, lanes), BF16)
    return total[gdof : gdof + 8, :]


def times_corner(matrix, rows, cv2):
    both = dot16(matrix[rows, :], cv2[...])
    lanes = both.shape[1] // 2
    return both[:, 0:lanes] + both[:, lanes:]


def column_sum(value):
    return jnp.sum(value, axis=0, keepdims=True)


def stage0_kernel(
    place, p2, c2, c4, c6, cvab, ng, t, bfs, cv2, ua, ub, uc, ud, cv
):
    corner_values(place, p2, c2, c4, c6, cvab, ng, cv, cv2)
    blocks = (ua, ub, uc, ud)
    for block, part, rows in sweep(ua.shape[0]):
        blocks[block][part, :] = t[rows, :] + times_corner(bfs, rows, cv2)


def shadow0_kernel(cv2, fts, dsw, v0):
    for start in range(0, v0.shape[0], CHUNK):
        rows = slice(start, start + CHUNK)
        v0[rows, :] = dsw[rows, :] + times_corner(fts, rows, cv2)


def shadow1_kernel(scal, cv2, fts, dsw, v0, r0, w0, v1, z1, r1):
    alpha = scal[0:1, :]
    for start in range(0, v0.shape[0], CHUNK):
        rows = slice(start, start + CHUNK)
        new = dsw[rows, :] + times_corner(fts, rows, cv2)
        v1[rows, :] = new
        z1[rows, :] = v0[rows, :] - alpha * new
        r1[rows, :] = r0[rows, :] - alpha * w0[rows, :]


def stage1_kernel(
    place, p2, c2, c4, c6, cvab, ng, bfs, t,
    u0a, u0b, u0c, u0d, cv2, bv1, scal, ua, ub, uc, ud, cv,
):
    dots = corner_values(place, p2, c2, c4, c6, cvab, ng, cv, cv2)
    alpha = dots[1:2, :] / dots[2:3, :]
    scal[...] = dots
    scal[0:1, :] = alpha
    olds, news = (u0a, u0b, u0c, u0d), (ua, ub, uc, ud)
    for block, part, rows in sweep(ua.shape[0]):
        image = t[rows, :] + times_corner(bfs, rows, cv2)
        bv1[rows, :] = image
        news[block][part, :] = olds[block][part, :] - alpha * image


def stage2_kernel(
    place, p2, c2, c4, c6, cvab, ng, fts, bfs, t, dsw, v0, w0, v1, bv1, z1, r1, s1, scal,
    u1a, u1b, u1c, u1d, z2, p1, r2, q1, scal2, dots2, ua, ub, uc, ud, cv, cv2,
):
    dots = corner_values(place, p2, c2, c4, c6, cvab, ng, cv, cv2)
    lanes = cv.shape[1]
    rz0 = scal[1:2, :]
    pq0 = scal[2:3, :]
    rz1 = dots[1:2, :]
    beta = rz1 / rz0
    pq1 = dots[2:3, :] + beta * (dots[3:4, :] + dots[4:5, :]) + beta * beta * pq0
    alpha = rz1 / pq1
    scal2[...] = jnp.zeros_like(scal2)
    scal2[0:1, :] = scal[0:1, :]
    scal2[1:2, :] = rz1
    scal2[2:3, :] = pq1
    scal2[3:4, :] = alpha
    olds, news = (u1a, u1b, u1c, u1d), (ua, ub, uc, ud)
    sums = [jnp.zeros((8, lanes), F32) for _ in range(4)]

    def folded(value):
        return jnp.sum(value.reshape(CHUNK // 8, 8, lanes), axis=0)

    for block, part, rows in sweep(ua.shape[0]):
        search = z1[rows, :] + beta * v0[rows, :]
        p1[rows, :] = search
        image_q = s1[rows, :] + beta * w0[rows, :]
        q1[rows, :] = image_q
        res = r1[rows, :] - alpha * image_q
        r2[rows, :] = res
        new = z1[rows, :] - alpha * (
            dsw[rows, :] + times_corner(fts, rows, cv2) + beta * v1[rows, :]
        )
        z2[rows, :] = new
        image = t[rows, :] + times_corner(bfs, rows, cv2) + beta * bv1[rows, :]
        fresh = olds[block][part, :] - alpha * image
        news[block][part, :] = fresh
        sums[0] = sums[0] + folded(res * new)
        sums[1] = sums[1] + folded(fresh * new)
        sums[2] = sums[2] + folded(image_q * new)
        sums[3] = sums[3] + folded(fresh * search)
    dots2[0] = jnp.zeros((8, lanes), F32)
    dots2[0, 1:2, :] = column_sum(sums[0])
    dots2[0, 2:3, :] = 2.0 * column_sum(sums[1])
    dots2[0, 3:4, :] = column_sum(sums[2])
    dots2[0, 4:5, :] = 2.0 * column_sum(sums[3])
    message = dots2[0]
    for other in range(1, dots2.shape[0]):
        dots2[other] = message


def jump_kernel(pairs, place, ua, ub, uc, ud, qa, qb, qc, qd, dsum, ct2, *rest):
    fields, (w, dsw, pay, w2) = rest[:-4], rest[-4:]
    lanes = w.shape[1]
    mine, theirs = (ua, ub, uc, ud), (qa, qb, qc, qd)
    sums = [jnp.zeros((8, lanes), F32) for _ in pairs]
    for block, part, rows in sweep(ua.shape[0]):
        live = live_chunk(place, block, part, lanes)
        value = jnp.where(live, mine[block][part, :] - theirs[block][part, :], 0.0)
        w[rows, :] = value
        dsw[rows, :] = dsum[rows, :] * value
        w2[rows, 0:lanes], w2[rows, lanes : 2 * lanes] = halves(value)
        for at, (left, right) in enumerate(pairs):
            first = value if left < 0 else fields[left][rows, :]
            product = first * fields[right][rows, :]
            sums[at] = sums[at] + jnp.sum(product.reshape(CHUNK // 8, 8, lanes), axis=0)
    send(pay, restricted(ct2, w2), [column_sum(v) for v in sums], SCALE_LANE + 1)


def sum_kernel(x, o):
    o[...] = jnp.sum(x[...], axis=0)


def add_kernel(first, *rest):
    *others, o = rest
    total = first[...]
    for other in others:
        total = total + other[...]
    o[...] = total


def home_kernel(idx, scal2, z2, p1, v0, z2n, p1n, xsn, xs):
    xs[...] = scal2[0:1, :] * v0[...] + scal2[3:4, :] * p1[...]
    go_home(idx, ((z2, z2n), (p1, p1n), (xs, xsn)))


def last_kernel(
    place, idx, z2, p1, xs, r2, q1, ua, ub, uc, ud, qa, qb, qc, qd, scal2, d0, d2, d4, d6,
    mult, resid, work,
):
    dots = (d0[...] + d2[...]) + (d4[...] + d6[...])
    lanes = work.shape[1]
    beta = dots[1:2, :] / scal2[1:2, :]
    pq = dots[2:3, :] + beta * (dots[3:4, :] + dots[4:5, :]) + beta * beta * scal2[2:3, :]
    alpha = dots[1:2, :] / pq
    mine, theirs = (ua, ub, uc, ud), (qa, qb, qc, qd)
    for block, part, rows in sweep(ua.shape[0]):
        live = live_chunk(place, block, part, lanes)
        image = jnp.where(live, mine[block][part, :] - theirs[block][part, :], 0.0)
        work[rows, :] = r2[rows, :] - alpha * (image + beta * q1[rows, :])
        mult[rows, :] = xs[rows, :] + alpha * (z2[rows, :] + beta * p1[rows, :])
    go_home(idx, ((work, resid),))


def body(
    dual_ops,
    rhs,
    corner_basis,
    scaling,
    cluster_corner_inverse,
    coarse_map,
    global_inv,
    row_index,
    pair_counts,
    corner_map,
):
    operator = dual_ops[0, 0]
    loads = rhs[0, 0]
    basis = corner_basis[0, 0]
    weights = scaling[0]
    factor = cluster_corner_inverse[0]
    lift_map = coarse_map[0]
    row_ids = row_index[0, 0]
    corners = corner_map[0]
    slot = row_ids.shape[1]
    order, lanes = loads.shape
    cdof = basis.shape[0]
    subs = lax.axis_size("sub")
    clusters = lax.axis_size("cluster")
    gdof = lift_map.shape[0]

    s = lax.axis_index("sub")
    c = lax.axis_index("cluster")
    s_odd = s % 2
    c_odd = c % 2
    pairs_a = [(i, i ^ 1) for i in range(subs)]
    pairs_b = [(i, (i + 1) % subs) for i in range(1, subs, 2)]
    pairs_b += [(j, i) for i, j in pairs_b]
    pairs_c = [(i, i ^ 1) for i in range(clusters)]
    pairs_d = [(i, (i + 1) % clusters) for i in range(1, clusters, 2)]
    pairs_d += [(j, i) for i, j in pairs_d]
    across = [[(i, i ^ k) for i in range(clusters)] for k in (2, 4, 6)]

    chip = c // 2
    next_chip = jnp.where(c_odd == 1, chip + 1, chip - 1)
    far = ((chip ^ next_chip) == 3).astype(jnp.int32)
    def chosen(array):
        return [
            jnp.where(s_odd == 0, array[1], array[0]),
            jnp.where(s_odd == 0, array[0], array[1]),
            jnp.where(c_odd == 0, array[3], array[2]),
            jnp.where(c_odd == 0, array[2], array[3]),
        ]

    sides = (1 - s_odd, s_odd, 3 - c_odd, 2 + c_odd)
    place = jnp.stack([v.astype(jnp.int32) for v in (c_odd, far, s, *sides)])
    place = jnp.concatenate([place, pair_counts[0, 0]])
    idx = jnp.concatenate(chosen(row_ids))
    idx, place = lax.optimization_barrier((idx, place))

    def exchange(blocks):
        return [
            lax.ppermute(blocks[0], "sub", pairs_a),
            lax.ppermute(blocks[1], "sub", pairs_b),
            lax.ppermute(blocks[2], "cluster", pairs_c),
            lax.ppermute(blocks[3], "cluster", pairs_d),
        ]

    def spread(messages, groups=None):
        return lax.all_to_all(messages, "sub", 0, 0, tiled=True, axis_index_groups=groups)

    z_count = subs // X_GROUP
    z_groups = [[X_GROUP * z + x for z in range(z_count)] for x in range(X_GROUP)]

    def together(*values):
        return lax.optimization_barrier(values)

    def clusterwise(p1, cvab):
        other = lax.ppermute(p1, "cluster", pairs_c)
        (p2,) = call(
            pair_kernel,
            [out(gdof + 8 + 2 * cdof, lanes)],
            [p1, other],
            smem=[place],
            name="pair",
        )
        moved = [lax.ppermute(p2, "cluster", k) for k in across]
        return [p2, *moved, cvab]

    block_out = [out(slot, lanes)] * 4
    full = out(order, lanes)
    small = [out(gdof + 8 + cdof, lanes), out(2 * cdof, lanes)]
    cv_scratch = [pltpu.VMEM((128, lanes), F32), pltpu.VMEM((256, 2 * lanes), BF16)]
    y2_scratch = [pltpu.VMEM((subs * BLOCK_ROWS, 2 * lanes), BF16)]
    cv2_out = out(256, 2 * lanes, dtype=BF16)
    w2_scratch = [pltpu.VMEM((order, 2 * lanes), BF16)]

    *packs, crow = pack_rows(idx, loads, basis, weights, corners, lift_map, slot)
    packs_in = exchange(packs)
    (ct2,) = call(
        own_kernel, [out(2 * BLOCK_ROWS, order, dtype=BF16)], [*packs], smem=[place], name="own"
    )
    coarse, gpad = call(
        coarse_kernel,
        [out(*factor.shape), out(128, gdof)],
        [factor, global_inv],
        name="coarse",
    )
    b2 = split_operator(operator)
    b2, ct2, coarse, gpad, *packs_in = together(b2, ct2, coarse, gpad, *packs_in)
    r0, pay = call(
        first_kernel,
        [full, out(z_count, BLOCK_ROWS, lanes)],
        [crow, *packs, *packs_in, ct2],
        smem=[place],
        scratch=w2_scratch,
        name="first",
    )

    def x_group(mine):
        return [mine] + [
            lax.ppermute(mine, "sub", [(i, i ^ k) for i in range(subs)])
            for k in range(1, X_GROUP)
        ]

    y = spread(pay, z_groups)
    y, r0 = together(y, r0)
    y = x_group(y.reshape(z_count * BLOCK_ROWS, lanes))
    fts, ft, dsum, dsw, ng = call(
        static_kernel,
        [
            out(order, 2 * lanes, dtype=BF16),
            full,
            full,
            full,
            out(128, gdof),
        ],
        [*packs, *packs_in, r0, gpad],
        smem=[place],
        scratch=[pltpu.VMEM((128, lanes), F32)],
        name="static",
    )
    t = apply_operator(idx, dsw, b2)
    t, *y = together(t, *y)
    table, p1, cvab = call(
        table_kernel,
        [out(256, subs * BLOCK_ROWS, dtype=BF16)] + small,
        [*y, packs[0], *packs_in[:2], coarse, lift_map],
        scratch=[pltpu.VMEM((256, factor.shape[0]), BF16), *y2_scratch],
        name="table",
    )
    cluster_part = clusterwise(p1, cvab)
    bf = apply_operator(idx, ft, b2)
    (bfs,) = call(split_kernel, [out(order, 2 * lanes, dtype=BF16)], [bf], name="split")
    cv2, *u0 = call(
        stage0_kernel,
        [cv2_out] + block_out,
        [*cluster_part, ng, t, bfs],
        smem=[place],
        scratch=cv_scratch[:1],
        name="stage0",
    )
    u0_in = exchange(u0)
    (v0,) = call(shadow0_kernel, [full], [cv2, fts, dsw], name="shadow0")
    v0, *u0_in = together(v0, *u0_in)
    w0, dsw, pay = call(
        functools.partial(jump_kernel, ((0, 1), (-1, 1))),
        [full, full, out(z_count, BLOCK_ROWS, lanes)],
        [*u0, *u0_in, dsum, ct2, r0, v0],
        smem=[place],
        scratch=w2_scratch,
        name="jump1",
    )

    y = spread(pay, z_groups)
    y, dsw = together(y, dsw)
    y = x_group(y.reshape(z_count * BLOCK_ROWS, lanes))
    t = apply_operator(idx, dsw, b2)
    t, *y = together(t, *y)
    p1, cvab = call(
        corner_kernel,
        small,
        [*y, table],
        scratch=y2_scratch,
        name="corner",
    )
    cluster_part = clusterwise(p1, cvab)
    cv2, bv1, scal, *u1 = call(
        stage1_kernel,
        [cv2_out, full, out(8, lanes)] + block_out,
        [*cluster_part, ng, bfs, t, *u0],
        smem=[place],
        scratch=cv_scratch[:1],
        name="stage1",
    )
    u1_in = exchange(u1)
    v1, z1, r1 = call(
        shadow1_kernel, [full] * 3, [scal, cv2, fts, dsw, v0, r0, w0], name="shadow1"
    )
    v1, z1, r1, *u1_in = together(v1, z1, r1, *u1_in)
    s1, dsw, pay = call(
        functools.partial(jump_kernel, ((0, 1), (-1, 1), (2, 1), (-1, 3))),
        [full, full, out(z_count, BLOCK_ROWS, lanes)],
        [*u1, *u1_in, dsum, ct2, r1, z1, w0, v0],
        smem=[place],
        scratch=w2_scratch,
        name="jump2",
    )

    y = spread(pay, z_groups)
    y, dsw = together(y, dsw)
    y = x_group(y.reshape(z_count * BLOCK_ROWS, lanes))
    t = apply_operator(idx, dsw, b2)
    t, *y = together(t, *y)
    p1, cvab = call(
        corner_kernel,
        small,
        [*y, table],
        scratch=y2_scratch,
        name="corner",
    )
    cluster_part = clusterwise(p1, cvab)
    z2, p1, r2, q1, scal2, dots2, *u2 = call(
        stage2_kernel,
        [full] * 4 + [out(8, lanes), out(subs, 8, lanes)] + block_out,
        [*cluster_part, ng, fts, bfs, t, dsw, v0, w0, v1, bv1, z1, r1, s1, scal, *u1],
        smem=[place],
        scratch=cv_scratch,
        name="stage2",
    )

    dots = spread(dots2)
    dots, z2, scal2, *u2 = together(dots, z2, scal2, *u2)
    u2_in = exchange(u2)
    (dots,) = call(sum_kernel, [out(8, lanes)], [dots], name="sum")
    other = lax.ppermute(dots, "cluster", pairs_c)
    (dots,) = call(add_kernel, [out(8, lanes)], [dots, other], name="add")
    moved = [lax.ppermute(dots, "cluster", k) for k in across]
    home = call(
        home_kernel,
        [full] * 3,
        [scal2, z2, p1, v0],
        smem=[idx],
        scratch=[pltpu.VMEM((order, lanes), F32)],
        name="home",
        flops=4_000_000_000,
    )
    multipliers, residual = call(
        last_kernel,
        [full, full],
        [*home, r2, q1, *u2, *u2_in, scal2, dots, *moved],
        smem=[place, idx],
        scratch=[pltpu.VMEM((order, lanes), F32)],
        name="last",
    )
    return (multipliers[None, None], residual[None, None])


def solution(mesh):
    in_specs = (
        P("cluster", "sub", None, None),
        P("cluster", "sub", None, None),
        P("cluster", "sub", None, None),
        P("cluster", "sub", None),
        P("cluster", None, None),
        P("cluster", None, None),
        P(),
        P("cluster", "sub", None, None),
        P("cluster", "sub", None),
        P("cluster", "sub", None),
    )
    out_specs = (P("cluster", "sub", None, None), P("cluster", "sub", None, None))
    return jax.shard_map(body, mesh=mesh, in_specs=in_specs, out_specs=out_specs, check_vma=False)
```

```python
import functools

import jax
import jax.numpy as jnp
from jax import lax
from jax.experimental import pallas as pl
from jax.experimental.pallas import tpu as pltpu
from jax.sharding import PartitionSpec as P

F32 = jnp.float32
BF16 = jnp.bfloat16
VMEM_LIMIT = 12 * 1024 * 1024
PACK_VMEM = 61_890_560
HALVES_VMEM = 42_000_384
CID_LANE = 25
SCALE_LANE = 24
MAP_LANE = 32
ROWS_AT_ONCE = 32
X_GROUP = 4
SUB_AT = 2
SIDE_AT = 3
COUNT_AT = 7
CHUNK = 128
BLOCK_ROWS = 32


def dot(left, right, contract=((1,), (0,))):
    return lax.dot_general(
        left, right, (contract, ((), ())), precision=lax.Precision.HIGHEST, preferred_element_type=F32
    )


def call(kernel, outs, vmem, smem=(), scratch=(), name=None, flops=0):
    specs = [pl.BlockSpec(memory_space=pltpu.SMEM)] * len(smem)
    specs += [pl.BlockSpec(memory_space=pltpu.VMEM)] * len(vmem)
    moved = sum(a.size * a.dtype.itemsize for a in vmem) + sum(o.size * o.dtype.itemsize for o in outs)
    return pl.pallas_call(
        kernel,
        out_shape=outs,
        in_specs=specs,
        out_specs=[pl.BlockSpec(memory_space=pltpu.VMEM)] * len(outs),
        scratch_shapes=list(scratch),
        compiler_params=pltpu.CompilerParams(vmem_limit_bytes=VMEM_LIMIT),
        cost_estimate=pl.CostEstimate(flops=flops, bytes_accessed=moved, transcendentals=0),
        name=name,
    )(*smem, *vmem)


def out(*shape, dtype=F32):
    return jax.ShapeDtypeStruct(shape, dtype)


def halves(value):
    high = value.astype(BF16)
    return high, (value - high.astype(F32)).astype(BF16)


def dot16(left, right):
    return jnp.dot(left, right, preferred_element_type=F32)


def live_block(count, slot, lanes):
    return lax.broadcasted_iota(jnp.int32, (slot, lanes), 0) < count


def pack_kernel(
    place, idx, rhs_in, basis_in, scaling_in, corners_in, cmap_in, pa, pb, pc, pd, crow, ct2,
    rhs, scaling, corners, wide, static, cpad, sems,
):
    cdof = basis_in.shape[0]
    slot = pa.shape[0] // 2
    lanes = pa.shape[1]
    wide[...] = jnp.zeros_like(wide)
    cpad[...] = jnp.zeros_like(cpad)
    moves = (
        (basis_in, wide.at[pl.ds(0, cdof)]),
        (scaling_in, scaling),
        (corners_in, corners),
        (cmap_in, cpad.at[pl.ds(MAP_LANE, cmap_in.shape[0])]),
        (rhs_in, rhs),
    )
    copies = [
        pltpu.make_async_copy(source, target, sems.at[at])
        for at, (source, target) in enumerate(moves)
    ]
    for copy in copies:
        copy.start()
    for copy in copies[:-1]:
        copy.wait()
    wide[SCALE_LANE : SCALE_LANE + 1, :] = scaling[...]
    static[...] = wide[...].T
    row = corners[...].astype(F32)
    lane = lax.broadcasted_iota(jnp.int32, (cdof, cdof), 1)
    ids = jnp.sum(
        jnp.where(lane == lax.broadcasted_iota(jnp.int32, (cdof, cdof), 0), row, 0.0),
        axis=1,
        keepdims=True,
    )
    onehot = jnp.where(
        ids == lax.broadcasted_iota(jnp.int32, (cdof, cpad.shape[1]), 1).astype(F32), 1.0, 0.0
    ).astype(F32)
    extra = dot(onehot, cpad[...], ((1,), (1,)))
    lane = lax.broadcasted_iota(jnp.int32, extra.shape, 1)
    extra = jnp.where(lane == CID_LANE, ids, extra)
    lane = lax.broadcasted_iota(jnp.int32, (8, lanes), 1)
    crow[...] = jnp.where((lane >= cdof) & (lane < BLOCK_ROWS), -1.0, 0.0)
    crow[0:1, 0:cdof] = row
    copies[-1].wait()
    for block, ref in enumerate((pa, pb, pc, pd)):

        def move(step, carry, block=block, ref=ref):
            base = step * ROWS_AT_ONCE
            for r in range(ROWS_AT_ONCE):
                row = idx[block * slot + base + r]
                ref[pl.ds(base + r, 1), :] = rhs[pl.ds(row, 1), :]
                ref[pl.ds(slot + base + r, 1), :] = static[pl.ds(row, 1), :]
            return carry

        lax.fori_loop(0, slot // ROWS_AT_ONCE, move, 0)
        stat = ref[slot : 2 * slot, :]
        live = live_block(place[COUNT_AT + place[SIDE_AT + block]], slot, lanes)
        own = lax.broadcasted_iota(jnp.int32, (slot, lanes), 1) < cdof
        value = jnp.where(own & live, stat, 0.0).T[0:BLOCK_ROWS, :]
        rows = slice(block * slot, (block + 1) * slot)
        ct2[0:BLOCK_ROWS, rows], ct2[BLOCK_ROWS : 2 * BLOCK_ROWS, rows] = halves(value)
        ref[slot : slot + cdof, :] = ref[slot : slot + cdof, :] + extra


def pack_rows(place, idx, rhs, basis, scaling, corners, cmap, slot):
    order, lanes = rhs.shape
    arrays = (rhs, basis, scaling, corners, cmap)
    outs = [out(2 * slot, lanes)] * 4 + [out(8, lanes)]
    outs += [out(2 * BLOCK_ROWS, order, dtype=BF16)]
    return pl.pallas_call(
        pack_kernel,
        out_shape=outs,
        in_specs=[pl.BlockSpec(memory_space=pltpu.SMEM)] * 2
        + [pl.BlockSpec(memory_space=pltpu.HBM)] * len(arrays),
        out_specs=[pl.BlockSpec(memory_space=pltpu.VMEM)] * len(outs),
        scratch_shapes=[
            pltpu.VMEM((order, lanes), F32),
            pltpu.VMEM(scaling.shape, F32),
            pltpu.VMEM(corners.shape, jnp.int32),
            pltpu.VMEM((128, order), F32),
            pltpu.VMEM((order, 128), F32),
            pltpu.VMEM((128, cmap.shape[1]), F32),
            pltpu.SemaphoreType.DMA((len(arrays),)),
        ],
        compiler_params=pltpu.CompilerParams(vmem_limit_bytes=PACK_VMEM),
        name="pack",
    )(place, idx, *arrays)


def restricted(ct2, w2):
    lanes = w2.shape[1] // 2
    both = dot16(ct2[...], w2[...])
    return both[0:BLOCK_ROWS, 0:lanes] + (
        both[0:BLOCK_ROWS, lanes : 2 * lanes] + both[BLOCK_ROWS : 2 * BLOCK_ROWS, 0:lanes]
    )


def send(pay, values, extra, start):
    pay[0] = values
    for at, row in enumerate(extra):
        pay[0, start + at : start + at + 1, :] = row
    message = pay[0]
    for other in range(1, pay.shape[0]):
        pay[other] = message


def sweep(slot):
    for block in range(4):
        for start in range(0, slot, CHUNK):
            yield block, slice(start, start + CHUNK), slice(
                block * slot + start, block * slot + start + CHUNK
            )


def live_chunk(place, block, rows, lanes):
    row = lax.broadcasted_iota(jnp.int32, (CHUNK, lanes), 0) + rows.start
    return row < place[COUNT_AT + place[SIDE_AT + block]]


def first_kernel(place, crow, pa, pb, pc, pd, qa, qb, qc, qd, ct2, r0, pay, w2):
    slot = pa.shape[0] // 2
    lanes = pa.shape[1]
    mine, theirs = (pa, pb, pc, pd), (qa, qb, qc, qd)
    for block, part, rows in sweep(slot):
        live = live_chunk(place, block, part, lanes)
        value = jnp.where(live, mine[block][part, :] - theirs[block][part, :], 0.0)
        r0[rows, :] = value
        w2[rows, 0:lanes], w2[rows, lanes : 2 * lanes] = halves(value)
    send(pay, restricted(ct2, w2), [crow[0:1, :]], SCALE_LANE)


def static_kernel(place, pa, pb, pc, pd, qa, qb, qc, qd, r0, ginv, fts, ft, dsum, dsw, ng, nq, gpad):
    slot = pa.shape[0] // 2
    cdof = SCALE_LANE
    lanes = pa.shape[1]
    lane = lax.broadcasted_iota(jnp.int32, (CHUNK, lanes), 1)
    own = lane < cdof
    mine, theirs = (pa, pb, pc, pd), (qa, qb, qc, qd)
    nq[...] = jnp.zeros_like(nq)
    nq[0:cdof, :] = pa[slot : slot + cdof, :]
    for block in range(4):
        start = cdof * (block + 1)
        nq[start : start + cdof, :] = theirs[block][slot : slot + cdof, :]
    gdof = ginv.shape[0]
    gpad[...] = jnp.zeros_like(gpad)
    gpad[MAP_LANE : MAP_LANE + gdof, :] = dot(ginv[...], ginv[...], ((0,), (0,)))
    ng[...] = dot(nq[...], gpad[...])
    for block, part, rows in sweep(slot):
        live = live_chunk(place, block, part, lanes)
        low_rows = slice(slot + part.start, slot + part.stop)
        stat = mine[block][low_rows, :]
        other = theirs[block][low_rows, :]
        basis_mine = jnp.where(own & live, stat, 0.0)
        basis_other = jnp.where(own & live, other, 0.0)
        full = basis_mine - pltpu.roll(basis_other, cdof * (block + 1), 1)
        fts[rows, 0:lanes], fts[rows, lanes : 2 * lanes] = halves(full)
        ft[rows, :] = full
        weight = jnp.sum(
            jnp.where((lane == cdof) & live, stat + other, 0.0), axis=1, keepdims=True
        )
        weight = jnp.broadcast_to(weight, (CHUNK, lanes))
        dsum[rows, :] = weight
        dsw[rows, :] = weight * r0[rows, :]


def split_kernel(x, split):
    lanes = x.shape[1]
    for start in range(0, x.shape[0], CHUNK):
        rows = slice(start, start + CHUNK)
        split[rows, 0:lanes], split[rows, lanes : 2 * lanes] = halves(x[rows, :])


def go_home(idx, pairs):
    def move(at, carry):
        base = at * ROWS_AT_ONCE
        for r in range(ROWS_AT_ONCE):
            row = idx[base + r]
            for source, target in pairs:
                target[pl.ds(row, 1), :] = source[pl.ds(base + r, 1), :]
        return carry

    lax.fori_loop(0, idx.shape[0] // ROWS_AT_ONCE, move, 0)


def halves_kernel(b, b2, parts, sems):
    count, tile, rows = parts.shape
    copies = [
        pltpu.make_async_copy(b.at[pl.ds(at * tile, tile)], parts.at[at], sems.at[at])
        for at in range(count)
    ]
    for copy in copies:
        copy.start()
    for at, copy in enumerate(copies):
        copy.wait()
        for start in range(0, tile, 64):
            value = parts[at, start : start + 64, :]
            part = slice(at * tile + start, at * tile + start + 64)
            b2[part, 0:rows], b2[part, rows : 2 * rows] = halves(value)


def split_operator(operator):
    rows = operator.shape[0]
    count = 6
    return pl.pallas_call(
        halves_kernel,
        out_shape=out(rows, 2 * rows, dtype=BF16),
        in_specs=[pl.BlockSpec(memory_space=pltpu.HBM)],
        out_specs=pl.BlockSpec(memory_space=pltpu.VMEM),
        scratch_shapes=[
            pltpu.VMEM((count, rows // count, rows), F32),
            pltpu.SemaphoreType.DMA((count,)),
        ],
        compiler_params=pltpu.CompilerParams(vmem_limit_bytes=HALVES_VMEM),
        cost_estimate=pl.CostEstimate(
            flops=0, bytes_accessed=8 * rows * rows, transcendentals=0
        ),
        name="halves",
    )(operator)


def operator_kernel(idx, x, b2, o, natural, split):
    rows, n = x.shape
    tile = rows // 2
    go_home(idx, ((x, natural),))
    for start in range(0, rows, CHUNK):
        part = slice(start, start + CHUNK)
        low_part = slice(rows + start, rows + start + CHUNK)
        high, low = halves(natural[part, :])
        split[part, 0:n] = high
        split[part, n : 2 * n] = low
        split[low_part, 0:n] = high
        split[low_part, n : 2 * n] = jnp.zeros((CHUNK, n), BF16)

    def multiply(at, carry):
        part = pl.ds(at * tile, tile)
        both = dot16(b2[part, :], split[...])
        natural[part, :] = both[:, 0:n] + both[:, n : 2 * n]
        return carry

    lax.fori_loop(0, rows // tile, multiply, 0)

    def move(at, carry):
        base = at * ROWS_AT_ONCE
        for r in range(ROWS_AT_ONCE):
            o[pl.ds(base + r, 1), :] = natural[pl.ds(idx[base + r], 1), :]
        return carry

    lax.fori_loop(0, rows // ROWS_AT_ONCE, move, 0)


def apply_operator(idx, x, b2):
    rows, n = x.shape
    (result,) = call(
        operator_kernel,
        [out(rows, n)],
        [x, b2],
        smem=[idx],
        scratch=[pltpu.VMEM((rows, n), F32), pltpu.VMEM((2 * rows, 2 * n), BF16)],
        name="operator",
        flops=6 * rows * rows * n,
    )
    return result


def gathered_product(y2, table, p1, cvab):
    lanes = p1.shape[1]
    both = dot16(table[...], y2[...])
    half = both.shape[0] // 2
    total = both[0:half, 0:lanes] + (both[0:half, lanes:] + both[half:, 0:lanes])
    top = p1.shape[0]
    p1[...] = total[0:top, :]
    cvab[...] = total[top:, :]


def table_kernel(ya, yb, yc, yd, pa, qa, qb, factor, cmap, table, p1, cvab, reach2, y2):
    rows, lanes = BLOCK_ROWS, ya.shape[1]
    cdof = SCALE_LANE
    slot = pa.shape[0] // 2
    gdof, ccl = cmap.shape
    number = lax.broadcasted_iota(jnp.int32, (cdof, ccl), 1).astype(F32)
    chosen = [
        jnp.where(ref[slot : slot + cdof, CID_LANE : CID_LANE + 1] == number, 1.0, 0.0)
        for ref in (pa, qa, qb)
    ]
    inner = dot(jnp.concatenate(chosen, axis=0), factor[...], ((1,), (1,)))
    reach = jnp.concatenate(
        [cmap[...], jnp.zeros((8, ccl), F32), dot(inner, factor[...])], axis=0
    )
    reach2[0:128, :], reach2[128:256, :] = halves(reach)
    per = lanes // rows
    which = lax.broadcasted_iota(jnp.int32, (ccl, lanes), 0).astype(F32)
    row = lax.broadcasted_iota(jnp.int32, (256, lanes), 0)
    column = lax.broadcasted_iota(jnp.int32, (256, lanes), 1) % rows
    kept = (row - gdof == column - cdof) & (row > gdof) & (row < gdof + 8)
    unit = jnp.where(kept, 1.0, 0.0)
    for part, y in enumerate((ya, yb, yc, yd)):
        first = part * y.shape[0]
        y2[first : first + y.shape[0], 0:lanes], y2[first : first + y.shape[0], lanes:] = halves(
            y[...]
        )
        for group in range(0, y.shape[0], per * rows):
            ids = y[group + cdof : group + cdof + 8, :]
            for r in range(1, per):
                start = group + r * rows + cdof
                ids = ids + pltpu.roll(y[start : start + 8, :], r * rows, 1)
            onehot = jnp.where(which == ids[0:1, :], 1.0, 0.0).astype(BF16)
            at = slice(first + group, first + group + lanes)
            table[:, at] = (dot16(reach2[...], onehot) + unit).astype(BF16)
    gathered_product(y2, table, p1, cvab)


def corner_kernel(ya, yb, yc, yd, table, p1, cvab, y2):
    lanes = ya.shape[1]
    for part, y in enumerate((ya, yb, yc, yd)):
        rows = slice(part * y.shape[0], (part + 1) * y.shape[0])
        y2[rows, 0:lanes], y2[rows, lanes:] = halves(y[...])
    gathered_product(y2, table, p1, cvab)


def pair_kernel(place, own, other, p2):
    cdof = SCALE_LANE
    top = own.shape[0] - cdof
    odd = place[0] == 1
    p2[0:top, :] = own[0:top, :] + other[0:top, :]
    mine = own[top : top + cdof, :]
    theirs = other[top : top + cdof, :]
    p2[top : top + cdof, :] = jnp.where(odd, theirs, mine)
    p2[top + cdof : top + 2 * cdof, :] = jnp.where(odd, mine, theirs)


def corner_values(place, p2, c2, c4, c6, cvab, ng, cv, cv2):
    cdof = SCALE_LANE
    top = p2.shape[0] - 2 * cdof
    gdof = top - 8
    lanes = cv.shape[1]
    even = slice(top, top + cdof)
    odd = slice(top + cdof, top + 2 * cdof)
    is_odd = place[0] == 1
    total = (p2[0:top, :] + c2[0:top, :]) + (c4[0:top, :] + c6[0:top, :])
    cv[0:cdof, :] = jnp.where(is_odd, p2[odd, :], p2[even, :])
    cv[cdof : 3 * cdof, :] = cvab[...]
    cv[3 * cdof : 4 * cdof, :] = jnp.where(is_odd, p2[even, :], p2[odd, :])
    far = place[1] == 1
    cv[4 * cdof : 5 * cdof, :] = jnp.where(
        is_odd,
        jnp.where(far, c6[even, :], c2[even, :]),
        jnp.where(far, c6[odd, :], c2[odd, :]),
    )
    cv[5 * cdof : 128, :] = jnp.zeros((128 - 5 * cdof, lanes), F32)
    high, low = halves(cv[...] + dot(ng[...], total[0:gdof, :]))
    cv2[0:128, 0:lanes] = high
    cv2[128:256, 0:lanes] = high
    cv2[0:128, lanes : 2 * lanes] = low
    cv2[128:256, lanes : 2 * lanes] = jnp.zeros((128, lanes), BF16)
    return total[gdof : gdof + 8, :]


def times_corner(matrix, rows, cv2):
    both = dot16(matrix[rows, :], cv2[...])
    lanes = both.shape[1] // 2
    return both[:, 0:lanes] + both[:, lanes:]


def column_sum(value):
    return jnp.sum(value, axis=0, keepdims=True)


def stage0_kernel(
    place, p2, c2, c4, c6, cvab, ng, t, bfs, cv2, ua, ub, uc, ud, cv
):
    corner_values(place, p2, c2, c4, c6, cvab, ng, cv, cv2)
    blocks = (ua, ub, uc, ud)
    for block, part, rows in sweep(ua.shape[0]):
        blocks[block][part, :] = t[rows, :] + times_corner(bfs, rows, cv2)


def shadow0_kernel(cv2, fts, dsw, v0):
    for start in range(0, v0.shape[0], CHUNK):
        rows = slice(start, start + CHUNK)
        v0[rows, :] = dsw[rows, :] + times_corner(fts, rows, cv2)


def shadow1_kernel(scal, cv2, fts, dsw, v0, r0, w0, v1, z1, r1):
    alpha = scal[0:1, :]
    for start in range(0, v0.shape[0], CHUNK):
        rows = slice(start, start + CHUNK)
        new = dsw[rows, :] + times_corner(fts, rows, cv2)
        v1[rows, :] = new
        z1[rows, :] = v0[rows, :] - alpha * new
        r1[rows, :] = r0[rows, :] - alpha * w0[rows, :]


def stage1_kernel(
    place, p2, c2, c4, c6, cvab, ng, bfs, t,
    u0a, u0b, u0c, u0d, cv2, bv1, scal, ua, ub, uc, ud, cv,
):
    dots = corner_values(place, p2, c2, c4, c6, cvab, ng, cv, cv2)
    alpha = dots[1:2, :] / dots[2:3, :]
    scal[...] = dots
    scal[0:1, :] = alpha
    olds, news = (u0a, u0b, u0c, u0d), (ua, ub, uc, ud)
    for block, part, rows in sweep(ua.shape[0]):
        image = t[rows, :] + times_corner(bfs, rows, cv2)
        bv1[rows, :] = image
        news[block][part, :] = olds[block][part, :] - alpha * image


def stage2_kernel(
    place, p2, c2, c4, c6, cvab, ng, fts, bfs, t, dsw, v0, w0, v1, bv1, z1, r1, s1, scal,
    u1a, u1b, u1c, u1d, z2, p1, r2, q1, scal2, dots2, ua, ub, uc, ud, cv, cv2,
):
    dots = corner_values(place, p2, c2, c4, c6, cvab, ng, cv, cv2)
    lanes = cv.shape[1]
    rz0 = scal[1:2, :]
    pq0 = scal[2:3, :]
    rz1 = dots[1:2, :]
    beta = rz1 / rz0
    pq1 = dots[2:3, :] + beta * (dots[3:4, :] + dots[4:5, :]) + beta * beta * pq0
    alpha = rz1 / pq1
    scal2[...] = jnp.zeros_like(scal2)
    scal2[0:1, :] = scal[0:1, :]
    scal2[1:2, :] = rz1
    scal2[2:3, :] = pq1
    scal2[3:4, :] = alpha
    olds, news = (u1a, u1b, u1c, u1d), (ua, ub, uc, ud)
    sums = [jnp.zeros((8, lanes), F32) for _ in range(4)]

    def folded(value):
        return jnp.sum(value.reshape(CHUNK // 8, 8, lanes), axis=0)

    for block, part, rows in sweep(ua.shape[0]):
        search = z1[rows, :] + beta * v0[rows, :]
        p1[rows, :] = search
        image_q = s1[rows, :] + beta * w0[rows, :]
        q1[rows, :] = image_q
        res = r1[rows, :] - alpha * image_q
        r2[rows, :] = res
        new = z1[rows, :] - alpha * (
            dsw[rows, :] + times_corner(fts, rows, cv2) + beta * v1[rows, :]
        )
        z2[rows, :] = new
        image = t[rows, :] + times_corner(bfs, rows, cv2) + beta * bv1[rows, :]
        fresh = olds[block][part, :] - alpha * image
        news[block][part, :] = fresh
        sums[0] = sums[0] + folded(res * new)
        sums[1] = sums[1] + folded(fresh * new)
        sums[2] = sums[2] + folded(image_q * new)
        sums[3] = sums[3] + folded(fresh * search)
    dots2[0] = jnp.zeros((8, lanes), F32)
    dots2[0, 1:2, :] = column_sum(sums[0])
    dots2[0, 2:3, :] = 2.0 * column_sum(sums[1])
    dots2[0, 3:4, :] = column_sum(sums[2])
    dots2[0, 4:5, :] = 2.0 * column_sum(sums[3])
    message = dots2[0]
    for other in range(1, dots2.shape[0]):
        dots2[other] = message


def jump_kernel(pairs, place, ua, ub, uc, ud, qa, qb, qc, qd, dsum, ct2, *rest):
    fields, (w, dsw, pay, w2) = rest[:-4], rest[-4:]
    lanes = w.shape[1]
    mine, theirs = (ua, ub, uc, ud), (qa, qb, qc, qd)
    sums = [jnp.zeros((8, lanes), F32) for _ in pairs]
    for block, part, rows in sweep(ua.shape[0]):
        live = live_chunk(place, block, part, lanes)
        value = jnp.where(live, mine[block][part, :] - theirs[block][part, :], 0.0)
        w[rows, :] = value
        dsw[rows, :] = dsum[rows, :] * value
        w2[rows, 0:lanes], w2[rows, lanes : 2 * lanes] = halves(value)
        for at, (left, right) in enumerate(pairs):
            first = value if left < 0 else fields[left][rows, :]
            product = first * fields[right][rows, :]
            sums[at] = sums[at] + jnp.sum(product.reshape(CHUNK // 8, 8, lanes), axis=0)
    send(pay, restricted(ct2, w2), [column_sum(v) for v in sums], SCALE_LANE + 1)


def sum_kernel(x, o):
    o[...] = jnp.sum(x[...], axis=0)


def add_kernel(first, *rest):
    *others, o = rest
    total = first[...]
    for other in others:
        total = total + other[...]
    o[...] = total


def home_kernel(idx, scal2, z2, p1, v0, z2n, p1n, xsn, xs):
    xs[...] = scal2[0:1, :] * v0[...] + scal2[3:4, :] * p1[...]
    go_home(idx, ((z2, z2n), (p1, p1n), (xs, xsn)))


def last_kernel(
    place, idx, z2, p1, xs, r2, q1, ua, ub, uc, ud, qa, qb, qc, qd, scal2, d0, d2, d4, d6,
    mult, resid, work,
):
    dots = (d0[...] + d2[...]) + (d4[...] + d6[...])
    lanes = work.shape[1]
    beta = dots[1:2, :] / scal2[1:2, :]
    pq = dots[2:3, :] + beta * (dots[3:4, :] + dots[4:5, :]) + beta * beta * scal2[2:3, :]
    alpha = dots[1:2, :] / pq
    mine, theirs = (ua, ub, uc, ud), (qa, qb, qc, qd)
    for block, part, rows in sweep(ua.shape[0]):
        live = live_chunk(place, block, part, lanes)
        image = jnp.where(live, mine[block][part, :] - theirs[block][part, :], 0.0)
        work[rows, :] = r2[rows, :] - alpha * (image + beta * q1[rows, :])
        mult[rows, :] = xs[rows, :] + alpha * (z2[rows, :] + beta * p1[rows, :])
    go_home(idx, ((work, resid),))


def body(
    dual_ops,
    rhs,
    corner_basis,
    scaling,
    cluster_corner_inverse,
    coarse_map,
    global_inv,
    row_index,
    pair_counts,
    corner_map,
):
    operator = dual_ops[0, 0]
    loads = rhs[0, 0]
    basis = corner_basis[0, 0]
    weights = scaling[0]
    factor = cluster_corner_inverse[0]
    lift_map = coarse_map[0]
    row_ids = row_index[0, 0]
    corners = corner_map[0]
    slot = row_ids.shape[1]
    order, lanes = loads.shape
    cdof = basis.shape[0]
    subs = lax.axis_size("sub")
    clusters = lax.axis_size("cluster")
    gdof = lift_map.shape[0]

    s = lax.axis_index("sub")
    c = lax.axis_index("cluster")
    s_odd = s % 2
    c_odd = c % 2
    pairs_a = [(i, i ^ 1) for i in range(subs)]
    pairs_b = [(i, (i + 1) % subs) for i in range(1, subs, 2)]
    pairs_b += [(j, i) for i, j in pairs_b]
    pairs_c = [(i, i ^ 1) for i in range(clusters)]
    pairs_d = [(i, (i + 1) % clusters) for i in range(1, clusters, 2)]
    pairs_d += [(j, i) for i, j in pairs_d]
    across = [[(i, i ^ k) for i in range(clusters)] for k in (2, 4, 6)]

    chip = c // 2
    next_chip = jnp.where(c_odd == 1, chip + 1, chip - 1)
    far = ((chip ^ next_chip) == 3).astype(jnp.int32)
    def chosen(array):
        return [
            jnp.where(s_odd == 0, array[1], array[0]),
            jnp.where(s_odd == 0, array[0], array[1]),
            jnp.where(c_odd == 0, array[3], array[2]),
            jnp.where(c_odd == 0, array[2], array[3]),
        ]

    sides = (1 - s_odd, s_odd, 3 - c_odd, 2 + c_odd)
    place = jnp.stack([v.astype(jnp.int32) for v in (c_odd, far, s, *sides)])
    place = jnp.concatenate([place, pair_counts[0, 0]])
    idx = jnp.concatenate(chosen(row_ids))
    idx, place = lax.optimization_barrier((idx, place))

    def exchange(blocks):
        return [
            lax.ppermute(blocks[0], "sub", pairs_a),
            lax.ppermute(blocks[1], "sub", pairs_b),
            lax.ppermute(blocks[2], "cluster", pairs_c),
            lax.ppermute(blocks[3], "cluster", pairs_d),
        ]

    def spread(messages, groups=None):
        return lax.all_to_all(messages, "sub", 0, 0, tiled=True, axis_index_groups=groups)

    z_count = subs // X_GROUP
    z_groups = [[X_GROUP * z + x for z in range(z_count)] for x in range(X_GROUP)]

    def together(*values):
        return lax.optimization_barrier(values)

    def clusterwise(p1, cvab):
        other = lax.ppermute(p1, "cluster", pairs_c)
        (p2,) = call(
            pair_kernel,
            [out(gdof + 8 + 2 * cdof, lanes)],
            [p1, other],
            smem=[place],
            name="pair",
        )
        moved = [lax.ppermute(p2, "cluster", k) for k in across]
        return [p2, *moved, cvab]

    block_out = [out(slot, lanes)] * 4
    full = out(order, lanes)
    small = [out(gdof + 8 + cdof, lanes), out(2 * cdof, lanes)]
    cv_scratch = [pltpu.VMEM((128, lanes), F32), pltpu.VMEM((256, 2 * lanes), BF16)]
    y2_scratch = [pltpu.VMEM((subs * BLOCK_ROWS, 2 * lanes), BF16)]
    cv2_out = out(256, 2 * lanes, dtype=BF16)
    w2_scratch = [pltpu.VMEM((order, 2 * lanes), BF16)]

    *packs, crow, ct2 = pack_rows(place, idx, loads, basis, weights, corners, lift_map, slot)
    packs_in = exchange(packs)
    b2 = split_operator(operator)
    b2, *packs_in = together(b2, *packs_in)
    r0, pay = call(
        first_kernel,
        [full, out(z_count, BLOCK_ROWS, lanes)],
        [crow, *packs, *packs_in, ct2],
        smem=[place],
        scratch=w2_scratch,
        name="first",
    )

    def x_group(mine):
        return [mine] + [
            lax.ppermute(mine, "sub", [(i, i ^ k) for i in range(subs)])
            for k in range(1, X_GROUP)
        ]

    y = spread(pay, z_groups)
    y, r0 = together(y, r0)
    y = x_group(y.reshape(z_count * BLOCK_ROWS, lanes))
    fts, ft, dsum, dsw, ng = call(
        static_kernel,
        [
            out(order, 2 * lanes, dtype=BF16),
            full,
            full,
            full,
            out(128, gdof),
        ],
        [*packs, *packs_in, r0, global_inv],
        smem=[place],
        scratch=[pltpu.VMEM((128, lanes), F32), pltpu.VMEM((128, gdof), F32)],
        name="static",
    )
    t = apply_operator(idx, dsw, b2)
    t, *y = together(t, *y)
    table, p1, cvab = call(
        table_kernel,
        [out(256, subs * BLOCK_ROWS, dtype=BF16)] + small,
        [*y, packs[0], *packs_in[:2], factor, lift_map],
        scratch=[pltpu.VMEM((256, factor.shape[0]), BF16), *y2_scratch],
        name="table",
    )
    cluster_part = clusterwise(p1, cvab)
    bf = apply_operator(idx, ft, b2)
    (bfs,) = call(split_kernel, [out(order, 2 * lanes, dtype=BF16)], [bf], name="split")
    cv2, *u0 = call(
        stage0_kernel,
        [cv2_out] + block_out,
        [*cluster_part, ng, t, bfs],
        smem=[place],
        scratch=cv_scratch[:1],
        name="stage0",
    )
    u0_in = exchange(u0)
    (v0,) = call(shadow0_kernel, [full], [cv2, fts, dsw], name="shadow0")
    v0, *u0_in = together(v0, *u0_in)
    w0, dsw, pay = call(
        functools.partial(jump_kernel, ((0, 1), (-1, 1))),
        [full, full, out(z_count, BLOCK_ROWS, lanes)],
        [*u0, *u0_in, dsum, ct2, r0, v0],
        smem=[place],
        scratch=w2_scratch,
        name="jump1",
    )

    y = spread(pay, z_groups)
    y, dsw = together(y, dsw)
    y = x_group(y.reshape(z_count * BLOCK_ROWS, lanes))
    t = apply_operator(idx, dsw, b2)
    t, *y = together(t, *y)
    p1, cvab = call(
        corner_kernel,
        small,
        [*y, table],
        scratch=y2_scratch,
        name="corner",
    )
    cluster_part = clusterwise(p1, cvab)
    cv2, bv1, scal, *u1 = call(
        stage1_kernel,
        [cv2_out, full, out(8, lanes)] + block_out,
        [*cluster_part, ng, bfs, t, *u0],
        smem=[place],
        scratch=cv_scratch[:1],
        name="stage1",
    )
    u1_in = exchange(u1)
    v1, z1, r1 = call(
        shadow1_kernel, [full] * 3, [scal, cv2, fts, dsw, v0, r0, w0], name="shadow1"
    )
    v1, z1, r1, *u1_in = together(v1, z1, r1, *u1_in)
    s1, dsw, pay = call(
        functools.partial(jump_kernel, ((0, 1), (-1, 1), (2, 1), (-1, 3))),
        [full, full, out(z_count, BLOCK_ROWS, lanes)],
        [*u1, *u1_in, dsum, ct2, r1, z1, w0, v0],
        smem=[place],
        scratch=w2_scratch,
        name="jump2",
    )

    y = spread(pay, z_groups)
    y, dsw = together(y, dsw)
    y = x_group(y.reshape(z_count * BLOCK_ROWS, lanes))
    t = apply_operator(idx, dsw, b2)
    t, *y = together(t, *y)
    p1, cvab = call(
        corner_kernel,
        small,
        [*y, table],
        scratch=y2_scratch,
        name="corner",
    )
    cluster_part = clusterwise(p1, cvab)
    z2, p1, r2, q1, scal2, dots2, *u2 = call(
        stage2_kernel,
        [full] * 4 + [out(8, lanes), out(subs, 8, lanes)] + block_out,
        [*cluster_part, ng, fts, bfs, t, dsw, v0, w0, v1, bv1, z1, r1, s1, scal, *u1],
        smem=[place],
        scratch=cv_scratch,
        name="stage2",
    )

    dots = spread(dots2)
    dots, z2, scal2, *u2 = together(dots, z2, scal2, *u2)
    u2_in = exchange(u2)
    (dots,) = call(sum_kernel, [out(8, lanes)], [dots], name="sum")
    other = lax.ppermute(dots, "cluster", pairs_c)
    (dots,) = call(add_kernel, [out(8, lanes)], [dots, other], name="add")
    moved = [lax.ppermute(dots, "cluster", k) for k in across]
    home = call(
        home_kernel,
        [full] * 3,
        [scal2, z2, p1, v0],
        smem=[idx],
        scratch=[pltpu.VMEM((order, lanes), F32)],
        name="home",
        flops=4_000_000_000,
    )
    multipliers, residual = call(
        last_kernel,
        [full, full],
        [*home, r2, q1, *u2, *u2_in, scal2, dots, *moved],
        smem=[place, idx],
        scratch=[pltpu.VMEM((order, lanes), F32)],
        name="last",
    )
    return (multipliers[None, None], residual[None, None])


def solution(mesh):
    in_specs = (
        P("cluster", "sub", None, None),
        P("cluster", "sub", None, None),
        P("cluster", "sub", None, None),
        P("cluster", "sub", None),
        P("cluster", None, None),
        P("cluster", None, None),
        P(),
        P("cluster", "sub", None, None),
        P("cluster", "sub", None),
        P("cluster", "sub", None),
    )
    out_specs = (P("cluster", "sub", None, None), P("cluster", "sub", None, None))
    return jax.shard_map(body, mesh=mesh, in_specs=in_specs, out_specs=out_specs, check_vma=False)
```

```python
import functools

import jax
import jax.numpy as jnp
from jax import lax
from jax.experimental import pallas as pl
from jax.experimental.pallas import tpu as pltpu
from jax.sharding import PartitionSpec as P

F32 = jnp.float32
BF16 = jnp.bfloat16
VMEM_LIMIT = 12 * 1024 * 1024
PACK_VMEM = 61_890_560
HALVES_VMEM = 42_000_384
CID_LANE = 25
SCALE_LANE = 24
MAP_LANE = 32
ROWS_AT_ONCE = 64
X_GROUP = 4
SUB_AT = 2
SIDE_AT = 3
COUNT_AT = 7
CHUNK = 128
BLOCK_ROWS = 32


def dot(left, right, contract=((1,), (0,))):
    return lax.dot_general(
        left, right, (contract, ((), ())), precision=lax.Precision.HIGHEST, preferred_element_type=F32
    )


def call(kernel, outs, vmem, smem=(), scratch=(), name=None, flops=0):
    specs = [pl.BlockSpec(memory_space=pltpu.SMEM)] * len(smem)
    specs += [pl.BlockSpec(memory_space=pltpu.VMEM)] * len(vmem)
    moved = sum(a.size * a.dtype.itemsize for a in vmem) + sum(o.size * o.dtype.itemsize for o in outs)
    return pl.pallas_call(
        kernel,
        out_shape=outs,
        in_specs=specs,
        out_specs=[pl.BlockSpec(memory_space=pltpu.VMEM)] * len(outs),
        scratch_shapes=list(scratch),
        compiler_params=pltpu.CompilerParams(vmem_limit_bytes=VMEM_LIMIT),
        cost_estimate=pl.CostEstimate(flops=flops, bytes_accessed=moved, transcendentals=0),
        name=name,
    )(*smem, *vmem)


def out(*shape, dtype=F32):
    return jax.ShapeDtypeStruct(shape, dtype)


def halves(value):
    high = value.astype(BF16)
    return high, (value - high.astype(F32)).astype(BF16)


def dot16(left, right):
    return jnp.dot(left, right, preferred_element_type=F32)


def live_block(count, slot, lanes):
    return lax.broadcasted_iota(jnp.int32, (slot, lanes), 0) < count


def pack_kernel(
    place, idx, rhs_in, basis_in, scaling_in, corners_in, cmap_in, pa, pb, pc, pd, crow, ct2,
    rhs, scaling, corners, wide, static, cpad, sems,
):
    cdof = basis_in.shape[0]
    slot = pa.shape[0] // 2
    lanes = pa.shape[1]
    wide[...] = jnp.zeros_like(wide)
    cpad[...] = jnp.zeros_like(cpad)
    moves = (
        (basis_in, wide.at[pl.ds(0, cdof)]),
        (scaling_in, scaling),
        (corners_in, corners),
        (cmap_in, cpad.at[pl.ds(MAP_LANE, cmap_in.shape[0])]),
        (rhs_in, rhs),
    )
    copies = [
        pltpu.make_async_copy(source, target, sems.at[at])
        for at, (source, target) in enumerate(moves)
    ]
    for copy in copies:
        copy.start()
    for copy in copies[:-1]:
        copy.wait()
    wide[SCALE_LANE : SCALE_LANE + 1, :] = scaling[...]
    static[...] = wide[...].T
    row = corners[...].astype(F32)
    lane = lax.broadcasted_iota(jnp.int32, (cdof, cdof), 1)
    ids = jnp.sum(
        jnp.where(lane == lax.broadcasted_iota(jnp.int32, (cdof, cdof), 0), row, 0.0),
        axis=1,
        keepdims=True,
    )
    onehot = jnp.where(
        ids == lax.broadcasted_iota(jnp.int32, (cdof, cpad.shape[1]), 1).astype(F32), 1.0, 0.0
    ).astype(F32)
    extra = dot(onehot, cpad[...], ((1,), (1,)))
    lane = lax.broadcasted_iota(jnp.int32, extra.shape, 1)
    extra = jnp.where(lane == CID_LANE, ids, extra)
    lane = lax.broadcasted_iota(jnp.int32, (8, lanes), 1)
    crow[...] = jnp.where((lane >= cdof) & (lane < BLOCK_ROWS), -1.0, 0.0)
    crow[0:1, 0:cdof] = row
    copies[-1].wait()
    for block, ref in enumerate((pa, pb, pc, pd)):

        def move(step, carry, block=block, ref=ref):
            base = step * ROWS_AT_ONCE
            for r in range(ROWS_AT_ONCE):
                row = idx[block * slot + base + r]
                ref[pl.ds(base + r, 1), :] = rhs[pl.ds(row, 1), :]
                ref[pl.ds(slot + base + r, 1), :] = static[pl.ds(row, 1), :]
            return carry

        lax.fori_loop(0, slot // ROWS_AT_ONCE, move, 0)
        stat = ref[slot : 2 * slot, :]
        live = live_block(place[COUNT_AT + place[SIDE_AT + block]], slot, lanes)
        own = lax.broadcasted_iota(jnp.int32, (slot, lanes), 1) < cdof
        value = jnp.where(own & live, stat, 0.0).T[0:BLOCK_ROWS, :]
        rows = slice(block * slot, (block + 1) * slot)
        ct2[0:BLOCK_ROWS, rows], ct2[BLOCK_ROWS : 2 * BLOCK_ROWS, rows] = halves(value)
        ref[slot : slot + cdof, :] = ref[slot : slot + cdof, :] + extra


def pack_rows(place, idx, rhs, basis, scaling, corners, cmap, slot):
    order, lanes = rhs.shape
    arrays = (rhs, basis, scaling, corners, cmap)
    outs = [out(2 * slot, lanes)] * 4 + [out(8, lanes)]
    outs += [out(2 * BLOCK_ROWS, order, dtype=BF16)]
    return pl.pallas_call(
        pack_kernel,
        out_shape=outs,
        in_specs=[pl.BlockSpec(memory_space=pltpu.SMEM)] * 2
        + [pl.BlockSpec(memory_space=pltpu.HBM)] * len(arrays),
        out_specs=[pl.BlockSpec(memory_space=pltpu.VMEM)] * len(outs),
        scratch_shapes=[
            pltpu.VMEM((order, lanes), F32),
            pltpu.VMEM(scaling.shape, F32),
            pltpu.VMEM(corners.shape, jnp.int32),
            pltpu.VMEM((128, order), F32),
            pltpu.VMEM((order, 128), F32),
            pltpu.VMEM((128, cmap.shape[1]), F32),
            pltpu.SemaphoreType.DMA((len(arrays),)),
        ],
        compiler_params=pltpu.CompilerParams(vmem_limit_bytes=PACK_VMEM),
        name="pack",
    )(place, idx, *arrays)


def restricted(ct2, w2):
    lanes = w2.shape[1] // 2
    both = dot16(ct2[...], w2[...])
    return both[0:BLOCK_ROWS, 0:lanes] + (
        both[0:BLOCK_ROWS, lanes : 2 * lanes] + both[BLOCK_ROWS : 2 * BLOCK_ROWS, 0:lanes]
    )


def send(pay, values, extra, start):
    pay[0] = values
    for at, row in enumerate(extra):
        pay[0, start + at : start + at + 1, :] = row
    message = pay[0]
    for other in range(1, pay.shape[0]):
        pay[other] = message


def sweep(slot):
    for block in range(4):
        for start in range(0, slot, CHUNK):
            yield block, slice(start, start + CHUNK), slice(
                block * slot + start, block * slot + start + CHUNK
            )


def live_chunk(place, block, rows, lanes):
    row = lax.broadcasted_iota(jnp.int32, (CHUNK, lanes), 0) + rows.start
    return row < place[COUNT_AT + place[SIDE_AT + block]]


def first_kernel(place, crow, pa, pb, pc, pd, qa, qb, qc, qd, ct2, r0, pay, w2):
    slot = pa.shape[0] // 2
    lanes = pa.shape[1]
    mine, theirs = (pa, pb, pc, pd), (qa, qb, qc, qd)
    for block, part, rows in sweep(slot):
        live = live_chunk(place, block, part, lanes)
        value = jnp.where(live, mine[block][part, :] - theirs[block][part, :], 0.0)
        r0[rows, :] = value
        w2[rows, 0:lanes], w2[rows, lanes : 2 * lanes] = halves(value)
    send(pay, restricted(ct2, w2), [crow[0:1, :]], SCALE_LANE)


def static_kernel(place, pa, pb, pc, pd, qa, qb, qc, qd, r0, ginv, fts, ft, dsum, dsw, ng, nq, gpad):
    slot = pa.shape[0] // 2
    cdof = SCALE_LANE
    lanes = pa.shape[1]
    lane = lax.broadcasted_iota(jnp.int32, (CHUNK, lanes), 1)
    own = lane < cdof
    mine, theirs = (pa, pb, pc, pd), (qa, qb, qc, qd)
    nq[...] = jnp.zeros_like(nq)
    nq[0:cdof, :] = pa[slot : slot + cdof, :]
    for block in range(4):
        start = cdof * (block + 1)
        nq[start : start + cdof, :] = theirs[block][slot : slot + cdof, :]
    gdof = ginv.shape[0]
    gpad[...] = jnp.zeros_like(gpad)
    gpad[MAP_LANE : MAP_LANE + gdof, :] = dot(ginv[...], ginv[...], ((0,), (0,)))
    ng[...] = dot(nq[...], gpad[...])
    for block, part, rows in sweep(slot):
        live = live_chunk(place, block, part, lanes)
        low_rows = slice(slot + part.start, slot + part.stop)
        stat = mine[block][low_rows, :]
        other = theirs[block][low_rows, :]
        basis_mine = jnp.where(own & live, stat, 0.0)
        basis_other = jnp.where(own & live, other, 0.0)
        full = basis_mine - pltpu.roll(basis_other, cdof * (block + 1), 1)
        fts[rows, 0:lanes], fts[rows, lanes : 2 * lanes] = halves(full)
        ft[rows, :] = full
        weight = jnp.sum(
            jnp.where((lane == cdof) & live, stat + other, 0.0), axis=1, keepdims=True
        )
        weight = jnp.broadcast_to(weight, (CHUNK, lanes))
        dsum[rows, :] = weight
        dsw[rows, :] = weight * r0[rows, :]


def coarse_kernel(factor, coarse):
    coarse[...] = dot(factor[...], factor[...], ((0,), (0,)))


def split_kernel(x, split):
    lanes = x.shape[1]
    for start in range(0, x.shape[0], CHUNK):
        rows = slice(start, start + CHUNK)
        split[rows, 0:lanes], split[rows, lanes : 2 * lanes] = halves(x[rows, :])


def go_home(idx, pairs):
    def move(at, carry):
        base = at * ROWS_AT_ONCE
        for r in range(ROWS_AT_ONCE):
            row = idx[base + r]
            for source, target in pairs:
                target[pl.ds(row, 1), :] = source[pl.ds(base + r, 1), :]
        return carry

    lax.fori_loop(0, idx.shape[0] // ROWS_AT_ONCE, move, 0)


def halves_kernel(b, b2, parts, sems):
    count, tile, rows = parts.shape
    copies = [
        pltpu.make_async_copy(b.at[pl.ds(at * tile, tile)], parts.at[at], sems.at[at])
        for at in range(count)
    ]
    for copy in copies:
        copy.start()
    for at, copy in enumerate(copies):
        copy.wait()
        for start in range(0, tile, 64):
            value = parts[at, start : start + 64, :]
            part = slice(at * tile + start, at * tile + start + 64)
            b2[part, 0:rows], b2[part, rows : 2 * rows] = halves(value)


def split_operator(operator):
    rows = operator.shape[0]
    count = 6
    return pl.pallas_call(
        halves_kernel,
        out_shape=out(rows, 2 * rows, dtype=BF16),
        in_specs=[pl.BlockSpec(memory_space=pltpu.HBM)],
        out_specs=pl.BlockSpec(memory_space=pltpu.VMEM),
        scratch_shapes=[
            pltpu.VMEM((count, rows // count, rows), F32),
            pltpu.SemaphoreType.DMA((count,)),
        ],
        compiler_params=pltpu.CompilerParams(vmem_limit_bytes=HALVES_VMEM),
        cost_estimate=pl.CostEstimate(
            flops=0, bytes_accessed=8 * rows * rows, transcendentals=0
        ),
        name="halves",
    )(operator)


def operator_kernel(idx, x, b2, o, natural, split):
    rows, n = x.shape
    tile = rows // 2
    go_home(idx, ((x, natural),))
    for start in range(0, rows, CHUNK):
        part = slice(start, start + CHUNK)
        low_part = slice(rows + start, rows + start + CHUNK)
        high, low = halves(natural[part, :])
        split[part, 0:n] = high
        split[part, n : 2 * n] = low
        split[low_part, 0:n] = high
        split[low_part, n : 2 * n] = jnp.zeros((CHUNK, n), BF16)

    def multiply(at, carry):
        part = pl.ds(at * tile, tile)
        both = dot16(b2[part, :], split[...])
        natural[part, :] = both[:, 0:n] + both[:, n : 2 * n]
        return carry

    lax.fori_loop(0, rows // tile, multiply, 0)

    def move(at, carry):
        base = at * ROWS_AT_ONCE
        for r in range(ROWS_AT_ONCE):
            o[pl.ds(base + r, 1), :] = natural[pl.ds(idx[base + r], 1), :]
        return carry

    lax.fori_loop(0, rows // ROWS_AT_ONCE, move, 0)


def apply_operator(idx, x, b2):
    rows, n = x.shape
    (result,) = call(
        operator_kernel,
        [out(rows, n)],
        [x, b2],
        smem=[idx],
        scratch=[pltpu.VMEM((rows, n), F32), pltpu.VMEM((2 * rows, 2 * n), BF16)],
        name="operator",
        flops=6 * rows * rows * n,
    )
    return result


def gathered_product(y2, table, p1, cvab):
    lanes = p1.shape[1]
    both = dot16(table[...], y2[...])
    half = both.shape[0] // 2
    total = both[0:half, 0:lanes] + (both[0:half, lanes:] + both[half:, 0:lanes])
    top = p1.shape[0]
    p1[...] = total[0:top, :]
    cvab[...] = total[top:, :]


def table_kernel(ya, yb, yc, yd, pa, qa, qb, coarse, cmap, table, p1, cvab, reach2, y2):
    rows, lanes = BLOCK_ROWS, ya.shape[1]
    cdof = SCALE_LANE
    slot = pa.shape[0] // 2
    gdof, ccl = cmap.shape
    number = lax.broadcasted_iota(jnp.int32, (cdof, ccl), 1).astype(F32)
    chosen = [
        jnp.where(ref[slot : slot + cdof, CID_LANE : CID_LANE + 1] == number, 1.0, 0.0)
        for ref in (pa, qa, qb)
    ]
    reach = jnp.concatenate(
        [cmap[...], jnp.zeros((8, ccl), F32), dot(jnp.concatenate(chosen, axis=0), coarse[...])],
        axis=0,
    )
    reach2[0:128, :], reach2[128:256, :] = halves(reach)
    per = lanes // rows
    which = lax.broadcasted_iota(jnp.int32, (ccl, lanes), 0).astype(F32)
    row = lax.broadcasted_iota(jnp.int32, (256, lanes), 0)
    column = lax.broadcasted_iota(jnp.int32, (256, lanes), 1) % rows
    kept = (row - gdof == column - cdof) & (row > gdof) & (row < gdof + 8)
    unit = jnp.where(kept, 1.0, 0.0)
    for part, y in enumerate((ya, yb, yc, yd)):
        first = part * y.shape[0]
        y2[first : first + y.shape[0], 0:lanes], y2[first : first + y.shape[0], lanes:] = halves(
            y[...]
        )
        for group in range(0, y.shape[0], per * rows):
            ids = y[group + cdof : group + cdof + 8, :]
            for r in range(1, per):
                start = group + r * rows + cdof
                ids = ids + pltpu.roll(y[start : start + 8, :], r * rows, 1)
            onehot = jnp.where(which == ids[0:1, :], 1.0, 0.0).astype(BF16)
            at = slice(first + group, first + group + lanes)
            table[:, at] = (dot16(reach2[...], onehot) + unit).astype(BF16)
    gathered_product(y2, table, p1, cvab)


def corner_kernel(ya, yb, yc, yd, table, p1, cvab, y2):
    lanes = ya.shape[1]
    for part, y in enumerate((ya, yb, yc, yd)):
        rows = slice(part * y.shape[0], (part + 1) * y.shape[0])
        y2[rows, 0:lanes], y2[rows, lanes:] = halves(y[...])
    gathered_product(y2, table, p1, cvab)


def pair_kernel(place, own, other, p2):
    cdof = SCALE_LANE
    top = own.shape[0] - cdof
    odd = place[0] == 1
    p2[0:top, :] = own[0:top, :] + other[0:top, :]
    mine = own[top : top + cdof, :]
    theirs = other[top : top + cdof, :]
    p2[top : top + cdof, :] = jnp.where(odd, theirs, mine)
    p2[top + cdof : top + 2 * cdof, :] = jnp.where(odd, mine, theirs)


def corner_values(place, p2, c2, c4, c6, cvab, ng, cv, cv2):
    cdof = SCALE_LANE
    top = p2.shape[0] - 2 * cdof
    gdof = top - 8
    lanes = cv.shape[1]
    even = slice(top, top + cdof)
    odd = slice(top + cdof, top + 2 * cdof)
    is_odd = place[0] == 1
    total = (p2[0:top, :] + c2[0:top, :]) + (c4[0:top, :] + c6[0:top, :])
    cv[0:cdof, :] = jnp.where(is_odd, p2[odd, :], p2[even, :])
    cv[cdof : 3 * cdof, :] = cvab[...]
    cv[3 * cdof : 4 * cdof, :] = jnp.where(is_odd, p2[even, :], p2[odd, :])
    far = place[1] == 1
    cv[4 * cdof : 5 * cdof, :] = jnp.where(
        is_odd,
        jnp.where(far, c6[even, :], c2[even, :]),
        jnp.where(far, c6[odd, :], c2[odd, :]),
    )
    cv[5 * cdof : 128, :] = jnp.zeros((128 - 5 * cdof, lanes), F32)
    high, low = halves(cv[...] + dot(ng[...], total[0:gdof, :]))
    cv2[0:128, 0:lanes] = high
    cv2[128:256, 0:lanes] = high
    cv2[0:128, lanes : 2 * lanes] = low
    cv2[128:256, lanes : 2 * lanes] = jnp.zeros((128, lanes), BF16)
    return total[gdof : gdof + 8, :]


def times_corner(matrix, rows, cv2):
    both = dot16(matrix[rows, :], cv2[...])
    lanes = both.shape[1] // 2
    return both[:, 0:lanes] + both[:, lanes:]


def column_sum(value):
    return jnp.sum(value, axis=0, keepdims=True)


def stage0_kernel(
    place, p2, c2, c4, c6, cvab, ng, t, bfs, cv2, ua, ub, uc, ud, cv
):
    corner_values(place, p2, c2, c4, c6, cvab, ng, cv, cv2)
    blocks = (ua, ub, uc, ud)
    for block, part, rows in sweep(ua.shape[0]):
        blocks[block][part, :] = t[rows, :] + times_corner(bfs, rows, cv2)


def shadow0_kernel(cv2, fts, dsw, v0):
    for start in range(0, v0.shape[0], CHUNK):
        rows = slice(start, start + CHUNK)
        v0[rows, :] = dsw[rows, :] + times_corner(fts, rows, cv2)


def shadow1_kernel(scal, cv2, fts, dsw, v0, r0, w0, v1, z1, r1):
    alpha = scal[0:1, :]
    for start in range(0, v0.shape[0], CHUNK):
        rows = slice(start, start + CHUNK)
        new = dsw[rows, :] + times_corner(fts, rows, cv2)
        v1[rows, :] = new
        z1[rows, :] = v0[rows, :] - alpha * new
        r1[rows, :] = r0[rows, :] - alpha * w0[rows, :]


def stage1_kernel(
    place, p2, c2, c4, c6, cvab, ng, bfs, t,
    u0a, u0b, u0c, u0d, cv2, bv1, scal, ua, ub, uc, ud, cv,
):
    dots = corner_values(place, p2, c2, c4, c6, cvab, ng, cv, cv2)
    alpha = dots[1:2, :] / dots[2:3, :]
    scal[...] = dots
    scal[0:1, :] = alpha
    olds, news = (u0a, u0b, u0c, u0d), (ua, ub, uc, ud)
    for block, part, rows in sweep(ua.shape[0]):
        image = t[rows, :] + times_corner(bfs, rows, cv2)
        bv1[rows, :] = image
        news[block][part, :] = olds[block][part, :] - alpha * image


def stage2_kernel(
    place, p2, c2, c4, c6, cvab, ng, fts, bfs, t, dsw, v0, w0, v1, bv1, z1, r1, s1, scal,
    u1a, u1b, u1c, u1d, z2, p1, r2, q1, scal2, dots2, ua, ub, uc, ud, cv, cv2,
):
    dots = corner_values(place, p2, c2, c4, c6, cvab, ng, cv, cv2)
    lanes = cv.shape[1]
    rz0 = scal[1:2, :]
    pq0 = scal[2:3, :]
    rz1 = dots[1:2, :]
    beta = rz1 / rz0
    pq1 = dots[2:3, :] + beta * (dots[3:4, :] + dots[4:5, :]) + beta * beta * pq0
    alpha = rz1 / pq1
    scal2[...] = jnp.zeros_like(scal2)
    scal2[0:1, :] = scal[0:1, :]
    scal2[1:2, :] = rz1
    scal2[2:3, :] = pq1
    scal2[3:4, :] = alpha
    olds, news = (u1a, u1b, u1c, u1d), (ua, ub, uc, ud)
    sums = [jnp.zeros((8, lanes), F32) for _ in range(4)]

    def folded(value):
        return jnp.sum(value.reshape(CHUNK // 8, 8, lanes), axis=0)

    for block, part, rows in sweep(ua.shape[0]):
        search = z1[rows, :] + beta * v0[rows, :]
        p1[rows, :] = search
        image_q = s1[rows, :] + beta * w0[rows, :]
        q1[rows, :] = image_q
        res = r1[rows, :] - alpha * image_q
        r2[rows, :] = res
        new = z1[rows, :] - alpha * (
            dsw[rows, :] + times_corner(fts, rows, cv2) + beta * v1[rows, :]
        )
        z2[rows, :] = new
        image = t[rows, :] + times_corner(bfs, rows, cv2) + beta * bv1[rows, :]
        fresh = olds[block][part, :] - alpha * image
        news[block][part, :] = fresh
        sums[0] = sums[0] + folded(res * new)
        sums[1] = sums[1] + folded(fresh * new)
        sums[2] = sums[2] + folded(image_q * new)
        sums[3] = sums[3] + folded(fresh * search)
    dots2[0] = jnp.zeros((8, lanes), F32)
    dots2[0, 1:2, :] = column_sum(sums[0])
    dots2[0, 2:3, :] = 2.0 * column_sum(sums[1])
    dots2[0, 3:4, :] = column_sum(sums[2])
    dots2[0, 4:5, :] = 2.0 * column_sum(sums[3])
    message = dots2[0]
    for other in range(1, dots2.shape[0]):
        dots2[other] = message


def jump_kernel(pairs, place, ua, ub, uc, ud, qa, qb, qc, qd, dsum, ct2, *rest):
    fields, (w, dsw, pay, w2) = rest[:-4], rest[-4:]
    lanes = w.shape[1]
    mine, theirs = (ua, ub, uc, ud), (qa, qb, qc, qd)
    sums = [jnp.zeros((8, lanes), F32) for _ in pairs]
    for block, part, rows in sweep(ua.shape[0]):
        live = live_chunk(place, block, part, lanes)
        value = jnp.where(live, mine[block][part, :] - theirs[block][part, :], 0.0)
        w[rows, :] = value
        dsw[rows, :] = dsum[rows, :] * value
        w2[rows, 0:lanes], w2[rows, lanes : 2 * lanes] = halves(value)
        for at, (left, right) in enumerate(pairs):
            first = value if left < 0 else fields[left][rows, :]
            product = first * fields[right][rows, :]
            sums[at] = sums[at] + jnp.sum(product.reshape(CHUNK // 8, 8, lanes), axis=0)
    send(pay, restricted(ct2, w2), [column_sum(v) for v in sums], SCALE_LANE + 1)


def sum_kernel(x, o):
    o[...] = jnp.sum(x[...], axis=0)


def add_kernel(first, *rest):
    *others, o = rest
    total = first[...]
    for other in others:
        total = total + other[...]
    o[...] = total


def home_kernel(idx, scal2, z2, p1, v0, z2n, p1n, xsn, xs):
    xs[...] = scal2[0:1, :] * v0[...] + scal2[3:4, :] * p1[...]
    go_home(idx, ((z2, z2n), (p1, p1n), (xs, xsn)))


def last_kernel(
    place, idx, z2, p1, xs, r2, q1, ua, ub, uc, ud, qa, qb, qc, qd, scal2, d0, d2, d4, d6,
    mult, resid, work,
):
    dots = (d0[...] + d2[...]) + (d4[...] + d6[...])
    lanes = work.shape[1]
    beta = dots[1:2, :] / scal2[1:2, :]
    pq = dots[2:3, :] + beta * (dots[3:4, :] + dots[4:5, :]) + beta * beta * scal2[2:3, :]
    alpha = dots[1:2, :] / pq
    mine, theirs = (ua, ub, uc, ud), (qa, qb, qc, qd)
    for block, part, rows in sweep(ua.shape[0]):
        live = live_chunk(place, block, part, lanes)
        image = jnp.where(live, mine[block][part, :] - theirs[block][part, :], 0.0)
        work[rows, :] = r2[rows, :] - alpha * (image + beta * q1[rows, :])
        mult[rows, :] = xs[rows, :] + alpha * (z2[rows, :] + beta * p1[rows, :])
    go_home(idx, ((work, resid),))


def body(
    dual_ops,
    rhs,
    corner_basis,
    scaling,
    cluster_corner_inverse,
    coarse_map,
    global_inv,
    row_index,
    pair_counts,
    corner_map,
):
    operator = dual_ops[0, 0]
    loads = rhs[0, 0]
    basis = corner_basis[0, 0]
    weights = scaling[0]
    factor = cluster_corner_inverse[0]
    lift_map = coarse_map[0]
    row_ids = row_index[0, 0]
    corners = corner_map[0]
    slot = row_ids.shape[1]
    order, lanes = loads.shape
    cdof = basis.shape[0]
    subs = lax.axis_size("sub")
    clusters = lax.axis_size("cluster")
    gdof = lift_map.shape[0]

    s = lax.axis_index("sub")
    c = lax.axis_index("cluster")
    s_odd = s % 2
    c_odd = c % 2
    pairs_a = [(i, i ^ 1) for i in range(subs)]
    pairs_b = [(i, (i + 1) % subs) for i in range(1, subs, 2)]
    pairs_b += [(j, i) for i, j in pairs_b]
    pairs_c = [(i, i ^ 1) for i in range(clusters)]
    pairs_d = [(i, (i + 1) % clusters) for i in range(1, clusters, 2)]
    pairs_d += [(j, i) for i, j in pairs_d]
    across = [[(i, i ^ k) for i in range(clusters)] for k in (2, 4, 6)]

    chip = c // 2
    next_chip = jnp.where(c_odd == 1, chip + 1, chip - 1)
    far = ((chip ^ next_chip) == 3).astype(jnp.int32)
    def chosen(array):
        return [
            jnp.where(s_odd == 0, array[1], array[0]),
            jnp.where(s_odd == 0, array[0], array[1]),
            jnp.where(c_odd == 0, array[3], array[2]),
            jnp.where(c_odd == 0, array[2], array[3]),
        ]

    sides = (1 - s_odd, s_odd, 3 - c_odd, 2 + c_odd)
    place = jnp.stack([v.astype(jnp.int32) for v in (c_odd, far, s, *sides)])
    place = jnp.concatenate([place, pair_counts[0, 0]])
    idx = jnp.concatenate(chosen(row_ids))
    idx, place = lax.optimization_barrier((idx, place))

    def exchange(blocks):
        return [
            lax.ppermute(blocks[0], "sub", pairs_a),
            lax.ppermute(blocks[1], "sub", pairs_b),
            lax.ppermute(blocks[2], "cluster", pairs_c),
            lax.ppermute(blocks[3], "cluster", pairs_d),
        ]

    def spread(messages, groups=None):
        return lax.all_to_all(messages, "sub", 0, 0, tiled=True, axis_index_groups=groups)

    z_count = subs // X_GROUP
    z_groups = [[X_GROUP * z + x for z in range(z_count)] for x in range(X_GROUP)]

    def together(*values):
        return lax.optimization_barrier(values)

    def clusterwise(p1, cvab):
        other = lax.ppermute(p1, "cluster", pairs_c)
        (p2,) = call(
            pair_kernel,
            [out(gdof + 8 + 2 * cdof, lanes)],
            [p1, other],
            smem=[place],
            name="pair",
        )
        moved = [lax.ppermute(p2, "cluster", k) for k in across]
        return [p2, *moved, cvab]

    block_out = [out(slot, lanes)] * 4
    full = out(order, lanes)
    small = [out(gdof + 8 + cdof, lanes), out(2 * cdof, lanes)]
    cv_scratch = [pltpu.VMEM((128, lanes), F32), pltpu.VMEM((256, 2 * lanes), BF16)]
    y2_scratch = [pltpu.VMEM((subs * BLOCK_ROWS, 2 * lanes), BF16)]
    cv2_out = out(256, 2 * lanes, dtype=BF16)
    w2_scratch = [pltpu.VMEM((order, 2 * lanes), BF16)]

    *packs, crow, ct2 = pack_rows(place, idx, loads, basis, weights, corners, lift_map, slot)
    packs_in = exchange(packs)
    (coarse,) = call(coarse_kernel, [out(*factor.shape)], [factor], name="coarse")
    b2 = split_operator(operator)
    b2, coarse, *packs_in = together(b2, coarse, *packs_in)
    r0, pay = call(
        first_kernel,
        [full, out(z_count, BLOCK_ROWS, lanes)],
        [crow, *packs, *packs_in, ct2],
        smem=[place],
        scratch=w2_scratch,
        name="first",
    )

    def x_group(mine):
        return [mine] + [
            lax.ppermute(mine, "sub", [(i, i ^ k) for i in range(subs)])
            for k in range(1, X_GROUP)
        ]

    y = spread(pay, z_groups)
    y, r0 = together(y, r0)
    y = x_group(y.reshape(z_count * BLOCK_ROWS, lanes))
    fts, ft, dsum, dsw, ng = call(
        static_kernel,
        [
            out(order, 2 * lanes, dtype=BF16),
            full,
            full,
            full,
            out(128, gdof),
        ],
        [*packs, *packs_in, r0, global_inv],
        smem=[place],
        scratch=[pltpu.VMEM((128, lanes), F32), pltpu.VMEM((128, gdof), F32)],
        name="static",
    )
    t = apply_operator(idx, dsw, b2)
    t, *y = together(t, *y)
    table, p1, cvab = call(
        table_kernel,
        [out(256, subs * BLOCK_ROWS, dtype=BF16)] + small,
        [*y, packs[0], *packs_in[:2], coarse, lift_map],
        scratch=[pltpu.VMEM((256, factor.shape[0]), BF16), *y2_scratch],
        name="table",
    )
    cluster_part = clusterwise(p1, cvab)
    bf = apply_operator(idx, ft, b2)
    (bfs,) = call(split_kernel, [out(order, 2 * lanes, dtype=BF16)], [bf], name="split")
    cv2, *u0 = call(
        stage0_kernel,
        [cv2_out] + block_out,
        [*cluster_part, ng, t, bfs],
        smem=[place],
        scratch=cv_scratch[:1],
        name="stage0",
    )
    u0_in = exchange(u0)
    (v0,) = call(shadow0_kernel, [full], [cv2, fts, dsw], name="shadow0")
    v0, *u0_in = together(v0, *u0_in)
    w0, dsw, pay = call(
        functools.partial(jump_kernel, ((0, 1), (-1, 1))),
        [full, full, out(z_count, BLOCK_ROWS, lanes)],
        [*u0, *u0_in, dsum, ct2, r0, v0],
        smem=[place],
        scratch=w2_scratch,
        name="jump1",
    )

    y = spread(pay, z_groups)
    y, dsw = together(y, dsw)
    y = x_group(y.reshape(z_count * BLOCK_ROWS, lanes))
    t = apply_operator(idx, dsw, b2)
    t, *y = together(t, *y)
    p1, cvab = call(
        corner_kernel,
        small,
        [*y, table],
        scratch=y2_scratch,
        name="corner",
    )
    cluster_part = clusterwise(p1, cvab)
    cv2, bv1, scal, *u1 = call(
        stage1_kernel,
        [cv2_out, full, out(8, lanes)] + block_out,
        [*cluster_part, ng, bfs, t, *u0],
        smem=[place],
        scratch=cv_scratch[:1],
        name="stage1",
    )
    u1_in = exchange(u1)
    v1, z1, r1 = call(
        shadow1_kernel, [full] * 3, [scal, cv2, fts, dsw, v0, r0, w0], name="shadow1"
    )
    v1, z1, r1, *u1_in = together(v1, z1, r1, *u1_in)
    s1, dsw, pay = call(
        functools.partial(jump_kernel, ((0, 1), (-1, 1), (2, 1), (-1, 3))),
        [full, full, out(z_count, BLOCK_ROWS, lanes)],
        [*u1, *u1_in, dsum, ct2, r1, z1, w0, v0],
        smem=[place],
        scratch=w2_scratch,
        name="jump2",
    )

    y = spread(pay, z_groups)
    y, dsw = together(y, dsw)
    y = x_group(y.reshape(z_count * BLOCK_ROWS, lanes))
    t = apply_operator(idx, dsw, b2)
    t, *y = together(t, *y)
    p1, cvab = call(
        corner_kernel,
        small,
        [*y, table],
        scratch=y2_scratch,
        name="corner",
    )
    cluster_part = clusterwise(p1, cvab)
    z2, p1, r2, q1, scal2, dots2, *u2 = call(
        stage2_kernel,
        [full] * 4 + [out(8, lanes), out(subs, 8, lanes)] + block_out,
        [*cluster_part, ng, fts, bfs, t, dsw, v0, w0, v1, bv1, z1, r1, s1, scal, *u1],
        smem=[place],
        scratch=cv_scratch,
        name="stage2",
    )

    dots = spread(dots2)
    dots, z2, scal2, *u2 = together(dots, z2, scal2, *u2)
    u2_in = exchange(u2)
    (dots,) = call(sum_kernel, [out(8, lanes)], [dots], name="sum")
    other = lax.ppermute(dots, "cluster", pairs_c)
    (dots,) = call(add_kernel, [out(8, lanes)], [dots, other], name="add")
    moved = [lax.ppermute(dots, "cluster", k) for k in across]
    home = call(
        home_kernel,
        [full] * 3,
        [scal2, z2, p1, v0],
        smem=[idx],
        scratch=[pltpu.VMEM((order, lanes), F32)],
        name="home",
        flops=4_000_000_000,
    )
    multipliers, residual = call(
        last_kernel,
        [full, full],
        [*home, r2, q1, *u2, *u2_in, scal2, dots, *moved],
        smem=[place, idx],
        scratch=[pltpu.VMEM((order, lanes), F32)],
        name="last",
    )
    return (multipliers[None, None], residual[None, None])


def solution(mesh):
    in_specs = (
        P("cluster", "sub", None, None),
        P("cluster", "sub", None, None),
        P("cluster", "sub", None, None),
        P("cluster", "sub", None),
        P("cluster", None, None),
        P("cluster", None, None),
        P(),
        P("cluster", "sub", None, None),
        P("cluster", "sub", None),
        P("cluster", "sub", None),
    )
    out_specs = (P("cluster", "sub", None, None), P("cluster", "sub", None, None))
    return jax.shard_map(body, mesh=mesh, in_specs=in_specs, out_specs=out_specs, check_vma=False)
```
